512 devices in a mesh: wave: 128 (over z, y, core), lev: 4 (over x).
Axes of the slice: x: 4, y: 8, z: 8, core: 2. Of those that a mesh axis runs over, the one named last changes fastest.
Arguments:
- fine_state: float32 [8, 3, 2, 384, 769], P('lev', None, None, 'wave'), may hold values from -6 to 6
- fold_pairs: int32 [384], replicated, may hold values from 0 to 383, each once
- legendre: bfloat16 [384, 1536, 769], P('wave', 'lev'), may hold values from -0.21875 to 0.21875
- gauss_weights: float32 [1536], P('lev'), may hold values from 0.5 to 3
- grid_coef: float32 [8, 2560], replicated, may hold values from -4 to 4
- modes_from: float32 [8, 8], replicated
- modes_to: float32 [8, 8], replicated, as said below
- mode_rates: float32 [8], replicated, may hold values from 0.2 to 20
Outputs:
- corrected: float32 [8, 2, 2, 384, 769], P('lev', None, None, 'wave')
- fine_tend: float32 [8, 3, 2, 384, 769], P('lev', None, None, 'wave')
The draws below stay inside these ranges and needn't reach their ends.
Inputs may be any that keep to these rules, and one draw needn't show every extreme that they name: Slot p holds zonal wavenumbers fold_pairs[p] and 767 - fold_pairs[p]; every value occurs once. modes_to is the inverse of modes_from.
All inputs are finite; a program needn't handle non-finite values.
Results may differ from the reference program's by a relative error of at most 0.02.
Values may be sent and summed in bfloat16 or wider, within the bound.
A program may use at most 64 MiB of HBM per device.

```python
import math
import jax
import jax.numpy as jnp
from jax import lax

NLON = 2560
LEV = 8
NODES = 3
WAVES = 768
LAT = 1536
ROWS = 769
PAIRS = 384
NC = 384


def vertical_pair(key):
    base_key = jax.random.fold_in(key, 71)
    noise_draw = jax.random.normal(base_key, (LEV, LEV), jnp.float32)
    eigen_basis = jnp.eye(LEV, dtype=jnp.float32) + 0.5 * noise_draw / math.sqrt(LEV)
    return (eigen_basis, jnp.linalg.inv(eigen_basis))


def draw_modes_from(key, part):
    return vertical_pair(key)[0]


def draw_modes_to(key, part):
    return vertical_pair(key)[1]


def block_scale(key, shape, cuts, least, high):
    def one(dim, parts):
        heights = jax.random.uniform(jax.random.fold_in(jax.random.fold_in(key, 6), dim), (parts,), jnp.float32, least / len(cuts), high / len(cuts))
        return jnp.repeat(jnp.exp(heights), shape[dim] // parts).reshape((-1,) + (1,) * (len(shape) - dim - 1))

    gain = one(*cuts[0])
    for cut in cuts[1:]:
        gain = gain * one(*cut)
    return gain


def scatter_about(own_key, extent, scale, limit, shards=(), held_as=jnp.bfloat16):
    level = block_scale(own_key, extent, shards, -0.22, 0.18) if shards else 1.0
    drawn = jax.random.normal(own_key, extent, jnp.float32) * scale * level
    return jnp.minimum(jnp.maximum(drawn, -limit), limit).astype(held_as)


def setup_inputs(seed: int = 0) -> dict:
    key_of = jax.random.split(jax.random.key(seed), 9)
    return {
        "fine_state": scatter_about(key_of[0], (LEV, NODES, 2, PAIRS, ROWS), 1.0, 6.0, ((0, 4), (3, 128)), jnp.float32),
        "fold_pairs": jax.random.permutation(key_of[1], PAIRS).astype(jnp.int32),
        "legendre": scatter_about(key_of[2], (PAIRS, LAT, ROWS), ROWS ** -0.5, 0.21875, ((0, 128), (1, 4))),
        "gauss_weights": jnp.clip(jnp.exp(math.log(3.0) - 1.7917595 * jax.random.uniform(key_of[3], (LAT,), jnp.float32) ** block_scale(key_of[3], (LAT,), ((0, 4),), -0.2, 0.2)), 0.5, 3.0),
        "grid_coef": jnp.clip(jax.random.uniform(key_of[4], (LEV, NLON), jnp.float32, -4.0, 4.0), -4.0, 4.0),
        "modes_from": draw_modes_from(jax.random.fold_in(key_of[8], 71), 0),
        "modes_to": draw_modes_to(jax.random.fold_in(key_of[8], 71), 0),
        "mode_rates": jnp.clip(jnp.exp(jax.random.uniform(key_of[7], (LEV,), jnp.float32, math.log(0.2), math.log(20.0))), 0.2, 20.0),
    }


STEP_HALF = 0.5
quad_weights = ((5.0 / 24.0, 1.0 / 3.0, -1.0 / 24.0), (-1.0 / 24.0, 1.0 / 3.0, 5.0 / 24.0))
HIGHEST = lax.Precision.HIGHEST

def fourier_table(waves, points, amplitude):
    steps = jnp.arange(points, dtype=jnp.int32)
    turns = waves[:, :, None] * steps[None, None, :] % points
    angles = turns.astype(jnp.float32) * (2.0 * math.pi / points)
    return jnp.stack([jnp.cos(angles) * amplitude, -jnp.sin(angles) * amplitude]).astype(jnp.bfloat16)

def fine_rows(small_wave, fine_width):
    row_ids = jnp.arange(fine_width + 1, dtype=jnp.int32)[None, :]
    return row_ids < fine_width - small_wave[:, None]

def coarse_rows(small_wave, coarse):
    row_ids = jnp.arange(coarse, dtype=jnp.int32)[None, :]
    coarse_keep = row_ids < coarse - small_wave[:, None]
    degree = (small_wave[:, None] + row_ids).astype(jnp.float32)
    return (coarse_keep, degree)

def pair_blocks(values, which_axis):
    leading = jnp.moveaxis(values, which_axis, 0)
    block_size = math.gcd(leading.shape[0], 16)
    return leading.reshape((leading.shape[0] // block_size, block_size) + leading.shape[1:])

def unblock(values, which_axis):
    flattened = values.reshape((values.shape[0] * values.shape[1],) + values.shape[2:])
    return jnp.moveaxis(flattened, 0, which_axis)

def legendre_inverse(spectral, legendre_table, row_mask):

    def block_step(items):
        spec_block, table_block, mask_block = items
        split_spec = spec_block.astype(jnp.float32)[:, :, :, :, None, :] * mask_block.astype(jnp.float32)[:, None, None, None, :, :]
        return jnp.einsum('pabcmr,plr->pabcml', split_spec, table_block.astype(jnp.float32), precision=HIGHEST).astype(jnp.bfloat16)
    mapped = lax.map(block_step, (pair_blocks(spectral, 3), pair_blocks(legendre_table, 0), pair_blocks(row_mask, 0)))
    return unblock(mapped, 3)

def legendre_forward(returned, legendre_table, row_mask):

    def block_step(items):
        back_block, table_block, mask_block = items
        members = jnp.einsum('pabcml,plr->pabcmr', back_block.astype(jnp.float32), table_block.astype(jnp.float32), precision=HIGHEST)
        return jnp.sum(members * mask_block.astype(jnp.float32)[:, None, None, None, :, :], axis=4)
    mapped = lax.map(block_step, (pair_blocks(returned, 3), pair_blocks(legendre_table, 0), pair_blocks(row_mask, 0)))
    return unblock(mapped, 3)

def grid_step(fourier, wave_table, coef, weights, factor):
    grid_field = jnp.einsum('abcpmz,cpmk->abzk', fourier.astype(jnp.float32), wave_table.astype(jnp.float32), precision=HIGHEST)
    product = (coef[:, None, None, :] * grid_field * grid_field).astype(jnp.bfloat16)
    returned = jnp.einsum('abzk,cpmk->abcpmz', product.astype(jnp.float32), wave_table.astype(jnp.float32), precision=HIGHEST)
    return (returned * (weights * factor)).astype(jnp.bfloat16)

def mix(matrix, values):
    return jnp.einsum('ql,lbcpr->qbcpr', matrix, values, precision=HIGHEST)

def reference(fine_state, fold_pairs, legendre, gauss_weights, grid_coef, modes_from, modes_to, mode_rates):
    first_member = fine_rows(fold_pairs, WAVES)
    member_mask = jnp.stack([first_member, jnp.logical_not(first_member)], 1).astype(jnp.bfloat16)
    coarse_keep, degree = coarse_rows(fold_pairs, NC)
    keep_mask = coarse_keep[:, None, :].astype(jnp.bfloat16)
    keep_float = coarse_keep.astype(jnp.float32)
    fine_table = fourier_table(jnp.stack([fold_pairs, WAVES - 1 - fold_pairs], 1), NLON, WAVES ** (-0.5))
    coarse_table = fourier_table(fold_pairs[:, None], NLON // 2, NC ** (-0.5))
    coarse_leg = legendre[:, :, :NC]
    coarse_coef = grid_coef[:, ::2]
    fine_fourier = legendre_inverse(fine_state.astype(jnp.bfloat16), legendre, member_mask)
    fine_back = grid_step(fine_fourier, fine_table, grid_coef, gauss_weights, 2.0 * WAVES / NLON)
    fine_tend = legendre_forward(fine_back, legendre, member_mask)

    def coarse_eval(modes):
        levels = (mix(modes_from, modes) * keep_float).astype(jnp.bfloat16)
        coarse_fourier = legendre_inverse(levels, coarse_leg, keep_mask)
        coarse_back = grid_step(coarse_fourier, coarse_table, coarse_coef, gauss_weights, 2.0 * NC / (NLON // 2))
        return mix(modes_to, legendre_forward(coarse_back, coarse_leg, keep_mask))
    old_state = mix(modes_to, fine_state[..., :NC] * keep_float)
    old_tend = mix(modes_to, fine_tend[..., :NC] * keep_float)
    old_coarse = coarse_eval(old_state[:, 1:2])
    stiffness = mode_rates[:, None, None, None] * (degree * (degree + 1.0) / (NC * (NC + 1.0)))[None, None]
    source = old_tend - stiffness[:, None] * old_state
    integral_mid = quad_weights[0][0] * source[:, 0] + quad_weights[0][1] * source[:, 1] + quad_weights[0][2] * source[:, 2]
    integral_end = quad_weights[1][0] * source[:, 0] + quad_weights[1][1] * source[:, 1] + quad_weights[1][2] * source[:, 2]
    divisor = 1.0 + STEP_HALF * stiffness
    next_mid = (old_state[:, 0] + STEP_HALF * stiffness * old_state[:, 1] + integral_mid) / divisor
    coarse_fresh = coarse_eval(next_mid[:, None])
    next_end = (next_mid + STEP_HALF * (coarse_fresh[:, 0] - old_coarse[:, 0]) + STEP_HALF * stiffness * old_state[:, 2] + integral_end) / divisor
    change = jnp.stack([next_mid - old_state[:, 1], next_end - old_state[:, 2]], 1)
    lifted = mix(modes_from, change)
    corrected = fine_state[:, 1:] + jnp.pad(lifted, ((0, 0), (0, 0), (0, 0), (0, 0), (0, ROWS - NC)))
    return (corrected, fine_tend)
```

```python
import functools
import math

import jax
import jax.numpy as jnp
import ml_dtypes
import numpy as np
from jax import lax
from jax.experimental import pallas as pl
from jax.experimental.pallas import tpu as pltpu
from jax.sharding import PartitionSpec as P

F32 = jnp.float32
BF16 = jnp.bfloat16
HIGHEST = lax.Precision.HIGHEST
MESH = pl.DeviceIdType.MESH

NLON, LEV, WAVES, ROWS, NC = 2560, 8, 768, 769, 384
HALF, CHALF = NLON // 2, NLON // 4
NZ, ND, NT = 8, 16, 4
FACTOR = 2.0 * WAVES / NLON
QUAD = ((5.0 / 24.0, 1.0 / 3.0, -1.0 / 24.0), (-1.0 / 24.0, 1.0 / 3.0, 5.0 / 24.0))


def table(waves, points, amplitude, count):
    turns = np.outer(waves, np.arange(count)) % points
    angles = turns * (2.0 * math.pi / points)
    return np.concatenate([np.cos(angles), -np.sin(angles)], 0).reshape(2, len(waves), count) * amplitude


def tables():
    t = np.arange(192)
    fine, coarse = [], []
    for parity in (0, 1):
        low = 2 * t + parity
        high = (WAVES - 2 - 2 * t) + parity
        fine.append(table(np.concatenate([low, high]), NLON, WAVES**-0.5, HALF).reshape(768, HALF))
        part = table(low, NLON // 2, NC**-0.5, CHALF)
        coarse.append(np.concatenate([part, np.zeros_like(part)], 1).reshape(768, CHALF))
    as_bf16 = lambda parts: np.stack(parts).astype(np.float32).astype(ml_dtypes.bfloat16)
    return as_bf16(fine), as_bf16(coarse)


def selectors():
    to_rows = np.zeros((96, 8), np.float32)
    to_mask = np.zeros((96, 64), np.float32)
    to_cols = np.zeros((8, 64), np.float32)
    for lev in range(4):
        for c in range(2):
            for rho in range(8):
                col = lev * 16 + c * 8 + rho
                to_cols[lev * 2 + rho % 2, col] = 1
                node = rho // 2
                for q in range(8):
                    if node < 3:
                        to_mask[node * 16 + c * 8 + q, col] = 1
                        to_mask[48 + c * 8 + q, col] = QUAD[0][node]
                        to_mask[64 + c * 8 + q, col] = QUAD[1][node]
                    else:
                        to_mask[80 + c * 8 + q, col] = 1
    for row in range(96):
        to_rows[row, row % 8] = 1
    mix_cols = np.zeros((8, 16), np.float32)
    mix_rows = np.zeros((208, 8), np.float32)
    mix_mask = np.zeros((208, 16), np.float32)
    for c in range(2):
        for q in range(8):
            mix_cols[q, c * 8 + q] = 1
            for a in range(8):
                mix_rows[c * 8 + a, a] = 1
                mix_mask[c * 8 + a, c * 8 + q] = 1
                for p in range(3):
                    row = 16 + p * 64 + (a // 2) * 16 + p * 4 + (a % 2) * 2 + c
                    mix_rows[row, a] = 1
                    mix_mask[row, c * 8 + q] = 1
    return to_rows, to_mask, to_cols, mix_rows, mix_mask, mix_cols


def dot(a, b, precision=None):
    return lax.dot_general(a, b, (((1,), (0,)), ((), ())), precision=precision, preferred_element_type=F32)


def dot_nt(a, b):
    return lax.dot_general(a, b, (((1,), (1,)), ((), ())), preferred_element_type=F32)


def kernel(
    fs, leg_hbm, fold_s, fold_col, gauss_s, rates_s, coef, mto, mfrom, tf_hbm, tc_hbm,
    to_rows, to_mask, to_cols, mix_rows, mix_mask, mix_cols,
    corr, tend_out,
    leg, tf, tc, xf, gat, m0s, m1s, onehot, perm, permt, coefx, ccoefx, wto, wmix,
    s1, r1, stage, s2, r2, s3, r3, s4, r4, vbuf, s5, r5, states, oldp, lift,
    s6, r6, cstage, s7, r7, s8, r8, s9, r9, s10, r10,
    load_sem, z_send, z_recv, d_send, d_recv, lev_send, lev_recv,
):
    w = lax.axis_index("wave")
    t = lax.axis_index("lev")
    z, d = w // ND, w % ND

    loads = [
        pltpu.make_async_copy(leg_hbm, leg, load_sem.at[0]),
        pltpu.make_async_copy(tf_hbm, tf, load_sem.at[1]),
        pltpu.make_async_copy(tc_hbm, tc, load_sem.at[2]),
    ]
    for load in loads:
        load.start()

    barrier = pltpu.get_barrier_semaphore()

    def lev_dev(k):
        return {"lev": lax.rem(t + k, NT)}

    def z_dev(k):
        return {"wave": lax.rem(z + k, NZ) * ND + d}

    def d_dev(k):
        return {"wave": z * ND + lax.rem(d + k, ND)}

    groups = ((NT, lev_dev), (NZ, z_dev), (ND, d_dev))
    for count, dev in groups:
        @pl.loop(1, count)
        def _(k):
            pl.semaphore_signal(barrier, inc=1, device_id=dev(k), device_id_type=MESH)

    def lev_copy(k, src, dst, row):
        return pltpu.make_async_remote_copy(
            src_ref=src, dst_ref=dst, send_sem=lev_send.at[row, k], recv_sem=lev_recv.at[row, k],
            device_id=lev_dev(k), device_id_type=MESH)

    def z_copy(k, src, dst, row):
        return pltpu.make_async_remote_copy(
            src_ref=src.at[lax.rem(z + k, NZ)], dst_ref=dst.at[z], send_sem=z_send.at[row, k],
            recv_sem=z_recv.at[row, k], device_id=z_dev(k), device_id_type=MESH)

    def d_copy(k, src, dst, row):
        return pltpu.make_async_remote_copy(
            src_ref=src.at[lax.rem(d + k, ND)], dst_ref=dst.at[d], send_sem=d_send.at[row, k],
            recv_sem=d_recv.at[row, k], device_id=d_dev(k), device_id_type=MESH)

    def gather_copy(k, buf, row):
        return lev_copy(k, buf.at[t], buf.at[t], row)

    def scatter_copy(k, src, dst, row):
        return lev_copy(k, src.at[lax.rem(t + k, NT)], dst.at[t], row)

    def start(count, make):
        @pl.loop(1, count)
        def _(k):
            make(k).start()

    def arrive(count, make):
        @pl.loop(1, count)
        def _(k):
            make(k).wait_recv()

    def sent(count, make):
        @pl.loop(1, count)
        def _(k):
            make(k).wait_send()

    for p in range(3):
        for c in range(2):
            for a in range(2):
                for b in range(3):
                    xf[p, pl.ds(c * 8 + b * 2 + a, 1), :] = fs[a, b, p, pl.ds(c, 1), :]
                xf[p, pl.ds(c * 8 + 6 + a, 1), :] = fs[a, 1, p, pl.ds(c, 1), :]
    gat[t] = xf[...].astype(BF16)
    pl.semaphore_wait(barrier, (NT - 1) + (NZ - 1) + (ND - 1))
    e1 = lambda k: gather_copy(k, gat, 0)
    start(NT, e1)

    folds = [fold_s[w * 3 + p] for p in range(3)]
    rho = lax.rem(lax.broadcasted_iota(jnp.int32, (16, ROWS), 0), 8)
    row_r = lax.broadcasted_iota(jnp.int32, (16, ROWS), 1)
    for p in range(3):
        first = jnp.where(row_r < WAVES - folds[p], 1.0, 0.0)
        keep = jnp.where(row_r < NC - folds[p], 1.0, 0.0)
        m0s[p] = jnp.where(rho < 6, first, keep)
        m1s[p] = jnp.where(rho < 6, 1.0 - first, 0.0)
    fold = fold_col[...]
    half_fold, odd = fold // 2, lax.rem(fold, 2)
    cols = lax.broadcasted_iota(jnp.int32, (NC, 2 * NC), 1)
    onehot[pl.ds(0, NC), :] = jnp.where(cols == half_fold + NC * odd, 1.0, 0.0).astype(BF16)
    onehot[pl.ds(NC, NC), :] = jnp.where(cols == 192 + half_fold + NC * (1 - odd), 1.0, 0.0).astype(BF16)
    pr = lax.broadcasted_iota(jnp.int32, (128, 128), 0)
    pc = lax.broadcasted_iota(jnp.int32, (128, 128), 1)
    perm[...] = jnp.where(pc == lax.rem(pr, NZ) * ND + pr // NZ, 1.0, 0.0).astype(BF16)
    permt[...] = jnp.where(pr == lax.rem(pc, NZ) * ND + pc // NZ, 1.0, 0.0).astype(BF16)
    for lev in range(NT):
        for n in range(4):
            coefx[pl.ds(lev * 8 + n * 2, 2), :] = coef[pl.ds(lev * 2, 2), :]
    sel_r = lax.broadcasted_iota(jnp.int32, (256, 128), 0)
    sel_c = lax.broadcasted_iota(jnp.int32, (256, 128), 1)
    even = jnp.where(sel_r == 2 * sel_c, 1.0, 0.0)
    chunks = jnp.concatenate([coef[:, pl.ds(n * 256, 256)] for n in range(10)], 0)
    picked = dot(chunks, even, HIGHEST)
    ccoef = jnp.concatenate([picked[n * 8 : n * 8 + 8] for n in range(10)], 1)
    for n in range(10):
        for lev in range(NT):
            for m in range(4):
                ccoefx[pl.ds(lev * 8 + m * 2, 2), pl.ds(n * 128, 128)] = picked[n * 8 + lev * 2 : n * 8 + lev * 2 + 2]
    wto[...] = dot(dot(to_rows[...], mto[...], HIGHEST), to_cols[...], HIGHEST) * to_mask[...]
    wmix[pl.ds(0, 208), :] = dot(dot(mix_rows[...], mfrom[...], HIGHEST), mix_cols[...], HIGHEST) * mix_mask[...]
    wmix[pl.ds(208, 16), :] = (
        dot(dot(mix_rows[pl.ds(0, 16), :], mto[...], HIGHEST), mix_cols[...], HIGHEST) * mix_mask[pl.ds(0, 16), :]
    )
    stage[...] = jnp.zeros_like(stage)
    cstage[...] = jnp.zeros_like(cstage)

    arrive(NT, e1)
    loads[0].wait()

    for p in range(3):
        x = gat[:, p].reshape(64, ROWS)
        k0 = jnp.concatenate([m0s[p].astype(BF16)] * 4, 0)
        k1 = jnp.concatenate([m1s[p].astype(BF16)] * 4, 0)
        f = dot(jnp.concatenate([x * k0, x * k1], 0), leg[p])
        s1[:, :, pl.ds(p * 128, 128)] = f.T.astype(BF16).reshape(NZ, 48, 128)
    e2a = lambda k: z_copy(k, s1, r1, 0)
    start(NZ, e2a)
    r1[z] = s1[z]

    for p in range(3):
        x = gat[:, p, :, pl.ds(0, NC)].reshape(64, NC).astype(F32)
        keep = m0s[p, pl.ds(6, 1), pl.ds(0, NC)]
        states[p] = dot(wto[pl.ds(0, 48), :], x, HIGHEST) * keep
    arrive(NZ, e2a)
    for j in range(3):
        o = dot(perm[...], r1[:, pl.ds(j * 16, 16), :].reshape(128, 384))
        for p in range(3):
            stage[:, pl.ds(j * 24 + p * 8, 8), :] = o[:, p * 128 : p * 128 + 128].reshape(ND, 8, 128)
    s2[...] = stage[...].astype(BF16)
    e2b = lambda k: d_copy(k, s2, r2, 0)
    start(ND, e2b)
    r2[d] = s2[d]
    loads[1].wait()
    loads[2].wait()
    arrive(ND, e2b)

    stage[...] = r2[...].astype(F32)
    turned = []
    for j in range(3):
        by_p = [stage[:, pl.ds(j * 24 + p * 8, 8), :].reshape(128, 128) for p in range(3)]
        turned.append(jnp.concatenate(by_p, 0).T)
    natural = []
    for c in range(2):
        rows = []
        for j in range(3):
            members = []
            for i in range(2):
                at = [i * 64 + lev * 16 + c * 8 for lev in range(NT)]
                members.append(jnp.concatenate([turned[j][r : r + 8] for r in at], 0))
            rows.append(jnp.concatenate(members, 1))
        x = jnp.concatenate(rows, 0).astype(BF16)
        natural.append(dot(x, onehot[...]).astype(BF16))
    weights = [gauss_s[z * 48 + j * 16 + d] * FACTOR for j in range(3)]

    def grid(x_even, x_odd, tab, width, coefs, reps):
        e = dot(x_even, tab[0])
        o = dot(x_odd, tab[1])
        low, high = e + o, e - o
        c_low = jnp.concatenate([coefs[:, pl.ds(0, width)]] * reps, 0)
        c_high = jnp.concatenate([coefs[:, pl.ds(width, width)]] * reps, 0)
        prod = jnp.concatenate([c_low * low * low, c_high * high * high], 0).astype(BF16)
        n = low.shape[0]
        back_e = dot_nt(prod, tab[0])
        back_o = dot_nt(prod, tab[1])
        return back_e[:n] + back_e[n:], back_o[:n] - back_o[n:]

    x_even = jnp.concatenate([n[:, :NC] for n in natural], 1)
    x_odd = jnp.concatenate([n[:, NC:] for n in natural], 1)
    fe, fo = grid(x_even, x_odd, tf, HALF, coefx, 3)
    ce, co = grid(x_even, x_odd, tc, CHALF, ccoefx, 3)
    row = lax.broadcasted_iota(jnp.int32, (96, 2 * NC), 0)
    is_coarse = lax.rem(row, 8) >= 6
    wt = jnp.where(row < 32, weights[0], jnp.where(row < 64, weights[1], weights[2]))
    be = (jnp.where(is_coarse, ce, fe) * wt).astype(BF16)
    bo = (jnp.where(is_coarse, co, fo) * wt).astype(BF16)
    slot = []
    for c in range(2):
        y = jnp.concatenate([be[:, c * NC : c * NC + NC], bo[:, c * NC : c * NC + NC]], 1)
        slot.append(dot_nt(y, onehot[...]))
    for j in range(3):
        pieces = []
        for i in range(2):
            for lev in range(NT):
                for c in range(2):
                    r = j * 32 + lev * 8
                    pieces.append(slot[c][r : r + 8, i * NC : i * NC + NC])
        back = jnp.concatenate(pieces, 0).T
        for p in range(3):
            stage[:, pl.ds(j * 24 + p * 8, 8), :] = back[p * 128 : p * 128 + 128].reshape(ND, 8, 128)
    s3[...] = stage[...].astype(BF16)
    e3a = lambda k: d_copy(k, s3, r3, 1)
    start(ND, e3a)
    r3[d] = s3[d]
    arrive(ND, e3a)
    stage[...] = r3[...].astype(F32)
    for j in range(3):
        by_p = [stage[:, pl.ds(j * 24 + p * 8, 8), :].reshape(128, 128) for p in range(3)]
        o = dot(permt[...], jnp.concatenate(by_p, 1).astype(BF16))
        s4[:, pl.ds(j * 16, 16), :] = o.astype(BF16).reshape(NZ, 16, 384)
    e3b = lambda k: z_copy(k, s4, r4, 1)
    start(NZ, e3b)
    r4[z] = s4[z]
    arrive(NZ, e3b)

    for p in range(3):
        x = r4[:, :, pl.ds(p * 128, 128)].reshape(NC, 128).astype(F32).T.astype(BF16)
        o = dot_nt(x, leg[p])
        k0 = jnp.concatenate([m0s[p]] * 4, 0)
        k1 = jnp.concatenate([m1s[p]] * 4, 0)
        part = o[:64] * k0 + o[64:] * k1
        s5[:, p] = part.astype(BF16).reshape(NT, 16, ROWS)
        keep = m0s[p, pl.ds(6, 1), pl.ds(0, NC)]
        mixed = dot(wto[pl.ds(48, 48), :], part[:, :NC] * keep, HIGHEST)
        vbuf[t, p] = mixed[:32].astype(BF16)
        oldp[p] = mixed[32:]
    e4 = lambda k: gather_copy(k, vbuf, 1)
    start(NT, e4)
    e4t = lambda k: scatter_copy(k, s5, r5, 2)
    start(NT, e4t)
    r5[t] = s5[t]
    arrive(NT, e4)

    mode = lax.rem(lax.broadcasted_iota(jnp.int32, (16, NC), 0), 8)
    rate = jnp.zeros((16, NC), F32)
    for q in range(8):
        rate = jnp.where(mode == q, rates_s[q], rate)
    col = lax.broadcasted_iota(jnp.int32, (16, NC), 1)
    lifted_mid = jnp.zeros((64, NC), F32)
    lifted_end = jnp.zeros((64, NC), F32)
    fourier, changes = [], []
    for p in range(3):
        degree = (col + folds[p]).astype(F32)
        stiff = rate * (degree * (degree + 1.0) / (NC * (NC + 1.0)))
        keep = m0s[p, pl.ds(6, 1), pl.ds(0, NC)]
        tend = (vbuf[0, p].astype(F32) + vbuf[1, p].astype(F32)) + (vbuf[2, p].astype(F32) + vbuf[3, p].astype(F32))
        old = [states[p, pl.ds(b * 16, 16), :] for b in range(3)]
        int_mid = tend[:16] - stiff * (QUAD[0][0] * old[0] + QUAD[0][1] * old[1] + QUAD[0][2] * old[2])
        int_end = tend[16:] - stiff * (QUAD[1][0] * old[0] + QUAD[1][1] * old[1] + QUAD[1][2] * old[2])
        inv = 1.0 / (1.0 + 0.5 * stiff)
        mid = (old[0] + 0.5 * stiff * old[1] + int_mid) * inv
        levels = (dot(wmix[pl.ds(0, 16), :], mid, HIGHEST) * keep).astype(BF16)
        fourier.append(dot(levels, leg[p, pl.ds(0, NC), :]))
        changes.append((mid - old[1], (mid + 0.5 * stiff * old[2] + int_end) * inv - old[2], 0.5 * inv))
    rest = jnp.zeros((80, NC), F32)
    s6[...] = jnp.concatenate(fourier + [rest], 0).T.astype(BF16).reshape(NZ, 48, 128)
    e5a = lambda k: z_copy(k, s6, r6, 2)
    start(NZ, e5a)
    r6[z] = s6[z]
    for p in range(3):
        place = wmix[pl.ds(16 + p * 64, 64), :]
        lifted_mid += dot(place, changes[p][0], HIGHEST)
        lifted_end += dot(place, changes[p][1], HIGHEST)
    lift[0] = lifted_mid.reshape(NT, 16, NC)
    lift[1] = lifted_end.reshape(NT, 16, NC)
    arrive(NZ, e5a)
    for j in range(3):
        o = dot(perm[...], r6[:, pl.ds(j * 16, 16), :].reshape(128, 128))
        cstage[:, pl.ds(j * 8, 8), :] = o.reshape(ND, 8, 128)
    s7[...] = cstage[...].astype(BF16)
    e5b = lambda k: d_copy(k, s7, r7, 2)
    start(ND, e5b)
    r7[d] = s7[d]
    arrive(NT, e4t)
    for p in range(3):
        total = (r5[0, p].astype(F32) + r5[1, p].astype(F32)) + (r5[2, p].astype(F32) + r5[3, p].astype(F32))
        for c in range(2):
            for a in range(2):
                for b in range(3):
                    r = c * 8 + b * 2 + a
                    tend_out[a, b, p, pl.ds(c, 1), :] = total[r : r + 1]
    arrive(ND, e5b)

    cstage[...] = r7[...].astype(F32)
    turned = [cstage[:, pl.ds(j * 8, 8), :].reshape(128, 128).T for j in range(3)]
    natural = []
    for c in range(2):
        rows = []
        for j in range(3):
            at = [p * 16 + c * 8 for p in range(3)]
            rows.append(jnp.concatenate([turned[j][r : r + 8] for r in at], 1))
        rows.append(jnp.zeros((8, NC), F32))
        x = jnp.concatenate(rows, 0).astype(BF16)
        natural.append(dot(x, onehot[pl.ds(0, NC), :]).astype(BF16))
    x_even = jnp.concatenate([n[:, :NC] for n in natural], 1)
    x_odd = jnp.concatenate([n[:, NC:] for n in natural], 1)
    e = dot(x_even, tc[0])
    o = dot(x_odd, tc[1])
    low, high = e + o, e - o
    c_low = jnp.concatenate([ccoef[:, :CHALF]] * 4, 0)
    c_high = jnp.concatenate([ccoef[:, CHALF:]] * 4, 0)
    prod = jnp.concatenate([c_low * low * low, c_high * high * high], 0).astype(BF16)
    back_e = dot_nt(prod, tc[0])
    back_o = dot_nt(prod, tc[1])
    row = lax.broadcasted_iota(jnp.int32, (32, 2 * NC), 0)
    wt = jnp.where(row < 8, weights[0], jnp.where(row < 16, weights[1], weights[2]))
    be = ((back_e[:32] + back_e[32:]) * wt).astype(BF16)
    bo = ((back_o[:32] - back_o[32:]) * wt).astype(BF16)
    slot = []
    for c in range(2):
        y = jnp.concatenate([be[:, c * NC : c * NC + NC], bo[:, c * NC : c * NC + NC]], 1)
        slot.append(dot_nt(y, onehot[pl.ds(0, NC), :]))
    for j in range(3):
        pieces = []
        for p in range(3):
            for c in range(2):
                pieces.append(slot[c][j * 8 : j * 8 + 8, p * 128 : p * 128 + 128])
        pieces.append(jnp.zeros((80, 128), F32))
        cstage[:, pl.ds(j * 8, 8), :] = jnp.concatenate(pieces, 0).T.reshape(ND, 8, 128)
    s8[...] = cstage[...].astype(BF16)
    e6a = lambda k: d_copy(k, s8, r8, 3)
    start(ND, e6a)
    r8[d] = s8[d]
    arrive(ND, e6a)
    cstage[...] = r8[...].astype(F32)
    for j in range(3):
        x = cstage[:, pl.ds(j * 8, 8), :].reshape(128, 128).astype(BF16)
        s9[:, pl.ds(j * 16, 16), :] = dot(permt[...], x).astype(BF16).reshape(NZ, 16, 128)
    e6b = lambda k: z_copy(k, s9, r9, 3)
    start(NZ, e6b)
    r9[z] = s9[z]
    for a in range(2):
        for b in range(2):
            for p in range(3):
                corr[a, b, p] = fs[a, b + 1, p]
    mid_own = lift[0, t]
    for p in range(3):
        for a in range(2):
            r = p * 4 + a * 2
            corr[a, 0, p, :, pl.ds(0, NC)] = fs[a, 1, p, :, pl.ds(0, NC)] + mid_own[r : r + 2]
    arrive(NZ, e6b)
    back = r9[...].reshape(NC, 128).astype(F32).T
    total = jnp.zeros((64, NC), F32)
    for p in range(3):
        part = dot_nt(back[p * 16 : p * 16 + 16].astype(BF16), leg[p, pl.ds(0, NC), :])
        keep = m0s[p, pl.ds(6, 1), pl.ds(0, NC)]
        diff = dot(wmix[pl.ds(208, 16), :], part * keep, HIGHEST) - oldp[p]
        total += dot(wmix[pl.ds(16 + p * 64, 64), :], diff * changes[p][2], HIGHEST)
    s10[...] = total.astype(BF16).reshape(NT, 16, NC)
    e7 = lambda k: scatter_copy(k, s10, r10, 3)
    start(NT, e7)
    r10[t] = s10[t]
    arrive(NT, e7)
    end_own = lift[1, t] + ((r10[0].astype(F32) + r10[1].astype(F32)) + (r10[2].astype(F32) + r10[3].astype(F32)))
    for p in range(3):
        for a in range(2):
            r = p * 4 + a * 2
            corr[a, 1, p, :, pl.ds(0, NC)] = fs[a, 2, p, :, pl.ds(0, NC)] + end_own[r : r + 2]
    for make in (e1, e4, e4t, e7):
        sent(NT, make)
    for make in (e2a, e3b, e5a, e6b):
        sent(NZ, make)
    for make in (e2b, e3a, e5b, e6a):
        sent(ND, make)


def per_device(fine_state, fold_pairs, legendre, gauss_weights, grid_coef, modes_from, modes_to, mode_rates):
    fine_table, coarse_table = tables()
    sels = selectors()
    fs = jnp.transpose(fine_state, (0, 1, 3, 2, 4))
    leg = jnp.transpose(legendre, (0, 2, 1))
    fold_col = fold_pairs.reshape(NZ, ND, 3).transpose(2, 1, 0).reshape(NC, 1)
    vm = pl.BlockSpec(memory_space=pltpu.VMEM)
    sm = pl.BlockSpec(memory_space=pltpu.SMEM)
    hbm = pl.BlockSpec(memory_space=pl.ANY)
    v = pltpu.VMEM
    dma = pltpu.SemaphoreType.DMA
    scratch = [
        v((3, ROWS, NC), BF16), v((2, 768, HALF), BF16), v((2, 768, CHALF), BF16),
        v((3, 16, ROWS), F32), v((NT, 3, 16, ROWS), BF16), v((3, 16, ROWS), F32), v((3, 16, ROWS), F32),
        v((768, 768), BF16), v((128, 128), BF16), v((128, 128), BF16),
        v((32, NLON), F32), v((32, NLON // 2), F32), v((96, 64), F32), v((224, 16), F32),
        v((NZ, 48, 384), BF16), v((NZ, 48, 384), BF16), v((ND, 80, 128), F32),
        v((ND, 80, 128), BF16), v((ND, 80, 128), BF16), v((ND, 80, 128), BF16), v((ND, 80, 128), BF16),
        v((NZ, 48, 384), BF16), v((NZ, 48, 384), BF16),
        v((NT, 3, 32, NC), BF16), v((NT, 3, 16, ROWS), BF16), v((NT, 3, 16, ROWS), BF16),
        v((3, 48, NC), F32), v((3, 16, NC), F32), v((2, NT, 16, NC), F32),
        v((NZ, 48, 128), BF16), v((NZ, 48, 128), BF16), v((ND, 32, 128), F32),
        v((ND, 32, 128), BF16), v((ND, 32, 128), BF16), v((ND, 32, 128), BF16), v((ND, 32, 128), BF16),
        v((NZ, 48, 128), BF16), v((NZ, 48, 128), BF16), v((NT, 16, NC), BF16), v((NT, 16, NC), BF16),
        dma((3,)), dma((4, NZ)), dma((4, NZ)), dma((4, ND)), dma((4, ND)),
        dma((4, NT)), dma((4, NT)),
    ]
    corr, tend = pl.pallas_call(
        kernel,
        out_shape=(
            jax.ShapeDtypeStruct((2, 2, 3, 2, ROWS), F32),
            jax.ShapeDtypeStruct((2, 3, 3, 2, ROWS), F32),
        ),
        in_specs=[vm, hbm, sm, vm, sm, sm, vm, vm, vm, hbm, hbm] + [vm] * 6,
        out_specs=(vm, vm),
        scratch_shapes=scratch,
        compiler_params=pltpu.CompilerParams(
            collective_id=0, has_side_effects=True, vmem_limit_bytes=48 * 1024 * 1024
        ),
        name="sweep",
    )(
        fs, leg, fold_pairs, fold_col, gauss_weights, mode_rates, grid_coef, modes_to, modes_from,
        jnp.asarray(fine_table), jnp.asarray(coarse_table), *[jnp.asarray(s) for s in sels],
    )
    return (jnp.transpose(corr, (0, 1, 3, 2, 4)), jnp.transpose(tend, (0, 1, 3, 2, 4)))


def solution(mesh):
    placed = (
        P("lev", None, None, "wave", None),
        P(),
        P("wave", "lev", None),
        P("lev"),
        P(),
        P(),
        P(),
        P(),
    )
    return jax.shard_map(
        per_device,
        mesh=mesh,
        in_specs=placed,
        out_specs=(P("lev", None, None, "wave", None), P("lev", None, None, "wave", None)),
        check_vma=False,
    )
```

```python
import functools
import math

import jax
import jax.numpy as jnp
import ml_dtypes
import numpy as np
from jax import lax
from jax.experimental import pallas as pl
from jax.experimental.pallas import tpu as pltpu
from jax.sharding import PartitionSpec as P

F32 = jnp.float32
BF16 = jnp.bfloat16
HIGHEST = lax.Precision.HIGHEST
MESH = pl.DeviceIdType.MESH

NLON, LEV, WAVES, ROWS, NC = 2560, 8, 768, 769, 384
HALF, CHALF = NLON // 2, NLON // 4
NZ, ND, NT = 8, 16, 4
FACTOR = 2.0 * WAVES / NLON
QUAD = ((5.0 / 24.0, 1.0 / 3.0, -1.0 / 24.0), (-1.0 / 24.0, 1.0 / 3.0, 5.0 / 24.0))


def table(waves, points, amplitude, count):
    turns = np.outer(waves, np.arange(count)) % points
    angles = turns * (2.0 * math.pi / points)
    return np.concatenate([np.cos(angles), -np.sin(angles)], 0).reshape(2, len(waves), count) * amplitude


def tables():
    t = np.arange(192)
    fine, coarse = [], []
    for parity in (0, 1):
        low = 2 * t + parity
        high = (WAVES - 2 - 2 * t) + parity
        fine.append(table(np.concatenate([low, high]), NLON, WAVES**-0.5, HALF).reshape(768, HALF))
        coarse.append(table(low, NLON // 2, NC**-0.5, CHALF).reshape(NC, CHALF))
    as_bf16 = lambda parts: np.stack(parts).astype(np.float32).astype(ml_dtypes.bfloat16)
    return as_bf16(fine), as_bf16(coarse)


def selectors():
    to_rows = np.zeros((80, 8), np.float32)
    to_mask = np.zeros((80, 64), np.float32)
    to_cols = np.zeros((8, 64), np.float32)
    for lev in range(4):
        for c in range(2):
            for rho in range(8):
                col = lev * 16 + c * 8 + rho
                to_cols[lev * 2 + rho % 2, col] = 1
                node = rho // 2
                for q in range(8):
                    if node < 3:
                        to_mask[node * 16 + c * 8 + q, col] = 1
                        to_mask[48 + c * 8 + q, col] = QUAD[0][node]
                        to_mask[64 + c * 8 + q, col] = QUAD[1][node]
    for row in range(80):
        to_rows[row, row % 8] = 1
    mix_cols = np.zeros((8, 16), np.float32)
    mix_rows = np.zeros((208, 8), np.float32)
    mix_mask = np.zeros((208, 16), np.float32)
    for c in range(2):
        for q in range(8):
            mix_cols[q, c * 8 + q] = 1
            for a in range(8):
                mix_rows[c * 8 + a, a] = 1
                mix_mask[c * 8 + a, c * 8 + q] = 1
                for p in range(3):
                    row = 16 + p * 64 + (a // 2) * 16 + p * 4 + (a % 2) * 2 + c
                    mix_rows[row, a] = 1
                    mix_mask[row, c * 8 + q] = 1
    return to_rows, to_mask, to_cols, mix_rows, mix_mask, mix_cols


def dot(a, b, precision=None):
    return lax.dot_general(a, b, (((1,), (0,)), ((), ())), precision=precision, preferred_element_type=F32)


def dot_nt(a, b):
    return lax.dot_general(a, b, (((1,), (1,)), ((), ())), preferred_element_type=F32)


def kernel(
    fs_hbm, leg_hbm, fold_hbm, gauss_hbm, rates_hbm, coef_hbm, mto_hbm, mfrom_hbm, tf_hbm, tc_hbm,
    to_rows_hbm, to_mask_hbm, to_cols_hbm, mix_rows_hbm, mix_mask_hbm, mix_cols_hbm,
    corr, tend_out,
    fs, fold_s, fold_v, gauss_s, rates_s, coef, mto, mfrom,
    to_rows, to_mask, to_cols, mix_rows, mix_mask, mix_cols,
    leg, tf, tc, xf, gat, m0s, m1s, onehot, perm, permt, coefx, ccoef, wto, wmix, states, parts, oldback, lift, xold,
    stage, stageb, cstage,
    s1a, r1a, s2a, r2a, s1b, r1b, s2b, r2b, s3a, r3a, s4a, r4a, s3b, r3b, s4b, r4b,
    vbuf, s5, r5, s6, r6, s7, r7, s8, r8, s9, r9, s10, r10,
    load_sem, z_send, z_recv, d_send, d_recv, lev_send, lev_recv,
):
    w = lax.axis_index("wave")
    t = lax.axis_index("lev")
    z, d = w // ND, w % ND

    pairs = (
        (leg_hbm, leg), (tf_hbm, tf), (tc_hbm, tc), (fs_hbm, fs), (fold_hbm, fold_s), (fold_hbm, fold_v),
        (gauss_hbm, gauss_s), (rates_hbm, rates_s), (coef_hbm, coef), (mto_hbm, mto), (mfrom_hbm, mfrom),
        (to_rows_hbm, to_rows), (to_mask_hbm, to_mask), (to_cols_hbm, to_cols), (mix_rows_hbm, mix_rows),
        (mix_mask_hbm, mix_mask), (mix_cols_hbm, mix_cols),
    )
    loads = [pltpu.make_async_copy(src, dst, load_sem.at[n]) for n, (src, dst) in enumerate(pairs)]
    for n in (3, 4, 5, 0) + tuple(range(6, 17)) + (1, 2):
        loads[n].start()

    barrier = pltpu.get_barrier_semaphore()

    def lev_dev(k):
        return {"lev": lax.rem(t + k, NT)}

    def z_dev(k):
        return {"wave": lax.rem(z + k, NZ) * ND + d}

    def d_dev(k):
        return {"wave": z * ND + lax.rem(d + k, ND)}

    groups = ((NT, lev_dev), (NZ, z_dev), (ND, d_dev))
    for count, dev in groups:
        @pl.loop(1, count)
        def _(k):
            pl.semaphore_signal(barrier, inc=1, device_id=dev(k), device_id_type=MESH)

    def lev_copy(k, src, dst, row):
        return pltpu.make_async_remote_copy(
            src_ref=src, dst_ref=dst, send_sem=lev_send.at[row, k], recv_sem=lev_recv.at[row, k],
            device_id=lev_dev(k), device_id_type=MESH)

    def z_copy(k, src, dst, row):
        return pltpu.make_async_remote_copy(
            src_ref=src.at[lax.rem(z + k, NZ)], dst_ref=dst.at[z], send_sem=z_send.at[row, k],
            recv_sem=z_recv.at[row, k], device_id=z_dev(k), device_id_type=MESH)

    def d_copy(k, src, dst, row):
        return pltpu.make_async_remote_copy(
            src_ref=src.at[lax.rem(d + k, ND)], dst_ref=dst.at[d], send_sem=d_send.at[row, k],
            recv_sem=d_recv.at[row, k], device_id=d_dev(k), device_id_type=MESH)

    def gather_copy(k, buf, row):
        return lev_copy(k, buf.at[t], buf.at[t], row)

    def scatter_copy(k, src, dst, row):
        return lev_copy(k, src.at[lax.rem(t + k, NT)], dst.at[t], row)

    def start(count, make):
        @pl.loop(1, count)
        def _(k):
            make(k).start()

    def arrive(count, make):
        @pl.loop(1, count)
        def _(k):
            make(k).wait_recv()

    def sent(count, make):
        @pl.loop(1, count)
        def _(k):
            make(k).wait_send()

    loads[3].wait()
    for p in range(3):
        for c in range(2):
            for a in range(2):
                for b in range(3):
                    xf[p, pl.ds(c * 8 + b * 2 + a, 1), :] = fs[a, b, p, pl.ds(c, 1), :]
                xf[p, pl.ds(c * 8 + 6 + a, 1), :] = fs[a, 1, p, pl.ds(c, 1), :]
    gat[t] = xf[...].astype(BF16)
    pl.semaphore_wait(barrier, (NT - 1) + (NZ - 1) + (ND - 1))
    e1 = lambda k: gather_copy(k, gat, 0)
    start(NT, e1)

    for n in range(4, 17):
        loads[n].wait()
    folds = [fold_s[w * 3 + p] for p in range(3)]
    rho = lax.rem(lax.broadcasted_iota(jnp.int32, (16, ROWS), 0), 8)
    row_r = lax.broadcasted_iota(jnp.int32, (16, ROWS), 1)
    for p in range(3):
        first = jnp.where(row_r < WAVES - folds[p], 1.0, 0.0)
        keep = jnp.where(row_r < NC - folds[p], 1.0, 0.0)
        m0s[p] = jnp.where(rho < 6, first, keep)
        m1s[p] = jnp.where(rho < 6, 1.0 - first, 0.0)
    pr = lax.broadcasted_iota(jnp.int32, (128, 128), 0)
    pc = lax.broadcasted_iota(jnp.int32, (128, 128), 1)
    perm[...] = jnp.where(pc == lax.rem(pr, NZ) * ND + pr // NZ, 1.0, 0.0).astype(BF16)
    permt[...] = jnp.where(pr == lax.rem(pc, NZ) * ND + pc // NZ, 1.0, 0.0).astype(BF16)
    stageb[:, pl.ds(24, 8), :] = jnp.zeros((ND, 8, 128), F32)
    arrive(NT, e1)
    loads[0].wait()

    def inverse(p):
        x = gat[:, p].reshape(64, ROWS)
        k0 = jnp.concatenate([m0s[p].astype(BF16)] * 4, 0)
        k1 = jnp.concatenate([m1s[p].astype(BF16)] * 4, 0)
        return dot(jnp.concatenate([x * k0, x * k1], 0), leg[p]).T.reshape(NZ, 48, 128)

    for p in range(2):
        s1a[:, :, pl.ds(p * 128, 128)] = inverse(p).astype(BF16)
    e2az = lambda k: z_copy(k, s1a, r1a, 0)
    start(NZ, e2az)
    r1a[z] = s1a[z]
    f = inverse(2).astype(BF16)
    for j in range(3):
        o = dot(perm[...], f[:, j * 16 : j * 16 + 16].reshape(128, 128))
        stageb[:, pl.ds(j * 8, 8), :] = o.reshape(ND, 8, 128)
    s1b[...] = stageb[...].astype(BF16)
    e2bd = lambda k: d_copy(k, s1b, r1b, 0)
    start(ND, e2bd)
    r1b[d] = s1b[d]

    sr = lax.broadcasted_iota(jnp.int32, (NC, NC), 0)
    sc = lax.broadcasted_iota(jnp.int32, (NC, NC), 1)
    slot_of = (lax.rem(sc, NZ) * ND + lax.rem(sc, 128) // NZ) * 3 + sc // 128
    to_order = jnp.where(sr == slot_of, 1.0, 0.0)
    fold = dot(jnp.broadcast_to(fold_v[...].reshape(1, NC).astype(F32), (8, NC)), to_order, HIGHEST)[:1]
    fold = (fold + 0.5).astype(jnp.int32)
    half_fold, odd = fold // 2, lax.rem(fold, 2)
    rows_n = lax.broadcasted_iota(jnp.int32, (2 * NC, NC), 0)
    onehot[:, pl.ds(0, NC)] = jnp.where(rows_n == 192 + half_fold + NC * (1 - odd), 1.0, 0.0).astype(BF16)
    onehot[:, pl.ds(NC, NC)] = jnp.where(rows_n == half_fold + NC * odd, 1.0, 0.0).astype(BF16)
    onehot[:, pl.ds(2 * NC, NC)] = jnp.where(rows_n == 192 + half_fold + NC * odd, 1.0, 0.0).astype(BF16)

    arrive(NZ, e2az)
    for j in range(3):
        o = dot(perm[...], r1a[:, pl.ds(j * 16, 16), :].reshape(128, 256))
        for p in range(2):
            stage[:, pl.ds(j * 16 + p * 8, 8), :] = o[:, p * 128 : p * 128 + 128].reshape(ND, 8, 128)
    s2a[...] = stage[...].astype(BF16)
    e2ad = lambda k: d_copy(k, s2a, r2a, 1)
    start(ND, e2ad)
    r2a[d] = s2a[d]
    arrive(ND, e2bd)
    stageb[...] = r1b[...].astype(F32)
    for j in range(3):
        x = stageb[:, pl.ds(j * 8, 8), :].reshape(128, 128).astype(BF16)
        s2b[:, pl.ds(j * 16, 16), :] = dot(permt[...], x).astype(BF16).reshape(NZ, 16, 128)
    e2bz = lambda k: z_copy(k, s2b, r2b, 1)
    start(NZ, e2bz)
    r2b[z] = s2b[z]

    for lev in range(NT):
        for n in range(4):
            coefx[pl.ds(lev * 8 + n * 2, 2), :] = coef[pl.ds(lev * 2, 2), :]
    sel_r = lax.broadcasted_iota(jnp.int32, (256, 128), 0)
    sel_c = lax.broadcasted_iota(jnp.int32, (256, 128), 1)
    even = jnp.where(sel_r == 2 * sel_c, 1.0, 0.0)
    chunks = jnp.concatenate([coef[:, pl.ds(n * 256, 256)] for n in range(10)], 0)
    picked = dot(chunks, even, HIGHEST)
    ccoef[...] = jnp.concatenate([picked[n * 8 : n * 8 + 8] for n in range(10)], 1)
    weights = [gauss_s[z * 48 + j * 16 + d] * FACTOR for j in range(3)]
    loads[1].wait()
    loads[2].wait()
    arrive(NZ, e2bz)
    arrive(ND, e2ad)

    stage[...] = r2a[...].astype(F32)
    turned = []
    for j in range(3):
        by_p = [stage[:, pl.ds(j * 16 + p * 8, 8), :].reshape(128, 128) for p in range(2)]
        by_p.append(dot(perm[...], r2b[:, pl.ds(j * 16, 16), :].reshape(128, 128)))
        turned.append(jnp.concatenate(by_p, 0).T)
    natural = []
    for c in range(2):
        rows = []
        for j in range(3):
            members = []
            for i in (1, 0):
                at = [i * 64 + lev * 16 + c * 8 for lev in range(NT)]
                members.append(jnp.concatenate([turned[j][r : r + 8] for r in at], 0))
            rows.append(jnp.concatenate(members, 1))
            for lev in range(NT):
                r = lev * 16 + c * 8 + 6
                xold[pl.ds(j * 8 + lev * 2, 2), pl.ds(c * NC, NC)] = turned[j][r : r + 2]
        x = jnp.concatenate(rows, 0).astype(BF16)
        natural.append(dot_nt(x, onehot[:, pl.ds(0, 2 * NC)]).astype(BF16))

    def grid(x_even, x_odd, tab, c_low, c_high):
        e = dot(x_even, tab[0])
        o = dot(x_odd, tab[1])
        low, high = e + o, e - o
        prod = jnp.concatenate([c_low * low * low, c_high * high * high], 0).astype(BF16)
        n = low.shape[0]
        back_e = dot_nt(prod, tab[0])
        back_o = dot_nt(prod, tab[1])
        return back_e[:n] + back_e[n:], back_o[:n] - back_o[n:]

    x_even = jnp.concatenate([n[:, :NC] for n in natural], 1)
    x_odd = jnp.concatenate([n[:, NC:] for n in natural], 1)
    fe, fo = grid(
        x_even, x_odd, tf,
        jnp.concatenate([coefx[:, pl.ds(0, HALF)]] * 3, 0), jnp.concatenate([coefx[:, pl.ds(HALF, HALF)]] * 3, 0),
    )
    row = lax.broadcasted_iota(jnp.int32, (96, 1), 0)
    wt = jnp.where(row < 32, weights[0], jnp.where(row < 64, weights[1], weights[2]))
    wt = jnp.where(lax.rem(row, 8) < 6, wt, 0.0)
    be = (fe * wt).astype(BF16)
    bo = (fo * wt).astype(BF16)
    slot = []
    for c in range(2):
        y = jnp.concatenate([be[:, c * NC : c * NC + NC], bo[:, c * NC : c * NC + NC]], 1)
        slot.append(dot(y, onehot[:, pl.ds(0, 2 * NC)]))
    for j in range(3):
        pieces = []
        for i in range(2):
            for lev in range(NT):
                for c in range(2):
                    r = j * 32 + lev * 8
                    pieces.append(slot[c][r : r + 8, (1 - i) * NC : (2 - i) * NC])
        back = jnp.concatenate(pieces, 0).T
        for p in range(2):
            stage[:, pl.ds(j * 16 + p * 8, 8), :] = back[p * 128 : p * 128 + 128].reshape(ND, 8, 128)
        o = dot(permt[...], back[256:].astype(BF16))
        s3b[:, pl.ds(j * 16, 16), :] = o.astype(BF16).reshape(NZ, 16, 128)
    s3a[...] = stage[...].astype(BF16)
    e3ad = lambda k: d_copy(k, s3a, r3a, 2)
    e3bz = lambda k: z_copy(k, s3b, r3b, 2)
    start(ND, e3ad)
    start(NZ, e3bz)
    r3a[d] = s3a[d]
    r3b[z] = s3b[z]

    row = lax.broadcasted_iota(jnp.int32, (32, 1), 0)
    wt_c = jnp.where(row < 8, weights[0], jnp.where(row < 16, weights[1], weights[2]))

    def coarse_grid(x):
        n = dot_nt(x, onehot[:, pl.ds(NC, 2 * NC)]).astype(BF16)
        ge, go = grid(
            n[:, :NC], n[:, NC:], tc,
            jnp.concatenate([ccoef[:, pl.ds(0, CHALF)]] * 4, 0), jnp.concatenate([ccoef[:, pl.ds(CHALF, CHALF)]] * 4, 0),
        )
        return jnp.concatenate([ge * wt_c, go * wt_c], 1)

    xold[pl.ds(24, 8), :] = jnp.zeros((8, 2 * NC), F32)
    oldback[...] = coarse_grid(xold[...].astype(BF16))

    arrive(ND, e3ad)
    stage[...] = r3a[...].astype(F32)
    for j in range(3):
        by_p = [stage[:, pl.ds(j * 16 + p * 8, 8), :].reshape(128, 128) for p in range(2)]
        o = dot(permt[...], jnp.concatenate(by_p, 1).astype(BF16))
        s4a[:, pl.ds(j * 16, 16), :] = o.astype(BF16).reshape(NZ, 16, 256)
    e3az = lambda k: z_copy(k, s4a, r4a, 3)
    start(NZ, e3az)
    r4a[z] = s4a[z]
    arrive(NZ, e3bz)
    for j in range(3):
        o = dot(perm[...], r3b[:, pl.ds(j * 16, 16), :].reshape(128, 128))
        stageb[:, pl.ds(j * 8, 8), :] = o.reshape(ND, 8, 128)
    s4b[...] = stageb[...].astype(BF16)
    e3bd = lambda k: d_copy(k, s4b, r4b, 3)
    start(ND, e3bd)
    r4b[d] = s4b[d]

    wto[...] = dot(dot(to_rows[...], mto[...], HIGHEST), to_cols[...], HIGHEST) * to_mask[...]
    wmix[pl.ds(0, 208), :] = dot(dot(mix_rows[...], mfrom[...], HIGHEST), mix_cols[...], HIGHEST) * mix_mask[...]
    wmix[pl.ds(208, 16), :] = (
        dot(dot(mix_rows[pl.ds(0, 16), :], mto[...], HIGHEST), mix_cols[...], HIGHEST) * mix_mask[pl.ds(0, 16), :]
    )
    keeps = [m0s[p, pl.ds(6, 1), pl.ds(0, NC)] for p in range(3)]
    for p in range(3):
        x = gat[:, p, :, pl.ds(0, NC)].reshape(64, NC).astype(F32)
        states[p] = dot(wto[pl.ds(0, 48), :], x, HIGHEST) * keeps[p]

    def forward(p, x):
        o = dot_nt(x.T.astype(BF16), leg[p])
        k0 = jnp.concatenate([m0s[p]] * 4, 0)
        k1 = jnp.concatenate([m1s[p]] * 4, 0)
        part = o[:64] * k0 + o[64:] * k1
        parts[p] = part
        vbuf[t, p] = dot(wto[pl.ds(48, 32), :], part[:, :NC] * keeps[p], HIGHEST).astype(BF16)

    arrive(ND, e3bd)
    stageb[...] = r4b[...].astype(F32)
    pieces = []
    for j in range(3):
        x = stageb[:, pl.ds(j * 8, 8), :].reshape(128, 128).astype(BF16)
        pieces.append(dot(permt[...], x).reshape(NZ, 16, 128))
    forward(2, jnp.concatenate(pieces, 1).reshape(NC, 128))
    arrive(NZ, e3az)
    for p in range(2):
        forward(p, r4a[:, :, pl.ds(p * 128, 128)].reshape(NC, 128).astype(F32))
    e4 = lambda k: gather_copy(k, vbuf, 1)
    start(NT, e4)
    for p in range(3):
        s5[:, p] = parts[p].astype(BF16).reshape(NT, 16, ROWS)

    mode = lax.rem(lax.broadcasted_iota(jnp.int32, (16, NC), 0), 8)
    rate = jnp.zeros((16, NC), F32)
    for q in range(8):
        rate = jnp.where(mode == q, rates_s[q], rate)
    col = lax.broadcasted_iota(jnp.int32, (16, NC), 1)
    known = []
    for p in range(3):
        degree = (col + folds[p]).astype(F32)
        stiff = rate * (degree * (degree + 1.0) / (NC * (NC + 1.0)))
        old = [states[p, pl.ds(b * 16, 16), :] for b in range(3)]
        int_mid = stiff * (QUAD[0][0] * old[0] + QUAD[0][1] * old[1] + QUAD[0][2] * old[2])
        int_end = stiff * (QUAD[1][0] * old[0] + QUAD[1][1] * old[1] + QUAD[1][2] * old[2])
        inv = 1.0 / (1.0 + 0.5 * stiff)
        known.append((inv, old[0] + 0.5 * stiff * old[1] - int_mid, 0.5 * stiff * old[2] - int_end, old[1], old[2]))
    arrive(NT, e4)
    e4t = lambda k: scatter_copy(k, s5, r5, 2)
    start(NT, e4t)
    r5[t] = s5[t]
    fourier, changes = [], []
    for p in range(3):
        inv, known_mid, known_end, old_1, old_2 = known[p]
        tend = (vbuf[0, p].astype(F32) + vbuf[1, p].astype(F32)) + (vbuf[2, p].astype(F32) + vbuf[3, p].astype(F32))
        mid = (known_mid + tend[:16]) * inv
        levels = (dot(wmix[pl.ds(0, 16), :], mid, HIGHEST) * keeps[p]).astype(BF16)
        fourier.append(dot(levels, leg[p, pl.ds(0, NC), :]))
        changes.append((mid - old_1, (mid + known_end + tend[16:]) * inv - old_2, 0.5 * inv))
    rest = jnp.zeros((80, NC), F32)
    f = jnp.concatenate(fourier + [rest], 0).T.reshape(NZ, 48, 128)
    s6[:, pl.ds(0, 16), :] = (f[:, :16] + pltpu.roll(f[:, 16:32], 64, 2)).astype(BF16)
    s6[:, pl.ds(16, 16), :] = f[:, 32:].astype(BF16)
    e5a = lambda k: z_copy(k, s6, r6, 4)
    start(NZ, e5a)
    r6[z] = s6[z]
    lifted_mid = jnp.zeros((64, NC), F32)
    lifted_end = jnp.zeros((64, NC), F32)
    for p in range(3):
        place = wmix[pl.ds(16 + p * 64, 64), :]
        lifted_mid += dot(place, changes[p][0], HIGHEST)
        lifted_end += dot(place, changes[p][1], HIGHEST)
    lift[0] = lifted_mid.reshape(NT, 16, NC)
    lift[1] = lifted_end.reshape(NT, 16, NC)
    arrive(NZ, e5a)
    for h in range(2):
        o = dot(perm[...], r6[:, pl.ds(h * 16, 16), :].reshape(128, 128))
        cstage[:, pl.ds(h * 8, 8), :] = o.reshape(ND, 8, 128)
    s7[...] = cstage[...].astype(BF16)
    e5b = lambda k: d_copy(k, s7, r7, 4)
    start(ND, e5b)
    r7[d] = s7[d]
    arrive(NT, e4t)
    for p in range(3):
        total = (r5[0, p].astype(F32) + r5[1, p].astype(F32)) + (r5[2, p].astype(F32) + r5[3, p].astype(F32))
        for c in range(2):
            for a in range(2):
                for b in range(3):
                    r = c * 8 + b * 2 + a
                    tend_out[a, b, p, pl.ds(c, 1), :] = total[r : r + 1]
    arrive(ND, e5b)

    cstage[...] = r7[...].astype(F32)
    turned = [cstage[:, pl.ds(h * 8, 8), :].reshape(128, 128).T for h in range(2)]
    at_j = ((0, 0), (0, 64), (1, 0))
    rows = []
    for h, first_row in at_j:
        at = [first_row + p * 16 + c * 8 for c in range(2) for p in range(3)]
        rows.append(jnp.concatenate([turned[h][r : r + 8] for r in at], 1))
    rows.append(jnp.zeros((8, 2 * NC), F32))
    fresh = coarse_grid(jnp.concatenate(rows, 0).astype(BF16))
    slot = dot((fresh - oldback[...]).astype(BF16), onehot[:, pl.ds(NC, 2 * NC)])
    by_j = []
    for j in range(3):
        by_j.append([slot[j * 8 : j * 8 + 8, c * NC + p * 128 : c * NC + p * 128 + 128] for p in range(3) for c in range(2)])
    gap = [jnp.zeros((16, 128), F32)]
    for h, group in enumerate((by_j[0] + gap + by_j[1] + gap, by_j[2] + gap * 5)):
        cstage[:, pl.ds(h * 8, 8), :] = jnp.concatenate(group, 0).T.reshape(ND, 8, 128)
    s8[...] = cstage[...].astype(BF16)
    e6a = lambda k: d_copy(k, s8, r8, 5)
    start(ND, e6a)
    r8[d] = s8[d]
    for a in range(2):
        for b in range(2):
            for p in range(3):
                corr[a, b, p] = fs[a, b + 1, p]
    mid_own = lift[0, t]
    for p in range(3):
        for a in range(2):
            r = p * 4 + a * 2
            corr[a, 0, p, :, pl.ds(0, NC)] = fs[a, 1, p, :, pl.ds(0, NC)] + mid_own[r : r + 2]
    arrive(ND, e6a)
    cstage[...] = r8[...].astype(F32)
    for h in range(2):
        x = cstage[:, pl.ds(h * 8, 8), :].reshape(128, 128).astype(BF16)
        s9[:, pl.ds(h * 16, 16), :] = dot(permt[...], x).astype(BF16).reshape(NZ, 16, 128)
    e6b = lambda k: z_copy(k, s9, r9, 5)
    start(NZ, e6b)
    r9[z] = s9[z]
    arrive(NZ, e6b)
    x = r9[...].astype(F32)
    back = jnp.concatenate([x[:, :16], pltpu.roll(x[:, :16], 64, 2), x[:, 16:]], 1).reshape(NC, 128).T
    total = jnp.zeros((64, NC), F32)
    for p in range(3):
        part = dot_nt(back[p * 16 : p * 16 + 16].astype(BF16), leg[p, pl.ds(0, NC), :])
        diff = dot(wmix[pl.ds(208, 16), :], part * keeps[p], HIGHEST)
        total += dot(wmix[pl.ds(16 + p * 64, 64), :], diff * changes[p][2], HIGHEST)
    s10[...] = total.astype(BF16).reshape(NT, 16, NC)
    e7 = lambda k: scatter_copy(k, s10, r10, 3)
    start(NT, e7)
    r10[t] = s10[t]
    arrive(NT, e7)
    end_own = lift[1, t] + ((r10[0].astype(F32) + r10[1].astype(F32)) + (r10[2].astype(F32) + r10[3].astype(F32)))
    for p in range(3):
        for a in range(2):
            r = p * 4 + a * 2
            corr[a, 1, p, :, pl.ds(0, NC)] = fs[a, 2, p, :, pl.ds(0, NC)] + end_own[r : r + 2]
    for make in (e1, e4, e4t, e7):
        sent(NT, make)
    for make in (e2az, e2bz, e3bz, e3az, e5a, e6b):
        sent(NZ, make)
    for make in (e2bd, e2ad, e3ad, e3bd, e5b, e6a):
        sent(ND, make)


def per_device(fine_state, fold_pairs, legendre, gauss_weights, grid_coef, modes_from, modes_to, mode_rates):
    fine_table, coarse_table = tables()
    sels = selectors()
    fs = jnp.transpose(fine_state, (0, 1, 3, 2, 4))
    leg = jnp.transpose(legendre, (0, 2, 1))
    vm = pl.BlockSpec(memory_space=pltpu.VMEM)
    hbm = pl.BlockSpec(memory_space=pltpu.HBM)
    v, sm = pltpu.VMEM, pltpu.SMEM
    dma = pltpu.SemaphoreType.DMA
    scratch = [
        v((2, 3, 3, 2, ROWS), F32), sm((NC,), jnp.int32), v((NC,), jnp.int32), sm((NC,), F32), sm((LEV,), F32),
        v((LEV, NLON), F32), v((8, 8), F32), v((8, 8), F32), v((80, 8), F32), v((80, 64), F32), v((8, 64), F32),
        v((208, 8), F32), v((208, 16), F32), v((8, 16), F32),
        v((3, ROWS, NC), BF16), v((2, 768, HALF), BF16), v((2, NC, CHALF), BF16),
        v((3, 16, ROWS), F32), v((NT, 3, 16, ROWS), BF16), v((3, 16, ROWS), F32), v((3, 16, ROWS), F32),
        v((768, 3 * NC), BF16), v((128, 128), BF16), v((128, 128), BF16),
        v((32, NLON), F32), v((LEV, NLON // 2), F32), v((80, 64), F32), v((224, 16), F32),
        v((3, 48, NC), F32), v((3, 64, ROWS), F32), v((32, 768), F32), v((2, NT, 16, NC), F32), v((32, 768), F32),
        v((ND, 48, 128), F32), v((ND, 32, 128), F32), v((ND, 16, 128), F32),
    ]
    z_two, z_one = v((NZ, 48, 256), BF16), v((NZ, 48, 128), BF16)
    d_two, d_one = v((ND, 48, 128), BF16), v((ND, 32, 128), BF16)
    scratch += [z_two, z_two, d_two, d_two, d_one, d_one, z_one, z_one]
    scratch += [d_two, d_two, z_two, z_two, z_one, z_one, d_one, d_one]
    scratch += [v((NT, 3, 32, NC), BF16), v((NT, 3, 16, ROWS), BF16), v((NT, 3, 16, ROWS), BF16)]
    z_coarse, d_coarse, lev_coarse = v((NZ, 32, 128), BF16), v((ND, 16, 128), BF16), v((NT, 16, NC), BF16)
    scratch += [z_coarse] * 2 + [d_coarse] * 4 + [z_coarse] * 2 + [lev_coarse] * 2
    scratch += [
        dma((17,)), dma((6, NZ)), dma((6, NZ)), dma((6, ND)), dma((6, ND)), dma((4, NT)), dma((4, NT)),
    ]
    corr, tend = pl.pallas_call(
        kernel,
        out_shape=(
            jax.ShapeDtypeStruct((2, 2, 3, 2, ROWS), F32),
            jax.ShapeDtypeStruct((2, 3, 3, 2, ROWS), F32),
        ),
        in_specs=[hbm] * 16,
        out_specs=(vm, vm),
        scratch_shapes=scratch,
        compiler_params=pltpu.CompilerParams(
            collective_id=0, has_side_effects=True, vmem_limit_bytes=64 * 1024 * 1024
        ),
        name="sweep",
    )(
        fs, leg, fold_pairs, gauss_weights, mode_rates, grid_coef, modes_to, modes_from,
        jnp.asarray(fine_table), jnp.asarray(coarse_table), *[jnp.asarray(s) for s in sels],
    )
    return (jnp.transpose(corr, (0, 1, 3, 2, 4)), jnp.transpose(tend, (0, 1, 3, 2, 4)))


def solution(mesh):
    placed = (
        P("lev", None, None, "wave", None),
        P(),
        P("wave", "lev", None),
        P("lev"),
        P(),
        P(),
        P(),
        P(),
    )
    return jax.shard_map(
        per_device,
        mesh=mesh,
        in_specs=placed,
        out_specs=(P("lev", None, None, "wave", None), P("lev", None, None, "wave", None)),
        check_vma=False,
    )
```

```python
import functools
import math

import jax
import jax.numpy as jnp
import ml_dtypes
import numpy as np
from jax import lax
from jax.experimental import pallas as pl
from jax.experimental.pallas import tpu as pltpu
from jax.sharding import PartitionSpec as P

F32 = jnp.float32
BF16 = jnp.bfloat16
HIGHEST = lax.Precision.HIGHEST
MESH = pl.DeviceIdType.MESH

NLON, LEV, WAVES, ROWS, NC = 2560, 8, 768, 769, 384
HALF, CLON = NLON // 2, NLON // 2
NZ, ND, NT = 8, 16, 4
FACTOR = 2.0 * WAVES / NLON
QUAD = ((5.0 / 24.0, 1.0 / 3.0, -1.0 / 24.0), (-1.0 / 24.0, 1.0 / 3.0, 5.0 / 24.0))


def table(waves, points, amplitude, count):
    turns = np.outer(waves, np.arange(count)) % points
    angles = turns * (2.0 * math.pi / points)
    return np.concatenate([np.cos(angles), -np.sin(angles)], 0).reshape(2, len(waves), count) * amplitude


def tables():
    t = np.arange(192)
    fine = []
    for parity in (0, 1):
        low = 2 * t + parity
        high = (WAVES - 2 - 2 * t) + parity
        fine.append(table(np.concatenate([low, high]), NLON, WAVES**-0.5, HALF).reshape(768, HALF))
    coarse = table(np.arange(NC), NLON // 2, NC**-0.5, NLON // 2)
    as_bf16 = lambda values: values.astype(np.float32).astype(ml_dtypes.bfloat16)
    return as_bf16(np.stack(fine)), as_bf16(coarse)


def selectors():
    to_rows = np.zeros((80, 8), np.float32)
    to_mask = np.zeros((80, 64), np.float32)
    to_cols = np.zeros((8, 64), np.float32)
    for lev in range(4):
        for c in range(2):
            for rho in range(8):
                col = lev * 16 + c * 8 + rho
                to_cols[lev * 2 + rho % 2, col] = 1
                node = rho // 2
                for q in range(8):
                    if node < 3:
                        to_mask[node * 16 + c * 8 + q, col] = 1
                        to_mask[48 + c * 8 + q, col] = QUAD[0][node]
                        to_mask[64 + c * 8 + q, col] = QUAD[1][node]
    for row in range(80):
        to_rows[row, row % 8] = 1
    mix_cols = np.zeros((8, 48), np.float32)
    mix_rows = np.zeros((80, 8), np.float32)
    mix_mask = np.zeros((80, 48), np.float32)
    for c in range(2):
        for q in range(8):
            for p in range(3):
                mix_cols[q, p * 16 + c * 8 + q] = 1
            for a in range(8):
                mix_rows[c * 8 + a, a] = 1
                mix_mask[c * 8 + a, c * 8 + q] = 1
                for p in range(3):
                    row = 16 + (a // 2) * 16 + p * 4 + (a % 2) * 2 + c
                    mix_rows[row, a] = 1
                    mix_mask[row, p * 16 + c * 8 + q] = 1
    return to_rows, to_mask, to_cols, mix_rows, mix_mask, mix_cols


def dot(a, b, precision=None):
    return lax.dot_general(a, b, (((1,), (0,)), ((), ())), precision=precision, preferred_element_type=F32)


def dot_nt(a, b):
    return lax.dot_general(a, b, (((1,), (1,)), ((), ())), preferred_element_type=F32)


def kernel(
    fs_hbm, leg_hbm, fold_hbm, gauss_hbm, rates_hbm, coef_hbm, mto_hbm, mfrom_hbm, tf_hbm, tc_hbm,
    to_rows_hbm, to_mask_hbm, to_cols_hbm, mix_rows_hbm, mix_mask_hbm, mix_cols_hbm,
    corr, tend_out,
    fs, fold_s, fold_v, gauss_s, rates_s, coef, mto, mfrom,
    to_rows, to_mask, to_cols, mix_rows, mix_mask, mix_cols,
    leg, tf, tc, xf, gat, m0s, m1s, onehot, ordered, tslot, perm, permt, coefx, ccoef, wto, wmix, wplace, states, parts, oldback, lift, xold,
    stage, stageb, cstage,
    s1a, r1a, s2a, r2a, s1b, r1b, s2b, r2b, s3a, r3a, s4a, r4a, s3b, r3b, s4b, r4b,
    vmid, vend, s5, r5, s6, r6, s7, r7, s8, r8, s9, r9, s10, r10,
    load_sem, z_send, z_recv, d_send, d_recv, lev_send, lev_recv,
):
    w = lax.axis_index("wave")
    t = lax.axis_index("lev")
    z, d = w // ND, w % ND

    pairs = (
        (leg_hbm, leg), (tf_hbm, tf), (tc_hbm, tc), (fs_hbm, fs), (fold_hbm, fold_s), (fold_hbm, fold_v),
        (gauss_hbm, gauss_s), (rates_hbm, rates_s), (coef_hbm, coef), (mto_hbm, mto), (mfrom_hbm, mfrom),
        (to_rows_hbm, to_rows), (to_mask_hbm, to_mask), (to_cols_hbm, to_cols), (mix_rows_hbm, mix_rows),
        (mix_mask_hbm, mix_mask), (mix_cols_hbm, mix_cols),
    )
    loads = [pltpu.make_async_copy(src, dst, load_sem.at[n]) for n, (src, dst) in enumerate(pairs)]
    for n in (3, 4, 5, 0) + tuple(range(6, 17)) + (1, 2):
        loads[n].start()

    barrier = pltpu.get_barrier_semaphore()

    def lev_dev(k):
        return {"lev": lax.rem(t + k, NT)}

    def z_dev(k):
        return {"wave": lax.rem(z + k, NZ) * ND + d}

    def d_dev(k):
        return {"wave": z * ND + lax.rem(d + k, ND)}

    groups = ((NT, lev_dev), (NZ, z_dev), (ND, d_dev))
    for count, dev in groups:
        @pl.loop(1, count)
        def _(k):
            pl.semaphore_signal(barrier, inc=1, device_id=dev(k), device_id_type=MESH)

    def lev_copy(k, src, dst, row):
        return pltpu.make_async_remote_copy(
            src_ref=src, dst_ref=dst, send_sem=lev_send.at[row, k], recv_sem=lev_recv.at[row, k],
            device_id=lev_dev(k), device_id_type=MESH)

    def z_copy(k, src, dst, row):
        return pltpu.make_async_remote_copy(
            src_ref=src.at[lax.rem(z + k, NZ)], dst_ref=dst.at[z], send_sem=z_send.at[row, k],
            recv_sem=z_recv.at[row, k], device_id=z_dev(k), device_id_type=MESH)

    def d_copy(k, src, dst, row):
        return pltpu.make_async_remote_copy(
            src_ref=src.at[lax.rem(d + k, ND)], dst_ref=dst.at[d], send_sem=d_send.at[row, k],
            recv_sem=d_recv.at[row, k], device_id=d_dev(k), device_id_type=MESH)

    def gather_copy(k, buf, row):
        return lev_copy(k, buf.at[t], buf.at[t], row)

    def scatter_copy(k, src, dst, row):
        return lev_copy(k, src.at[lax.rem(t + k, NT)], dst.at[t], row)

    def start(count, make):
        @pl.loop(1, count)
        def _(k):
            make(k).start()

    def arrive(count, make):
        @pl.loop(1, count)
        def _(k):
            make(k).wait_recv()

    def sent(count, make):
        @pl.loop(1, count)
        def _(k):
            make(k).wait_send()

    loads[3].wait()
    for p in range(3):
        for c in range(2):
            for a in range(2):
                for b in range(3):
                    xf[p, pl.ds(c * 8 + b * 2 + a, 1), :] = fs[a, b, p, pl.ds(c, 1), :]
                xf[p, pl.ds(c * 8 + 6 + a, 1), :] = fs[a, 1, p, pl.ds(c, 1), :]
    for p in range(3):
        gat[p, t] = xf[p].astype(BF16)
    pl.semaphore_wait(barrier, (NT - 1) + (NZ - 1) + (ND - 1))
    e1 = [lambda k, p=p: gather_copy(k, gat.at[p], 5 + p) for p in range(3)]
    for p in (2, 0, 1):
        start(NT, e1[p])

    for n in range(4, 17):
        loads[n].wait()
    folds = [fold_s[w * 3 + p] for p in range(3)]
    rho = lax.rem(lax.broadcasted_iota(jnp.int32, (16, ROWS), 0), 8)
    row_r = lax.broadcasted_iota(jnp.int32, (16, ROWS), 1)
    for p in range(3):
        first = jnp.where(row_r < WAVES - folds[p], 1.0, 0.0)
        keep = jnp.where(row_r < NC - folds[p], 1.0, 0.0)
        m0s[p] = jnp.where(rho < 6, first, keep)
        m1s[p] = jnp.where(rho < 6, 1.0 - first, 0.0)
    pr = lax.broadcasted_iota(jnp.int32, (128, 128), 0)
    pc = lax.broadcasted_iota(jnp.int32, (128, 128), 1)
    perm[...] = jnp.where(pc == lax.rem(pr, NZ) * ND + pr // NZ, 1.0, 0.0).astype(BF16)
    permt[...] = jnp.where(pr == lax.rem(pc, NZ) * ND + pc // NZ, 1.0, 0.0).astype(BF16)
    stageb[:, pl.ds(24, 8), :] = jnp.zeros((ND, 8, 128), F32)
    loads[0].wait()

    def inverse(p):
        arrive(NT, e1[p])
        x = gat[p].reshape(64, ROWS)
        k0 = jnp.concatenate([m0s[p].astype(BF16)] * 4, 0)
        k1 = jnp.concatenate([m1s[p].astype(BF16)] * 4, 0)
        return dot(jnp.concatenate([x * k0, x * k1], 0), leg[p]).T.reshape(NZ, 48, 128)

    f = inverse(2).astype(BF16)
    for j in range(3):
        o = dot(perm[...], f[:, j * 16 : j * 16 + 16].reshape(128, 128))
        stageb[:, pl.ds(j * 8, 8), :] = o.reshape(ND, 8, 128)
    s1b[...] = stageb[...].astype(BF16)
    e2bd = lambda k: d_copy(k, s1b, r1b, 0)
    start(ND, e2bd)
    r1b[d] = s1b[d]

    for p in range(2):
        s1a[:, :, pl.ds(p * 128, 128)] = inverse(p).astype(BF16)
    e2az = lambda k: z_copy(k, s1a, r1a, 0)
    start(NZ, e2az)
    r1a[z] = s1a[z]

    sr = lax.broadcasted_iota(jnp.int32, (NC, NC), 0)
    sc = lax.broadcasted_iota(jnp.int32, (NC, NC), 1)
    slot_of = (lax.rem(sc, NZ) * ND + lax.rem(sc, 128) // NZ) * 3 + sc // 128
    to_order = jnp.where(sr == slot_of, 1.0, 0.0)
    fold = dot(jnp.broadcast_to(fold_v[...].reshape(1, NC).astype(F32), (8, NC)), to_order, HIGHEST)[:1]
    fold = (fold + 0.5).astype(jnp.int32)
    half_fold, odd = fold // 2, lax.rem(fold, 2)
    rows_n = lax.broadcasted_iota(jnp.int32, (2 * NC, NC), 0)
    onehot[:, pl.ds(0, NC)] = jnp.where(rows_n == half_fold + NC * odd, 1.0, 0.0).astype(BF16)
    onehot[:, pl.ds(NC, NC)] = jnp.where(rows_n == 192 + half_fold + NC * (1 - odd), 1.0, 0.0).astype(BF16)
    ordered[...] = jnp.where(sr == fold, 1.0, 0.0).T.astype(BF16)

    arrive(NZ, e2az)
    for j in range(3):
        o = dot(perm[...], r1a[:, pl.ds(j * 16, 16), :].reshape(128, 256))
        for p in range(2):
            stage[:, pl.ds(j * 16 + p * 8, 8), :] = o[:, p * 128 : p * 128 + 128].reshape(ND, 8, 128)
    s2a[...] = stage[...].astype(BF16)
    e2ad = lambda k: d_copy(k, s2a, r2a, 1)
    start(ND, e2ad)
    r2a[d] = s2a[d]
    arrive(ND, e2bd)
    stageb[...] = r1b[...].astype(F32)
    for j in range(3):
        x = stageb[:, pl.ds(j * 8, 8), :].reshape(128, 128).astype(BF16)
        s2b[:, pl.ds(j * 16, 16), :] = dot(permt[...], x).astype(BF16).reshape(NZ, 16, 128)
    e2bz = lambda k: z_copy(k, s2b, r2b, 1)
    start(NZ, e2bz)
    r2b[z] = s2b[z]

    for lev in range(NT):
        for n in range(4):
            coefx[pl.ds(lev * 8 + n * 2, 2), :] = coef[pl.ds(lev * 2, 2), :]
    sel_r = lax.broadcasted_iota(jnp.int32, (256, 128), 0)
    sel_c = lax.broadcasted_iota(jnp.int32, (256, 128), 1)
    even = jnp.where(sel_r == 2 * sel_c, 1.0, 0.0)
    chunks = jnp.concatenate([coef[:, pl.ds(n * 256, 256)] for n in range(10)], 0)
    picked = dot(chunks, even, HIGHEST)
    ccoef[...] = jnp.concatenate([picked[n * 8 : n * 8 + 8] for n in range(10)], 1)
    weights = [gauss_s[z * 48 + j * 16 + d] * FACTOR for j in range(3)]
    loads[1].wait()
    loads[2].wait()
    arrive(NZ, e2bz)
    arrive(ND, e2ad)

    stage[...] = r2a[...].astype(F32)
    turned = []
    for j in range(3):
        by_p = [stage[:, pl.ds(j * 16 + p * 8, 8), :].reshape(128, 128) for p in range(2)]
        by_p.append(dot(perm[...], r2b[:, pl.ds(j * 16, 16), :].reshape(128, 128)))
        turned.append(jnp.concatenate(by_p, 0).T)
    natural = []
    for c in range(2):
        rows = []
        for j in range(3):
            members = []
            for i in range(2):
                at = [i * 64 + lev * 16 + c * 8 for lev in range(NT)]
                members.append(jnp.concatenate([turned[j][r : r + 8] for r in at], 0))
            rows.append(jnp.concatenate(members, 1))
            for lev in range(NT):
                r = lev * 16 + c * 8 + 6
                xold[pl.ds(j * 8 + lev * 2, 2), pl.ds(c * NC, NC)] = turned[j][r : r + 2]
        x = jnp.concatenate(rows, 0).astype(BF16)
        natural.append(dot_nt(x, onehot[...]).astype(BF16))

    def grid(x_even, x_odd, tab, c_low, c_high):
        e = dot(x_even, tab[0])
        o = dot(x_odd, tab[1])
        low, high = e + o, e - o
        prod = jnp.concatenate([c_low * low * low, c_high * high * high], 0).astype(BF16)
        n = low.shape[0]
        back_e = dot_nt(prod, tab[0])
        back_o = dot_nt(prod, tab[1])
        return back_e[:n] + back_e[n:], back_o[:n] - back_o[n:]

    x_even = jnp.concatenate([n[:, :NC] for n in natural], 1)
    x_odd = jnp.concatenate([n[:, NC:] for n in natural], 1)
    fe, fo = grid(
        x_even, x_odd, tf,
        jnp.concatenate([coefx[:, pl.ds(0, HALF)]] * 3, 0), jnp.concatenate([coefx[:, pl.ds(HALF, HALF)]] * 3, 0),
    )
    row = lax.broadcasted_iota(jnp.int32, (96, 1), 0)
    wt = jnp.where(row < 32, weights[0], jnp.where(row < 64, weights[1], weights[2]))
    wt = jnp.where(lax.rem(row, 8) < 6, wt, 0.0)
    be = (fe * wt).astype(BF16)
    bo = (fo * wt).astype(BF16)
    slot = []
    for c in range(2):
        y = jnp.concatenate([be[:, c * NC : c * NC + NC], bo[:, c * NC : c * NC + NC]], 1)
        slot.append(dot(y, onehot[...]))
    for j in range(3):
        pieces = []
        for i in range(2):
            for lev in range(NT):
                for c in range(2):
                    r = j * 32 + lev * 8
                    pieces.append(slot[c][r : r + 8, i * NC : i * NC + NC])
        back = jnp.concatenate(pieces, 0).T
        for p in range(2):
            stage[:, pl.ds(j * 16 + p * 8, 8), :] = back[p * 128 : p * 128 + 128].reshape(ND, 8, 128)
        o = dot(permt[...], back[256:].astype(BF16))
        s3b[:, pl.ds(j * 16, 16), :] = o.astype(BF16).reshape(NZ, 16, 128)
    s3a[...] = stage[...].astype(BF16)
    e3ad = lambda k: d_copy(k, s3a, r3a, 2)
    e3bz = lambda k: z_copy(k, s3b, r3b, 2)
    start(ND, e3ad)
    start(NZ, e3bz)
    r3a[d] = s3a[d]
    r3b[z] = s3b[z]

    row = lax.broadcasted_iota(jnp.int32, (32, 1), 0)
    wt_c = jnp.where(row < 8, weights[0], jnp.where(row < 16, weights[1], weights[2]))

    def coarse_grid(x):
        g = dot(x, tslot[...])
        prod = (jnp.concatenate([ccoef[...]] * 4, 0) * g * g).astype(BF16)
        return dot_nt(prod, tslot[...]) * wt_c

    for c in range(2):
        tslot[pl.ds(c * NC, NC), :] = dot(ordered[...], tc[c]).astype(BF16)
    xold[pl.ds(24, 8), :] = jnp.zeros((8, 2 * NC), F32)
    oldback[...] = coarse_grid(xold[...].astype(BF16))

    arrive(ND, e3ad)
    stage[...] = r3a[...].astype(F32)
    for j in range(3):
        by_p = [stage[:, pl.ds(j * 16 + p * 8, 8), :].reshape(128, 128) for p in range(2)]
        o = dot(permt[...], jnp.concatenate(by_p, 1).astype(BF16))
        s4a[:, pl.ds(j * 16, 16), :] = o.astype(BF16).reshape(NZ, 16, 256)
    e3az = lambda k: z_copy(k, s4a, r4a, 3)
    start(NZ, e3az)
    r4a[z] = s4a[z]
    arrive(NZ, e3bz)
    for j in range(3):
        o = dot(perm[...], r3b[:, pl.ds(j * 16, 16), :].reshape(128, 128))
        stageb[:, pl.ds(j * 8, 8), :] = o.reshape(ND, 8, 128)
    s4b[...] = stageb[...].astype(BF16)
    e3bd = lambda k: d_copy(k, s4b, r4b, 3)
    start(ND, e3bd)
    r4b[d] = s4b[d]

    wto[...] = dot(dot(to_rows[...], mto[...], HIGHEST), to_cols[...], HIGHEST) * to_mask[...]
    mixed = dot(dot(mix_rows[...], mfrom[...], HIGHEST), mix_cols[...], HIGHEST) * mix_mask[...]
    wmix[pl.ds(0, 16), :] = mixed[:16, :16]
    wplace[...] = mixed[16:]
    mixed = dot(dot(mix_rows[pl.ds(0, 16), :], mto[...], HIGHEST), mix_cols[...], HIGHEST) * mix_mask[pl.ds(0, 16), :]
    wmix[pl.ds(16, 16), :] = mixed[:, :16]
    keeps = [m0s[p, pl.ds(6, 1), pl.ds(0, NC)] for p in range(3)]
    for p in range(3):
        x = gat[p, :, :, pl.ds(0, NC)].reshape(64, NC).astype(F32)
        states[p] = dot(wto[pl.ds(0, 48), :], x, HIGHEST) * keeps[p]

    def forward(p, x):
        o = dot_nt(x.T.astype(BF16), leg[p])
        k0 = jnp.concatenate([m0s[p]] * 4, 0)
        k1 = jnp.concatenate([m1s[p]] * 4, 0)
        part = o[:64] * k0 + o[64:] * k1
        parts[p] = part
        mixed = dot(wto[pl.ds(48, 32), :], part[:, :NC] * keeps[p], HIGHEST).astype(BF16)
        vmid[t, p] = mixed[:16]
        vend[t, p] = mixed[16:]

    arrive(ND, e3bd)
    stageb[...] = r4b[...].astype(F32)
    pieces = []
    for j in range(3):
        x = stageb[:, pl.ds(j * 8, 8), :].reshape(128, 128).astype(BF16)
        pieces.append(dot(permt[...], x).reshape(NZ, 16, 128))
    forward(2, jnp.concatenate(pieces, 1).reshape(NC, 128))
    arrive(NZ, e3az)
    for p in range(2):
        forward(p, r4a[:, :, pl.ds(p * 128, 128)].reshape(NC, 128).astype(F32))
    e4 = lambda k: gather_copy(k, vmid, 1)
    start(NT, e4)
    for p in range(3):
        s5[:, p] = parts[p].astype(BF16).reshape(NT, 16, ROWS)

    mode = lax.rem(lax.broadcasted_iota(jnp.int32, (16, NC), 0), 8)
    rate = jnp.zeros((16, NC), F32)
    for q in range(8):
        rate = jnp.where(mode == q, rates_s[q], rate)
    col = lax.broadcasted_iota(jnp.int32, (16, NC), 1)
    known = []
    for p in range(3):
        degree = (col + folds[p]).astype(F32)
        stiff = rate * (degree * (degree + 1.0) / (NC * (NC + 1.0)))
        old = [states[p, pl.ds(b * 16, 16), :] for b in range(3)]
        int_mid = stiff * (QUAD[0][0] * old[0] + QUAD[0][1] * old[1] + QUAD[0][2] * old[2])
        int_end = stiff * (QUAD[1][0] * old[0] + QUAD[1][1] * old[1] + QUAD[1][2] * old[2])
        inv = 1.0 / (1.0 + 0.5 * stiff)
        known.append((inv, old[0] + 0.5 * stiff * old[1] - int_mid, 0.5 * stiff * old[2] - int_end, old[1], old[2]))
    arrive(NT, e4)
    fourier, mids = [], []
    for p in range(3):
        inv, known_mid, known_end, old_1, old_2 = known[p]
        tend = (vmid[0, p].astype(F32) + vmid[1, p].astype(F32)) + (vmid[2, p].astype(F32) + vmid[3, p].astype(F32))
        mid = (known_mid + tend) * inv
        levels = (dot(wmix[pl.ds(0, 16), :], mid, HIGHEST) * keeps[p]).astype(BF16)
        fourier.append(dot(levels, leg[p, pl.ds(0, NC), :]))
        mids.append(mid)
    rest = jnp.zeros((80, NC), F32)
    f = jnp.concatenate(fourier + [rest], 0).T.reshape(NZ, 48, 128)
    s6[:, pl.ds(0, 16), :] = (f[:, :16] + pltpu.roll(f[:, 16:32], 64, 2)).astype(BF16)
    s6[:, pl.ds(16, 16), :] = f[:, 32:].astype(BF16)
    e5a = lambda k: z_copy(k, s6, r6, 4)
    start(NZ, e5a)
    r6[z] = s6[z]
    e4e = lambda k: gather_copy(k, vend, 4)
    start(NT, e4e)
    e4t = lambda k: scatter_copy(k, s5, r5, 2)
    start(NT, e4t)
    r5[t] = s5[t]
    place = wplace[...]
    lift[0] = dot(place, jnp.concatenate([mids[p] - known[p][3] for p in range(3)], 0), HIGHEST).reshape(NT, 16, NC)
    arrive(NZ, e5a)
    for h in range(2):
        o = dot(perm[...], r6[:, pl.ds(h * 16, 16), :].reshape(128, 128))
        cstage[:, pl.ds(h * 8, 8), :] = o.reshape(ND, 8, 128)
    s7[...] = cstage[...].astype(BF16)
    e5b = lambda k: d_copy(k, s7, r7, 4)
    start(ND, e5b)
    r7[d] = s7[d]
    arrive(NT, e4e)
    ends = []
    for p in range(3):
        inv, known_mid, known_end, old_1, old_2 = known[p]
        tend = (vend[0, p].astype(F32) + vend[1, p].astype(F32)) + (vend[2, p].astype(F32) + vend[3, p].astype(F32))
        ends.append((mids[p] + known_end + tend) * inv - old_2)
    lift[1] = dot(place, jnp.concatenate(ends, 0), HIGHEST).reshape(NT, 16, NC)
    arrive(ND, e5b)

    cstage[...] = r7[...].astype(F32)
    turned = [cstage[:, pl.ds(h * 8, 8), :].reshape(128, 128).T for h in range(2)]
    at_j = ((0, 0), (0, 64), (1, 0))
    rows = []
    for h, first_row in at_j:
        at = [first_row + p * 16 + c * 8 for c in range(2) for p in range(3)]
        rows.append(jnp.concatenate([turned[h][r : r + 8] for r in at], 1))
    rows.append(jnp.zeros((8, 2 * NC), F32))
    fresh = coarse_grid(jnp.concatenate(rows, 0).astype(BF16))
    slot = (fresh - oldback[...]).astype(BF16).astype(F32)
    by_j = []
    for j in range(3):
        by_j.append([slot[j * 8 : j * 8 + 8, c * NC + p * 128 : c * NC + p * 128 + 128] for p in range(3) for c in range(2)])
    gap = [jnp.zeros((16, 128), F32)]
    for h, group in enumerate((by_j[0] + gap + by_j[1] + gap, by_j[2] + gap * 5)):
        cstage[:, pl.ds(h * 8, 8), :] = jnp.concatenate(group, 0).T.reshape(ND, 8, 128)
    s8[...] = cstage[...].astype(BF16)
    e6a = lambda k: d_copy(k, s8, r8, 5)
    start(ND, e6a)
    r8[d] = s8[d]
    for a in range(2):
        for b in range(2):
            for p in range(3):
                corr[a, b, p] = fs[a, b + 1, p]
    mid_own = lift[0, t]
    for p in range(3):
        for a in range(2):
            r = p * 4 + a * 2
            corr[a, 0, p, :, pl.ds(0, NC)] = fs[a, 1, p, :, pl.ds(0, NC)] + mid_own[r : r + 2]
    for make in (*e1, e4, e4e, e4t):
        sent(NT, make)
    for make in (e2az, e2bz, e3bz, e3az, e5a):
        sent(NZ, make)
    for make in (e2bd, e2ad, e3ad, e3bd, e5b):
        sent(ND, make)
    arrive(NT, e4t)
    for p in range(3):
        total = (r5[0, p].astype(F32) + r5[1, p].astype(F32)) + (r5[2, p].astype(F32) + r5[3, p].astype(F32))
        for c in range(2):
            for a in range(2):
                for b in range(3):
                    r = c * 8 + b * 2 + a
                    tend_out[a, b, p, pl.ds(c, 1), :] = total[r : r + 1]
    arrive(ND, e6a)
    cstage[...] = r8[...].astype(F32)
    for h in range(2):
        x = cstage[:, pl.ds(h * 8, 8), :].reshape(128, 128).astype(BF16)
        s9[:, pl.ds(h * 16, 16), :] = dot(permt[...], x).astype(BF16).reshape(NZ, 16, 128)
    e6b = lambda k: z_copy(k, s9, r9, 5)
    start(NZ, e6b)
    r9[z] = s9[z]
    sent(ND, e6a)
    arrive(NZ, e6b)
    x = r9[...].astype(F32)
    back = jnp.concatenate([x[:, :16], pltpu.roll(x[:, :16], 64, 2), x[:, 16:]], 1).reshape(NC, 128).T
    partial = []
    for p in range(3):
        partial.append(dot_nt(back[p * 16 : p * 16 + 16].astype(BF16), leg[p, pl.ds(0, NC), :]) * keeps[p])
    diff = dot(wmix[pl.ds(16, 16), :], jnp.concatenate(partial, 1), HIGHEST)
    scaled = [diff[:, p * NC : p * NC + NC] * (0.5 * known[p][0]) for p in range(3)]
    total = dot(place, jnp.concatenate(scaled, 0), HIGHEST)
    s10[...] = total.astype(BF16).reshape(NT, 16, NC)
    e7 = lambda k: scatter_copy(k, s10, r10, 3)
    start(NT, e7)
    r10[t] = s10[t]
    arrive(NT, e7)
    end_own = lift[1, t] + ((r10[0].astype(F32) + r10[1].astype(F32)) + (r10[2].astype(F32) + r10[3].astype(F32)))
    for p in range(3):
        for a in range(2):
            r = p * 4 + a * 2
            corr[a, 1, p, :, pl.ds(0, NC)] = fs[a, 2, p, :, pl.ds(0, NC)] + end_own[r : r + 2]
    sent(NT, e7)
    sent(NZ, e6b)


def per_device(fine_state, fold_pairs, legendre, gauss_weights, grid_coef, modes_from, modes_to, mode_rates):
    fine_table, coarse_table = tables()
    sels = selectors()
    fs = jnp.transpose(fine_state, (0, 1, 3, 2, 4))
    leg = jnp.transpose(legendre, (0, 2, 1))
    vm = pl.BlockSpec(memory_space=pltpu.VMEM)
    hbm = pl.BlockSpec(memory_space=pltpu.HBM)
    v, sm = pltpu.VMEM, pltpu.SMEM
    dma = pltpu.SemaphoreType.DMA
    scratch = [
        v((2, 3, 3, 2, ROWS), F32), sm((NC,), jnp.int32), v((NC,), jnp.int32), sm((NC,), F32), sm((LEV,), F32),
        v((LEV, NLON), F32), v((8, 8), F32), v((8, 8), F32), v((80, 8), F32), v((80, 64), F32), v((8, 64), F32),
        v((80, 8), F32), v((80, 48), F32), v((8, 48), F32),
        v((3, ROWS, NC), BF16), v((2, 768, HALF), BF16), v((2, NC, CLON), BF16),
        v((3, 16, ROWS), F32), v((3, NT, 16, ROWS), BF16), v((3, 16, ROWS), F32), v((3, 16, ROWS), F32),
        v((768, 768), BF16), v((NC, NC), BF16), v((768, CLON), BF16), v((128, 128), BF16), v((128, 128), BF16),
        v((32, NLON), F32), v((LEV, CLON), F32), v((80, 64), F32), v((32, 16), F32), v((64, 48), F32),
        v((3, 48, NC), F32), v((3, 64, ROWS), F32), v((32, 768), F32), v((2, NT, 16, NC), F32), v((32, 768), F32),
        v((ND, 48, 128), F32), v((ND, 32, 128), F32), v((ND, 16, 128), F32),
    ]
    z_two, z_one = v((NZ, 48, 256), BF16), v((NZ, 48, 128), BF16)
    d_two, d_one = v((ND, 48, 128), BF16), v((ND, 32, 128), BF16)
    scratch += [z_two, z_two, d_two, d_two, d_one, d_one, z_one, z_one]
    scratch += [d_two, d_two, z_two, z_two, z_one, z_one, d_one, d_one]
    scratch += [v((NT, 3, 16, NC), BF16), v((NT, 3, 16, NC), BF16), v((NT, 3, 16, ROWS), BF16), v((NT, 3, 16, ROWS), BF16)]
    z_coarse, d_coarse, lev_coarse = v((NZ, 32, 128), BF16), v((ND, 16, 128), BF16), v((NT, 16, NC), BF16)
    scratch += [z_coarse] * 2 + [d_coarse] * 4 + [z_coarse] * 2 + [lev_coarse] * 2
    scratch += [
        dma((17,)), dma((6, NZ)), dma((6, NZ)), dma((6, ND)), dma((6, ND)), dma((8, NT)), dma((8, NT)),
    ]
    operands = [
        fs, leg, fold_pairs, gauss_weights, mode_rates, grid_coef, modes_to, modes_from,
        jnp.asarray(fine_table), jnp.asarray(coarse_table), *[jnp.asarray(s) for s in sels],
    ]
    corr, tend = pl.pallas_call(
        kernel,
        out_shape=(
            jax.ShapeDtypeStruct((2, 2, 3, 2, ROWS), F32),
            jax.ShapeDtypeStruct((2, 3, 3, 2, ROWS), F32),
        ),
        in_specs=[hbm] * 16,
        out_specs=(vm, vm),
        scratch_shapes=scratch,
        compiler_params=pltpu.CompilerParams(
            collective_id=0, has_side_effects=True, vmem_limit_bytes=48 * 1024 * 1024
        ),
        name="sweep",
    )(*[pltpu.with_memory_space_constraint(x, pltpu.HBM) for x in operands])
    return (jnp.transpose(corr, (0, 1, 3, 2, 4)), jnp.transpose(tend, (0, 1, 3, 2, 4)))


def solution(mesh):
    placed = (
        P("lev", None, None, "wave", None),
        P(),
        P("wave", "lev", None),
        P("lev"),
        P(),
        P(),
        P(),
        P(),
    )
    return jax.shard_map(
        per_device,
        mesh=mesh,
        in_specs=placed,
        out_specs=(P("lev", None, None, "wave", None), P("lev", None, None, "wave", None)),
        check_vma=False,
    )
```

```python
import functools
import math

import jax
import jax.numpy as jnp
import ml_dtypes
import numpy as np
from jax import lax
from jax.experimental import pallas as pl
from jax.experimental.pallas import tpu as pltpu
from jax.sharding import PartitionSpec as P

F32 = jnp.float32
BF16 = jnp.bfloat16
HIGHEST = lax.Precision.HIGHEST
MESH = pl.DeviceIdType.MESH

NLON, LEV, WAVES, ROWS, NC = 2560, 8, 768, 769, 384
HALF, CLON = NLON // 2, NLON // 2
NZ, ND, NT = 8, 16, 4
FACTOR = 2.0 * WAVES / NLON
QUAD = ((5.0 / 24.0, 1.0 / 3.0, -1.0 / 24.0), (-1.0 / 24.0, 1.0 / 3.0, 5.0 / 24.0))


def table(waves, points, amplitude, count):
    turns = np.outer(waves, np.arange(count)) % points
    angles = turns * (2.0 * math.pi / points)
    return np.concatenate([np.cos(angles), -np.sin(angles)], 0).reshape(2, len(waves), count) * amplitude


def tables():
    t = np.arange(192)
    fine = []
    for parity in (0, 1):
        low = 2 * t + parity
        high = (WAVES - 2 - 2 * t) + parity
        fine.append(table(np.concatenate([low, high]), NLON, WAVES**-0.5, HALF).reshape(768, HALF))
    coarse = table(np.arange(NC), NLON // 2, NC**-0.5, NLON // 2)
    as_bf16 = lambda values: values.astype(np.float32).astype(ml_dtypes.bfloat16)
    return as_bf16(np.stack(fine)), as_bf16(coarse)


def selectors():
    to_rows = np.zeros((80, 8), np.float32)
    to_mask = np.zeros((80, 64), np.float32)
    to_cols = np.zeros((8, 64), np.float32)
    for lev in range(4):
        for c in range(2):
            for rho in range(8):
                col = lev * 16 + c * 8 + rho
                to_cols[lev * 2 + rho % 2, col] = 1
                node = rho // 2
                for q in range(8):
                    if node < 3:
                        to_mask[node * 16 + c * 8 + q, col] = 1
                        to_mask[48 + c * 8 + q, col] = QUAD[0][node]
                        to_mask[64 + c * 8 + q, col] = QUAD[1][node]
    for row in range(80):
        to_rows[row, row % 8] = 1
    mix_cols = np.zeros((8, 48), np.float32)
    mix_rows = np.zeros((80, 8), np.float32)
    mix_mask = np.zeros((80, 48), np.float32)
    for c in range(2):
        for q in range(8):
            for p in range(3):
                mix_cols[q, p * 16 + c * 8 + q] = 1
            for a in range(8):
                mix_rows[c * 8 + a, a] = 1
                mix_mask[c * 8 + a, c * 8 + q] = 1
                for p in range(3):
                    row = 16 + (a // 2) * 16 + p * 4 + (a % 2) * 2 + c
                    mix_rows[row, a] = 1
                    mix_mask[row, p * 16 + c * 8 + q] = 1
    return to_rows, to_mask, to_cols, mix_rows, mix_mask, mix_cols


def dot(a, b, precision=None):
    return lax.dot_general(a, b, (((1,), (0,)), ((), ())), precision=precision, preferred_element_type=F32)


def dot_nt(a, b):
    return lax.dot_general(a, b, (((1,), (1,)), ((), ())), preferred_element_type=F32)


def kernel(
    fs_hbm, leg_hbm, fold_hbm, gauss_hbm, rates_hbm, coef_hbm, mto_hbm, mfrom_hbm, tf_hbm, tc_hbm,
    to_rows_hbm, to_mask_hbm, to_cols_hbm, mix_rows_hbm, mix_mask_hbm, mix_cols_hbm,
    corr, tend_out,
    fs, fold_s, fold_v, gauss_s, rates_s, coef, mto, mfrom,
    to_rows, to_mask, to_cols, mix_rows, mix_mask, mix_cols,
    leg, tf, tc, xf, gat, m0s, m1s, onehot, ordered, tslot, perm, permt, coefx, ccoef, wto, wmix, wplace, states, parts, oldback, lift, xold,
    stage, stageb, cstage,
    s1a, r1a, s2a, r2a, s1b, r1b, s2b, r2b, s3a, r3a, s4a, r4a, s3b, r3b, s4b, r4b,
    vmid, vend, s5, r5, s6, r6, s7, r7, s8, r8, s9, r9, s10, r10,
    load_sem, z_send, z_recv, d_send, d_recv, lev_send, lev_recv,
):
    w = lax.axis_index("wave")
    t = lax.axis_index("lev")
    z, d = w // ND, w % ND

    pairs = (
        (leg_hbm, leg), (tf_hbm, tf), (tc_hbm, tc), (fs_hbm, fs), (fold_hbm, fold_s), (fold_hbm, fold_v),
        (gauss_hbm, gauss_s), (rates_hbm, rates_s), (coef_hbm, coef), (mto_hbm, mto), (mfrom_hbm, mfrom),
        (to_rows_hbm, to_rows), (to_mask_hbm, to_mask), (to_cols_hbm, to_cols), (mix_rows_hbm, mix_rows),
        (mix_mask_hbm, mix_mask), (mix_cols_hbm, mix_cols),
    )
    loads = [pltpu.make_async_copy(src, dst, load_sem.at[n]) for n, (src, dst) in enumerate(pairs)]
    loads[3].start()

    barrier = pltpu.get_barrier_semaphore()

    def lev_dev(k):
        return {"lev": lax.rem(t + k, NT)}

    def z_dev(k):
        return {"wave": lax.rem(z + k, NZ) * ND + d}

    def d_dev(k):
        return {"wave": z * ND + lax.rem(d + k, ND)}

    groups = ((NT, lev_dev), (NZ, z_dev), (ND, d_dev))
    for count, dev in groups:
        @pl.loop(1, count)
        def _(k):
            pl.semaphore_signal(barrier, inc=1, device_id=dev(k), device_id_type=MESH)

    for n in (0, 4, 5) + tuple(range(6, 17)) + (1, 2):
        loads[n].start()

    def lev_copy(k, src, dst, row):
        return pltpu.make_async_remote_copy(
            src_ref=src, dst_ref=dst, send_sem=lev_send.at[row, k], recv_sem=lev_recv.at[row, k],
            device_id=lev_dev(k), device_id_type=MESH)

    def z_copy(k, src, dst, row):
        return pltpu.make_async_remote_copy(
            src_ref=src.at[lax.rem(z + k, NZ)], dst_ref=dst.at[z], send_sem=z_send.at[row, k],
            recv_sem=z_recv.at[row, k], device_id=z_dev(k), device_id_type=MESH)

    def d_copy(k, src, dst, row):
        return pltpu.make_async_remote_copy(
            src_ref=src.at[lax.rem(d + k, ND)], dst_ref=dst.at[d], send_sem=d_send.at[row, k],
            recv_sem=d_recv.at[row, k], device_id=d_dev(k), device_id_type=MESH)

    def gather_copy(k, buf, row):
        return lev_copy(k, buf.at[t], buf.at[t], row)

    def scatter_copy(k, src, dst, row):
        return lev_copy(k, src.at[lax.rem(t + k, NT)], dst.at[t], row)

    def start(count, make):
        @pl.loop(1, count)
        def _(k):
            make(k).start()

    def arrive(count, make):
        @pl.loop(1, count)
        def _(k):
            make(k).wait_recv()

    def sent(count, make):
        @pl.loop(1, count)
        def _(k):
            make(k).wait_send()

    loads[3].wait()
    for p in range(3):
        for c in range(2):
            for a in range(2):
                for b in range(3):
                    xf[p, pl.ds(c * 8 + b * 2 + a, 1), :] = fs[a, b, p, pl.ds(c, 1), :]
                xf[p, pl.ds(c * 8 + 6 + a, 1), :] = fs[a, 1, p, pl.ds(c, 1), :]
    for p in range(3):
        gat[p, t] = xf[p].astype(BF16)
    pl.semaphore_wait(barrier, (NT - 1) + (NZ - 1) + (ND - 1))
    e1 = [lambda k, p=p: gather_copy(k, gat.at[p], 5 + p) for p in range(3)]
    for p in (2, 0, 1):
        start(NT, e1[p])

    for n in range(4, 17):
        loads[n].wait()
    folds = [fold_s[w * 3 + p] for p in range(3)]
    rho = lax.rem(lax.broadcasted_iota(jnp.int32, (16, ROWS), 0), 8)
    row_r = lax.broadcasted_iota(jnp.int32, (16, ROWS), 1)
    for p in range(3):
        first = jnp.where(row_r < WAVES - folds[p], 1.0, 0.0)
        keep = jnp.where(row_r < NC - folds[p], 1.0, 0.0)
        m0s[p] = jnp.where(rho < 6, first, keep)
        m1s[p] = jnp.where(rho < 6, 1.0 - first, 0.0)
    pr = lax.broadcasted_iota(jnp.int32, (128, 128), 0)
    pc = lax.broadcasted_iota(jnp.int32, (128, 128), 1)
    perm[...] = jnp.where(pc == lax.rem(pr, NZ) * ND + pr // NZ, 1.0, 0.0).astype(BF16)
    permt[...] = jnp.where(pr == lax.rem(pc, NZ) * ND + pc // NZ, 1.0, 0.0).astype(BF16)
    stageb[:, pl.ds(24, 8), :] = jnp.zeros((ND, 8, 128), F32)
    loads[0].wait()

    def inverse(p):
        arrive(NT, e1[p])
        x = gat[p].reshape(64, ROWS)
        k0 = jnp.concatenate([m0s[p].astype(BF16)] * 4, 0)
        k1 = jnp.concatenate([m1s[p].astype(BF16)] * 4, 0)
        low = pl.ds(0, ROWS - 1)
        both = jnp.concatenate([(x * k0)[:, : ROWS - 1], (x * k1)[:, : ROWS - 1]], 0)
        f = dot(both, leg[p, low, :])
        last = (x * k1)[:, ROWS - 1 :].astype(F32) * leg[p, pl.ds(ROWS - 1, 1), :].astype(F32)
        f = jnp.concatenate([f[:64], f[64:] + last], 0)
        return f.astype(BF16).T.reshape(NZ, 48, 128)

    f = inverse(2)
    for j in range(3):
        o = dot(perm[...], f[:, j * 16 : j * 16 + 16].reshape(128, 128))
        stageb[:, pl.ds(j * 8, 8), :] = o.reshape(ND, 8, 128)
    s1b[...] = stageb[...].astype(BF16)
    e2bd = lambda k: d_copy(k, s1b, r1b, 0)
    start(ND, e2bd)
    r1b[d] = s1b[d]
    e2az = [lambda k, p=p: z_copy(k, s1a.at[p], r1a.at[p], p * 6) for p in range(2)]
    for p in range(2):
        s1a[p] = inverse(p)
        start(NZ, e2az[p])
        r1a[p, z] = s1a[p, z]

    sr = lax.broadcasted_iota(jnp.int32, (NC, NC), 0)
    sc = lax.broadcasted_iota(jnp.int32, (NC, NC), 1)
    slot_of = (lax.rem(sc, NZ) * ND + lax.rem(sc, 128) // NZ) * 3 + sc // 128
    to_order = jnp.where(sr == slot_of, 1.0, 0.0)
    fold = dot(jnp.broadcast_to(fold_v[...].reshape(1, NC).astype(F32), (8, NC)), to_order, HIGHEST)[:1]
    fold = (fold + 0.5).astype(jnp.int32)
    half_fold, odd = fold // 2, lax.rem(fold, 2)
    rows_n = lax.broadcasted_iota(jnp.int32, (2 * NC, NC), 0)
    onehot[:, pl.ds(0, NC)] = jnp.where(rows_n == half_fold + NC * odd, 1.0, 0.0).astype(BF16)
    onehot[:, pl.ds(NC, NC)] = jnp.where(rows_n == 192 + half_fold + NC * (1 - odd), 1.0, 0.0).astype(BF16)
    ordered[...] = jnp.where(sr == fold, 1.0, 0.0).T.astype(BF16)

    for p in range(2):
        arrive(NZ, e2az[p])
        for j in range(3):
            o = dot(perm[...], r1a[p, :, pl.ds(j * 16, 16), :].reshape(128, 128))
            stage[:, pl.ds(j * 16 + p * 8, 8), :] = o.reshape(ND, 8, 128)
    s2a[...] = stage[...].astype(BF16)
    e2ad = lambda k: d_copy(k, s2a, r2a, 1)
    start(ND, e2ad)
    r2a[d] = s2a[d]
    arrive(ND, e2bd)
    stageb[...] = r1b[...].astype(F32)
    for j in range(3):
        x = stageb[:, pl.ds(j * 8, 8), :].reshape(128, 128).astype(BF16)
        s2b[:, pl.ds(j * 16, 16), :] = dot(permt[...], x).astype(BF16).reshape(NZ, 16, 128)
    e2bz = lambda k: z_copy(k, s2b, r2b, 1)
    start(NZ, e2bz)
    r2b[z] = s2b[z]

    for lev in range(NT):
        for n in range(4):
            coefx[pl.ds(lev * 8 + n * 2, 2), :] = coef[pl.ds(lev * 2, 2), :]
    sel_r = lax.broadcasted_iota(jnp.int32, (256, 128), 0)
    sel_c = lax.broadcasted_iota(jnp.int32, (256, 128), 1)
    even = jnp.where(sel_r == 2 * sel_c, 1.0, 0.0)
    chunks = jnp.concatenate([coef[:, pl.ds(n * 256, 256)] for n in range(10)], 0)
    picked = dot(chunks, even, HIGHEST)
    ccoef[...] = jnp.concatenate([picked[n * 8 : n * 8 + 8] for n in range(10)], 1)
    weights = [gauss_s[z * 48 + j * 16 + d] * FACTOR for j in range(3)]
    loads[1].wait()
    loads[2].wait()
    arrive(NZ, e2bz)
    arrive(ND, e2ad)

    stage[...] = r2a[...].astype(F32)
    turned = []
    for j in range(3):
        by_p = [stage[:, pl.ds(j * 16 + p * 8, 8), :].reshape(128, 128) for p in range(2)]
        by_p.append(dot(perm[...], r2b[:, pl.ds(j * 16, 16), :].reshape(128, 128)))
        turned.append(jnp.concatenate(by_p, 0).T)
    rows = []
    for c in range(2):
        for j in range(3):
            members = []
            for i in range(2):
                at = [i * 64 + lev * 16 + c * 8 for lev in range(NT)]
                members.append(jnp.concatenate([turned[j][r : r + 8] for r in at], 0))
            rows.append(jnp.concatenate(members, 1))
            for lev in range(NT):
                r = lev * 16 + c * 8 + 6
                xold[pl.ds(j * 8 + lev * 2, 2), pl.ds(c * NC, NC)] = turned[j][r : r + 2]
    natural = dot_nt(jnp.concatenate(rows, 0).astype(BF16), onehot[...]).astype(BF16)

    def grid(x_even, x_odd, tab, c_low, c_high):
        e = dot(x_even, tab[0])
        o = dot(x_odd, tab[1])
        low, high = e + o, e - o
        prod = jnp.concatenate([c_low * low * low, c_high * high * high], 0).astype(BF16)
        n = low.shape[0]
        back_e = dot_nt(prod, tab[0])
        back_o = dot_nt(prod, tab[1])
        return back_e[:n] + back_e[n:], back_o[:n] - back_o[n:]

    x_even = jnp.concatenate([natural[:96, :NC], natural[96:, :NC]], 1)
    x_odd = jnp.concatenate([natural[:96, NC:], natural[96:, NC:]], 1)
    fe, fo = grid(
        x_even, x_odd, tf,
        jnp.concatenate([coefx[:, pl.ds(0, HALF)]] * 3, 0), jnp.concatenate([coefx[:, pl.ds(HALF, HALF)]] * 3, 0),
    )
    row = lax.broadcasted_iota(jnp.int32, (96, 1), 0)
    wt = jnp.where(row < 32, weights[0], jnp.where(row < 64, weights[1], weights[2]))
    wt = jnp.where(lax.rem(row, 8) < 6, wt, 0.0)
    be = (fe * wt).astype(BF16)
    bo = (fo * wt).astype(BF16)
    y = [jnp.concatenate([be[:, c * NC : c * NC + NC], bo[:, c * NC : c * NC + NC]], 1) for c in range(2)]
    slot = dot(jnp.concatenate(y, 0), onehot[...])
    for j in range(3):
        pieces = []
        for i in range(2):
            for lev in range(NT):
                for c in range(2):
                    r = c * 96 + j * 32 + lev * 8
                    pieces.append(slot[r : r + 8, i * NC : i * NC + NC])
        back = jnp.concatenate(pieces, 0).T
        for p in range(2):
            stage[:, pl.ds(j * 16 + p * 8, 8), :] = back[p * 128 : p * 128 + 128].reshape(ND, 8, 128)
        o = dot(permt[...], back[256:].astype(BF16))
        s3b[:, pl.ds(j * 16, 16), :] = o.astype(BF16).reshape(NZ, 16, 128)
    s3a[...] = stage[...].astype(BF16)
    e3ad = lambda k: d_copy(k, s3a, r3a, 2)
    e3bz = lambda k: z_copy(k, s3b, r3b, 2)
    start(ND, e3ad)
    start(NZ, e3bz)
    r3a[d] = s3a[d]
    r3b[z] = s3b[z]

    row = lax.broadcasted_iota(jnp.int32, (32, 1), 0)
    wt_c = jnp.where(row < 8, weights[0], jnp.where(row < 16, weights[1], weights[2]))

    def coarse_grid(x):
        g = dot(x, tslot[...])
        prod = (jnp.concatenate([ccoef[...]] * 4, 0) * g * g).astype(BF16)
        return dot_nt(prod, tslot[...]) * wt_c

    for c in range(2):
        tslot[pl.ds(c * NC, NC), :] = dot(ordered[...], tc[c]).astype(BF16)
    xold[pl.ds(24, 8), :] = jnp.zeros((8, 2 * NC), F32)
    oldback[...] = coarse_grid(xold[...].astype(BF16))

    arrive(ND, e3ad)
    stage[...] = r3a[...].astype(F32)
    e3az = [lambda k, p=p: z_copy(k, s4a.at[p], r4a.at[p], 3 + p * 4) for p in range(2)]
    for p in range(2):
        for j in range(3):
            x = stage[:, pl.ds(j * 16 + p * 8, 8), :].reshape(128, 128).astype(BF16)
            s4a[p, :, pl.ds(j * 16, 16), :] = dot(permt[...], x).astype(BF16).reshape(NZ, 16, 128)
        start(NZ, e3az[p])
        r4a[p, z] = s4a[p, z]
    arrive(NZ, e3bz)
    for j in range(3):
        o = dot(perm[...], r3b[:, pl.ds(j * 16, 16), :].reshape(128, 128))
        stageb[:, pl.ds(j * 8, 8), :] = o.reshape(ND, 8, 128)
    s4b[...] = stageb[...].astype(BF16)
    e3bd = lambda k: d_copy(k, s4b, r4b, 3)
    start(ND, e3bd)
    r4b[d] = s4b[d]

    wto[...] = dot(dot(to_rows[...], mto[...], HIGHEST), to_cols[...], HIGHEST) * to_mask[...]
    mixed = dot(dot(mix_rows[...], mfrom[...], HIGHEST), mix_cols[...], HIGHEST) * mix_mask[...]
    wmix[pl.ds(0, 16), :] = mixed[:16, :16]
    wplace[...] = mixed[16:]
    mixed = dot(dot(mix_rows[pl.ds(0, 16), :], mto[...], HIGHEST), mix_cols[...], HIGHEST) * mix_mask[pl.ds(0, 16), :]
    wmix[pl.ds(16, 16), :] = mixed[:, :16]
    keeps = [m0s[p, pl.ds(6, 1), pl.ds(0, NC)] for p in range(3)]
    for p in range(3):
        x = gat[p, :, :, pl.ds(0, NC)].reshape(64, NC).astype(F32)
        states[p] = dot(wto[pl.ds(0, 48), :], x, HIGHEST) * keeps[p]

    def forward(p, x):
        o = dot_nt(x.T, leg[p])
        k0 = jnp.concatenate([m0s[p]] * 4, 0)
        k1 = jnp.concatenate([m1s[p]] * 4, 0)
        part = o[:64] * k0 + o[64:] * k1
        parts[p] = part
        mixed = dot(wto[pl.ds(48, 32), :], part[:, :NC] * keeps[p], HIGHEST).astype(BF16)
        vmid[t, p] = mixed[:16]
        vend[t, p] = mixed[16:]

    arrive(ND, e3bd)
    stageb[...] = r4b[...].astype(F32)
    pieces = []
    for j in range(3):
        x = stageb[:, pl.ds(j * 8, 8), :].reshape(128, 128).astype(BF16)
        pieces.append(dot(permt[...], x).astype(BF16).reshape(NZ, 16, 128))
    forward(2, jnp.concatenate(pieces, 1).reshape(NC, 128))
    for p in range(2):
        arrive(NZ, e3az[p])
        forward(p, r4a[p].reshape(NC, 128))
    e4 = lambda k: gather_copy(k, vmid, 1)
    start(NT, e4)
    for p in range(3):
        s5[:, p] = parts[p].astype(BF16).reshape(NT, 16, ROWS)

    mode = lax.rem(lax.broadcasted_iota(jnp.int32, (16, NC), 0), 8)
    rate = jnp.zeros((16, NC), F32)
    for q in range(8):
        rate = jnp.where(mode == q, rates_s[q], rate)
    col = lax.broadcasted_iota(jnp.int32, (16, NC), 1)
    known = []
    for p in range(3):
        degree = (col + folds[p]).astype(F32)
        stiff = rate * (degree * (degree + 1.0) / (NC * (NC + 1.0)))
        old = [states[p, pl.ds(b * 16, 16), :] for b in range(3)]
        int_mid = stiff * (QUAD[0][0] * old[0] + QUAD[0][1] * old[1] + QUAD[0][2] * old[2])
        int_end = stiff * (QUAD[1][0] * old[0] + QUAD[1][1] * old[1] + QUAD[1][2] * old[2])
        inv = 1.0 / (1.0 + 0.5 * stiff)
        known.append((inv, old[0] + 0.5 * stiff * old[1] - int_mid, 0.5 * stiff * old[2] - int_end, old[1], old[2]))
    arrive(NT, e4)
    mids = []
    for p in range(3):
        tend = (vmid[0, p].astype(F32) + vmid[1, p].astype(F32)) + (vmid[2, p].astype(F32) + vmid[3, p].astype(F32))
        mids.append((known[p][1] + tend) * known[p][0])
    levels = dot(wmix[pl.ds(0, 16), :], jnp.concatenate(mids, 1), HIGHEST)
    fourier = []
    for p in range(3):
        x = (levels[:, p * NC : p * NC + NC] * keeps[p]).astype(BF16)
        fourier.append(dot(x, leg[p, pl.ds(0, NC), :]))
    rest = jnp.zeros((80, NC), F32)
    f = jnp.concatenate(fourier + [rest], 0).T.reshape(NZ, 48, 128)
    s6[:, pl.ds(0, 16), :] = (f[:, :16] + pltpu.roll(f[:, 16:32], 64, 2)).astype(BF16)
    s6[:, pl.ds(16, 16), :] = f[:, 32:].astype(BF16)
    e5a = lambda k: z_copy(k, s6, r6, 4)
    start(NZ, e5a)
    r6[z] = s6[z]
    e4e = lambda k: gather_copy(k, vend, 4)
    start(NT, e4e)
    e4t = lambda k: scatter_copy(k, s5, r5, 2)
    start(NT, e4t)
    r5[t] = s5[t]
    place = wplace[...]
    lift[0] = dot(place, jnp.concatenate([mids[p] - known[p][3] for p in range(3)], 0), HIGHEST).reshape(NT, 16, NC)
    arrive(NZ, e5a)
    for h in range(2):
        o = dot(perm[...], r6[:, pl.ds(h * 16, 16), :].reshape(128, 128))
        cstage[:, pl.ds(h * 8, 8), :] = o.reshape(ND, 8, 128)
    s7[...] = cstage[...].astype(BF16)
    e5b = lambda k: d_copy(k, s7, r7, 4)
    start(ND, e5b)
    r7[d] = s7[d]
    arrive(NT, e4e)
    ends = []
    for p in range(3):
        inv, known_mid, known_end, old_1, old_2 = known[p]
        tend = (vend[0, p].astype(F32) + vend[1, p].astype(F32)) + (vend[2, p].astype(F32) + vend[3, p].astype(F32))
        ends.append((mids[p] + known_end + tend) * inv - old_2)
    lift[1] = dot(place, jnp.concatenate(ends, 0), HIGHEST).reshape(NT, 16, NC)
    arrive(ND, e5b)

    cstage[...] = r7[...].astype(F32)
    turned = [cstage[:, pl.ds(h * 8, 8), :].reshape(128, 128).T for h in range(2)]
    at_j = ((0, 0), (0, 64), (1, 0))
    rows = []
    for h, first_row in at_j:
        at = [first_row + p * 16 + c * 8 for c in range(2) for p in range(3)]
        rows.append(jnp.concatenate([turned[h][r : r + 8] for r in at], 1))
    rows.append(jnp.zeros((8, 2 * NC), F32))
    fresh = coarse_grid(jnp.concatenate(rows, 0).astype(BF16))
    slot = (fresh - oldback[...]).astype(BF16).astype(F32)
    by_j = []
    for j in range(3):
        by_j.append([slot[j * 8 : j * 8 + 8, c * NC + p * 128 : c * NC + p * 128 + 128] for p in range(3) for c in range(2)])
    gap = [jnp.zeros((16, 128), F32)]
    for h, group in enumerate((by_j[0] + gap + by_j[1] + gap, by_j[2] + gap * 5)):
        cstage[:, pl.ds(h * 8, 8), :] = jnp.concatenate(group, 0).T.reshape(ND, 8, 128)
    s8[...] = cstage[...].astype(BF16)
    e6a = lambda k: d_copy(k, s8, r8, 5)
    start(ND, e6a)
    r8[d] = s8[d]
    for a in range(2):
        for b in range(2):
            for p in range(3):
                corr[a, b, p] = fs[a, b + 1, p]
    mid_own = lift[0, t]
    for p in range(3):
        for a in range(2):
            r = p * 4 + a * 2
            corr[a, 0, p, :, pl.ds(0, NC)] = fs[a, 1, p, :, pl.ds(0, NC)] + mid_own[r : r + 2]
    for make in (*e1, e4, e4e, e4t):
        sent(NT, make)
    for make in (*e2az, e2bz, e3bz, *e3az, e5a):
        sent(NZ, make)
    for make in (e2bd, e2ad, e3ad, e3bd, e5b):
        sent(ND, make)
    arrive(NT, e4t)
    for p in range(3):
        total = (r5[0, p].astype(F32) + r5[1, p].astype(F32)) + (r5[2, p].astype(F32) + r5[3, p].astype(F32))
        for c in range(2):
            for a in range(2):
                for b in range(3):
                    r = c * 8 + b * 2 + a
                    tend_out[a, b, p, pl.ds(c, 1), :] = total[r : r + 1]
    arrive(ND, e6a)
    cstage[...] = r8[...].astype(F32)
    for h in range(2):
        x = cstage[:, pl.ds(h * 8, 8), :].reshape(128, 128).astype(BF16)
        s9[:, pl.ds(h * 16, 16), :] = dot(permt[...], x).astype(BF16).reshape(NZ, 16, 128)
    e6b = lambda k: z_copy(k, s9, r9, 5)
    start(NZ, e6b)
    r9[z] = s9[z]
    sent(ND, e6a)
    arrive(NZ, e6b)
    x = r9[...].astype(F32)
    back = jnp.concatenate([x[:, :16], pltpu.roll(x[:, :16], 64, 2), x[:, 16:]], 1).reshape(NC, 128).T
    partial = []
    for p in range(3):
        partial.append(dot_nt(back[p * 16 : p * 16 + 16].astype(BF16), leg[p, pl.ds(0, NC), :]) * keeps[p])
    diff = dot(wmix[pl.ds(16, 16), :], jnp.concatenate(partial, 1), HIGHEST)
    scaled = [diff[:, p * NC : p * NC + NC] * (0.5 * known[p][0]) for p in range(3)]
    total = dot(place, jnp.concatenate(scaled, 0), HIGHEST)
    s10[...] = total.astype(BF16).reshape(NT, 16, NC)
    e7 = lambda k: scatter_copy(k, s10, r10, 3)
    start(NT, e7)
    r10[t] = s10[t]
    arrive(NT, e7)
    end_own = lift[1, t] + ((r10[0].astype(F32) + r10[1].astype(F32)) + (r10[2].astype(F32) + r10[3].astype(F32)))
    for p in range(3):
        for a in range(2):
            r = p * 4 + a * 2
            corr[a, 1, p, :, pl.ds(0, NC)] = fs[a, 2, p, :, pl.ds(0, NC)] + end_own[r : r + 2]
    sent(NT, e7)
    sent(NZ, e6b)


def per_device(fine_state, fold_pairs, legendre, gauss_weights, grid_coef, modes_from, modes_to, mode_rates):
    fine_table, coarse_table = tables()
    sels = selectors()
    fs = jnp.transpose(fine_state, (0, 1, 3, 2, 4))
    leg = jnp.transpose(legendre, (0, 2, 1))
    vm = pl.BlockSpec(memory_space=pltpu.VMEM)
    hbm = pl.BlockSpec(memory_space=pltpu.HBM)
    v, sm = pltpu.VMEM, pltpu.SMEM
    dma = pltpu.SemaphoreType.DMA
    scratch = [
        v((2, 3, 3, 2, ROWS), F32), sm((NC,), jnp.int32), v((NC,), jnp.int32), sm((NC,), F32), sm((LEV,), F32),
        v((LEV, NLON), F32), v((8, 8), F32), v((8, 8), F32), v((80, 8), F32), v((80, 64), F32), v((8, 64), F32),
        v((80, 8), F32), v((80, 48), F32), v((8, 48), F32),
        v((3, ROWS, NC), BF16), v((2, 768, HALF), BF16), v((2, NC, CLON), BF16),
        v((3, 16, ROWS), F32), v((3, NT, 16, ROWS), BF16), v((3, 16, ROWS), F32), v((3, 16, ROWS), F32),
        v((768, 768), BF16), v((NC, NC), BF16), v((768, CLON), BF16), v((128, 128), BF16), v((128, 128), BF16),
        v((32, NLON), F32), v((LEV, CLON), F32), v((80, 64), F32), v((32, 16), F32), v((64, 48), F32),
        v((3, 48, NC), F32), v((3, 64, ROWS), F32), v((32, 768), F32), v((2, NT, 16, NC), F32), v((32, 768), F32),
        v((ND, 48, 128), F32), v((ND, 32, 128), F32), v((ND, 16, 128), F32),
    ]
    z_two, z_one = v((2, NZ, 48, 128), BF16), v((NZ, 48, 128), BF16)
    d_two, d_one = v((ND, 48, 128), BF16), v((ND, 32, 128), BF16)
    scratch += [z_two, z_two, d_two, d_two, d_one, d_one, z_one, z_one]
    scratch += [d_two, d_two, z_two, z_two, z_one, z_one, d_one, d_one]
    scratch += [v((NT, 3, 16, NC), BF16), v((NT, 3, 16, NC), BF16), v((NT, 3, 16, ROWS), BF16), v((NT, 3, 16, ROWS), BF16)]
    z_coarse, d_coarse, lev_coarse = v((NZ, 32, 128), BF16), v((ND, 16, 128), BF16), v((NT, 16, NC), BF16)
    scratch += [z_coarse] * 2 + [d_coarse] * 4 + [z_coarse] * 2 + [lev_coarse] * 2
    scratch += [
        dma((17,)), dma((8, NZ)), dma((8, NZ)), dma((6, ND)), dma((6, ND)), dma((8, NT)), dma((8, NT)),
    ]
    operands = [
        fs, leg, fold_pairs, gauss_weights, mode_rates, grid_coef, modes_to, modes_from,
        jnp.asarray(fine_table), jnp.asarray(coarse_table), *[jnp.asarray(s) for s in sels],
    ]
    corr, tend = pl.pallas_call(
        kernel,
        out_shape=(
            jax.ShapeDtypeStruct((2, 2, 3, 2, ROWS), F32),
            jax.ShapeDtypeStruct((2, 3, 3, 2, ROWS), F32),
        ),
        in_specs=[hbm] * 16,
        out_specs=(vm, vm),
        scratch_shapes=scratch,
        compiler_params=pltpu.CompilerParams(
            collective_id=0, has_side_effects=True, vmem_limit_bytes=48 * 1024 * 1024
        ),
        name="sweep",
    )(*[pltpu.with_memory_space_constraint(x, pltpu.HBM) for x in operands])
    return (jnp.transpose(corr, (0, 1, 3, 2, 4)), jnp.transpose(tend, (0, 1, 3, 2, 4)))


def solution(mesh):
    placed = (
        P("lev", None, None, "wave", None),
        P(),
        P("wave", "lev", None),
        P("lev"),
        P(),
        P(),
        P(),
        P(),
    )
    return jax.shard_map(
        per_device,
        mesh=mesh,
        in_specs=placed,
        out_specs=(P("lev", None, None, "wave", None), P("lev", None, None, "wave", None)),
        check_vma=False,
    )
```

```python
import functools
import math

import jax
import jax.numpy as jnp
import ml_dtypes
import numpy as np
from jax import lax
from jax.experimental import pallas as pl
from jax.experimental.pallas import tpu as pltpu
from jax.sharding import PartitionSpec as P

F32 = jnp.float32
BF16 = jnp.bfloat16
HIGHEST = lax.Precision.HIGHEST
MESH = pl.DeviceIdType.MESH

NLON, LEV, WAVES, ROWS, NC = 2560, 8, 768, 769, 384
HALF, CLON = NLON // 2, NLON // 2
NZ, ND, NT = 8, 16, 4
FACTOR = 2.0 * WAVES / NLON
QUAD = ((5.0 / 24.0, 1.0 / 3.0, -1.0 / 24.0), (-1.0 / 24.0, 1.0 / 3.0, 5.0 / 24.0))


def table(waves, points, amplitude, count):
    turns = np.outer(waves, np.arange(count)) % points
    angles = turns * (2.0 * math.pi / points)
    return np.concatenate([np.cos(angles), -np.sin(angles)], 0).reshape(2, len(waves), count) * amplitude


def tables():
    t = np.arange(192)
    fine = []
    for parity in (0, 1):
        low = 2 * t + parity
        high = (WAVES - 2 - 2 * t) + parity
        fine.append(table(np.concatenate([low, high]), NLON, WAVES**-0.5, HALF).reshape(768, HALF))
    coarse = table(np.arange(NC), NLON // 2, NC**-0.5, NLON // 2)
    as_bf16 = lambda values: values.astype(np.float32).astype(ml_dtypes.bfloat16)
    return as_bf16(np.stack(fine)), as_bf16(coarse)


def selectors():
    to_rows = np.zeros((80, 8), np.float32)
    to_mask = np.zeros((80, 64), np.float32)
    to_cols = np.zeros((8, 64), np.float32)
    for lev in range(4):
        for c in range(2):
            for rho in range(8):
                col = lev * 16 + c * 8 + rho
                to_cols[lev * 2 + rho % 2, col] = 1
                node = rho // 2
                for q in range(8):
                    if node < 3:
                        to_mask[node * 16 + c * 8 + q, col] = 1
                        to_mask[48 + c * 8 + q, col] = QUAD[0][node]
                        to_mask[64 + c * 8 + q, col] = QUAD[1][node]
    for row in range(80):
        to_rows[row, row % 8] = 1
    mix_cols = np.zeros((8, 48), np.float32)
    mix_rows = np.zeros((80, 8), np.float32)
    mix_mask = np.zeros((80, 48), np.float32)
    for c in range(2):
        for q in range(8):
            for p in range(3):
                mix_cols[q, p * 16 + c * 8 + q] = 1
            for a in range(8):
                mix_rows[c * 8 + a, a] = 1
                mix_mask[c * 8 + a, c * 8 + q] = 1
                for p in range(3):
                    row = 16 + (a // 2) * 16 + p * 4 + (a % 2) * 2 + c
                    mix_rows[row, a] = 1
                    mix_mask[row, p * 16 + c * 8 + q] = 1
    return to_rows, to_mask, to_cols, mix_rows, mix_mask, mix_cols


def dot(a, b, precision=None):
    return lax.dot_general(a, b, (((1,), (0,)), ((), ())), precision=precision, preferred_element_type=F32)


def dot_nt(a, b):
    return lax.dot_general(a, b, (((1,), (1,)), ((), ())), preferred_element_type=F32)


def kernel(
    fs_hbm, leg_hbm, fold_hbm, gauss_hbm, rates_hbm, coef_hbm, mto_hbm, mfrom_hbm, tf_hbm, tc_hbm,
    to_rows_hbm, to_mask_hbm, to_cols_hbm, mix_rows_hbm, mix_mask_hbm, mix_cols_hbm,
    corr, tend_out,
    fs, fold_s, fold_v, gauss_s, rates_s, coef, mto, mfrom,
    to_rows, to_mask, to_cols, mix_rows, mix_mask, mix_cols,
    leg, tf, tc, xf, gat, m0s, m1s, onehot, ordered, tslot, perm, permt, coefx, ccoef, wto, wmix, wplace, states, parts, oldback, lift, xold,
    stage, stageb, cstage,
    s1a, r1a, s2a, r2a, s1b, r1b, s2b, r2b, s3a, r3a, s4a, r4a, s3b, r3b, s4b, r4b,
    vmid, vend, s5, r5, s6, r6, s7, r7, s8, r8, s9, r9, s10, r10,
    load_sem, z_send, z_recv, d_send, d_recv, lev_send, lev_recv,
):
    w = lax.axis_index("wave")
    t = lax.axis_index("lev")
    z, d = w // ND, w % ND

    pairs = (
        (leg_hbm, leg), (tf_hbm, tf), (tc_hbm, tc), (fs_hbm, fs), (fold_hbm, fold_s), (fold_hbm, fold_v),
        (gauss_hbm, gauss_s), (rates_hbm, rates_s), (coef_hbm, coef), (mto_hbm, mto), (mfrom_hbm, mfrom),
        (to_rows_hbm, to_rows), (to_mask_hbm, to_mask), (to_cols_hbm, to_cols), (mix_rows_hbm, mix_rows),
        (mix_mask_hbm, mix_mask), (mix_cols_hbm, mix_cols),
    )
    loads = [pltpu.make_async_copy(src, dst, load_sem.at[n]) for n, (src, dst) in enumerate(pairs)]
    loads[3].start()

    barrier = pltpu.get_barrier_semaphore()

    def lev_dev(k):
        return {"lev": lax.rem(t + k, NT)}

    def z_dev(k):
        return {"wave": lax.rem(z + k, NZ) * ND + d}

    def d_dev(k):
        return {"wave": z * ND + lax.rem(d + k, ND)}

    groups = ((NT, lev_dev), (NZ, z_dev), (ND, d_dev))
    for count, dev in groups:
        @pl.loop(1, count)
        def _(k):
            pl.semaphore_signal(barrier, inc=1, device_id=dev(k), device_id_type=MESH)

    for n in (0, 4, 5) + tuple(range(6, 17)) + (1, 2):
        loads[n].start()

    def lev_copy(k, src, dst, row):
        return pltpu.make_async_remote_copy(
            src_ref=src, dst_ref=dst, send_sem=lev_send.at[row, k], recv_sem=lev_recv.at[row, k],
            device_id=lev_dev(k), device_id_type=MESH)

    def z_copy(k, src, dst, row):
        return pltpu.make_async_remote_copy(
            src_ref=src.at[lax.rem(z + k, NZ)], dst_ref=dst.at[z], send_sem=z_send.at[row, k],
            recv_sem=z_recv.at[row, k], device_id=z_dev(k), device_id_type=MESH)

    def d_copy(k, src, dst, row):
        return pltpu.make_async_remote_copy(
            src_ref=src.at[lax.rem(d + k, ND)], dst_ref=dst.at[d], send_sem=d_send.at[row, k],
            recv_sem=d_recv.at[row, k], device_id=d_dev(k), device_id_type=MESH)

    def gather_copy(k, buf, row):
        return lev_copy(k, buf.at[t], buf.at[t], row)

    def scatter_copy(k, src, dst, row):
        return lev_copy(k, src.at[lax.rem(t + k, NT)], dst.at[t], row)

    def start(count, make):
        @pl.loop(1, count)
        def _(k):
            make(k).start()

    def arrive(count, make):
        @pl.loop(1, count)
        def _(k):
            make(k).wait_recv()

    def sent(count, make):
        @pl.loop(1, count)
        def _(k):
            make(k).wait_send()

    loads[3].wait()
    for p in range(3):
        for c in range(2):
            for a in range(2):
                for b in range(3):
                    xf[p, pl.ds(c * 8 + b * 2 + a, 1), :] = fs[a, b, p, pl.ds(c, 1), :]
                xf[p, pl.ds(c * 8 + 6 + a, 1), :] = fs[a, 1, p, pl.ds(c, 1), :]
    for p in range(3):
        gat[p, t] = xf[p].astype(BF16)
    pl.semaphore_wait(barrier, (NT - 1) + (NZ - 1) + (ND - 1))
    e1 = [lambda k, p=p: gather_copy(k, gat.at[p], 5 + p) for p in range(3)]
    for p in (2, 0, 1):
        start(NT, e1[p])

    for n in range(4, 17):
        loads[n].wait()
    folds = [fold_s[w * 3 + p] for p in range(3)]
    rho = lax.rem(lax.broadcasted_iota(jnp.int32, (16, ROWS), 0), 8)
    row_r = lax.broadcasted_iota(jnp.int32, (16, ROWS), 1)
    for p in range(3):
        first = jnp.where(row_r < WAVES - folds[p], 1.0, 0.0)
        keep = jnp.where(row_r < NC - folds[p], 1.0, 0.0)
        m0s[p] = jnp.where(rho < 6, first, keep)
        m1s[p] = jnp.where(rho < 6, 1.0 - first, 0.0)
    pr = lax.broadcasted_iota(jnp.int32, (128, 128), 0)
    pc = lax.broadcasted_iota(jnp.int32, (128, 128), 1)
    perm[...] = jnp.where(pc == lax.rem(pr, NZ) * ND + pr // NZ, 1.0, 0.0).astype(BF16)
    permt[...] = jnp.where(pr == lax.rem(pc, NZ) * ND + pc // NZ, 1.0, 0.0).astype(BF16)
    stageb[:, pl.ds(24, 8), :] = jnp.zeros((ND, 8, 128), F32)
    loads[0].wait()

    def inverse(p):
        arrive(NT, e1[p])
        x = gat[p].reshape(64, ROWS)
        k0 = jnp.concatenate([m0s[p].astype(BF16)] * 4, 0)
        k1 = jnp.concatenate([m1s[p].astype(BF16)] * 4, 0)
        low = pl.ds(0, ROWS - 1)
        both = jnp.concatenate([(x * k0)[:, : ROWS - 1], (x * k1)[:, : ROWS - 1]], 0)
        f = dot(both, leg[p, low, :])
        last = (x * k1)[:, ROWS - 1 :].astype(F32) * leg[p, pl.ds(ROWS - 1, 1), :].astype(F32)
        f = jnp.concatenate([f[:64], f[64:] + last], 0)
        return f.astype(BF16).T.reshape(NZ, 48, 128)

    f = inverse(2)
    for j in range(3):
        o = dot(perm[...], f[:, j * 16 : j * 16 + 16].reshape(128, 128))
        stageb[:, pl.ds(j * 8, 8), :] = o.reshape(ND, 8, 128)
    s1b[...] = stageb[...].astype(BF16)
    e2bd = lambda k: d_copy(k, s1b, r1b, 0)
    start(ND, e2bd)
    r1b[d] = s1b[d]
    e2az = [lambda k, p=p: z_copy(k, s1a.at[p], r1a.at[p], p * 6) for p in range(2)]
    for p in range(2):
        s1a[p] = inverse(p)
        start(NZ, e2az[p])
        r1a[p, z] = s1a[p, z]

    sr = lax.broadcasted_iota(jnp.int32, (NC, NC), 0)
    sc = lax.broadcasted_iota(jnp.int32, (NC, NC), 1)
    slot_of = (lax.rem(sc, NZ) * ND + lax.rem(sc, 128) // NZ) * 3 + sc // 128
    to_order = jnp.where(sr == slot_of, 1.0, 0.0)
    fold = dot(jnp.broadcast_to(fold_v[...].reshape(1, NC).astype(F32), (8, NC)), to_order, HIGHEST)[:1]
    fold = (fold + 0.5).astype(jnp.int32)
    half_fold, odd = fold // 2, lax.rem(fold, 2)
    rows_n = lax.broadcasted_iota(jnp.int32, (2 * NC, NC), 0)
    onehot[:, pl.ds(0, NC)] = jnp.where(rows_n == half_fold + NC * odd, 1.0, 0.0).astype(BF16)
    onehot[:, pl.ds(NC, NC)] = jnp.where(rows_n == 192 + half_fold + NC * (1 - odd), 1.0, 0.0).astype(BF16)
    ordered[...] = jnp.where(sr == fold, 1.0, 0.0).T.astype(BF16)

    for p in range(2):
        arrive(NZ, e2az[p])
        for j in range(3):
            o = dot(perm[...], r1a[p, :, pl.ds(j * 16, 16), :].reshape(128, 128))
            stage[:, pl.ds(j * 16 + p * 8, 8), :] = o.reshape(ND, 8, 128)
    s2a[...] = stage[...].astype(BF16)
    e2ad = lambda k: d_copy(k, s2a, r2a, 1)
    start(ND, e2ad)
    r2a[d] = s2a[d]
    arrive(ND, e2bd)
    stageb[...] = r1b[...].astype(F32)
    for j in range(3):
        x = stageb[:, pl.ds(j * 8, 8), :].reshape(128, 128).astype(BF16)
        s2b[:, pl.ds(j * 16, 16), :] = dot(permt[...], x).astype(BF16).reshape(NZ, 16, 128)
    e2bz = lambda k: z_copy(k, s2b, r2b, 1)
    start(NZ, e2bz)
    r2b[z] = s2b[z]

    for lev in range(NT):
        for n in range(4):
            coefx[pl.ds(lev * 8 + n * 2, 2), :] = coef[pl.ds(lev * 2, 2), :]
    sel_r = lax.broadcasted_iota(jnp.int32, (256, 128), 0)
    sel_c = lax.broadcasted_iota(jnp.int32, (256, 128), 1)
    even = jnp.where(sel_r == 2 * sel_c, 1.0, 0.0)
    chunks = jnp.concatenate([coef[:, pl.ds(n * 256, 256)] for n in range(10)], 0)
    picked = dot(chunks, even, HIGHEST)
    ccoef[...] = jnp.concatenate([picked[n * 8 : n * 8 + 8] for n in range(10)], 1)
    weights = [gauss_s[z * 48 + j * 16 + d] * FACTOR for j in range(3)]
    loads[1].wait()
    loads[2].wait()
    for c in range(2):
        tslot[pl.ds(c * NC, NC), :] = dot(ordered[...], tc[c]).astype(BF16)
    arrive(NZ, e2bz)
    arrive(ND, e2ad)

    stage[...] = r2a[...].astype(F32)
    turned = []
    for j in range(3):
        by_p = [stage[:, pl.ds(j * 16 + p * 8, 8), :].reshape(128, 128) for p in range(2)]
        by_p.append(dot(perm[...], r2b[:, pl.ds(j * 16, 16), :].reshape(128, 128)))
        turned.append(jnp.concatenate(by_p, 0).T)
    rows = []
    for c in range(2):
        for j in range(3):
            members = []
            for i in range(2):
                at = [i * 64 + lev * 16 + c * 8 for lev in range(NT)]
                members.append(jnp.concatenate([turned[j][r : r + 8] for r in at], 0))
            rows.append(jnp.concatenate(members, 1))
            for lev in range(NT):
                r = lev * 16 + c * 8 + 6
                xold[pl.ds(j * 8 + lev * 2, 2), pl.ds(c * NC, NC)] = turned[j][r : r + 2]
    natural = dot_nt(jnp.concatenate(rows, 0).astype(BF16), onehot[...]).astype(BF16)

    def grid(x_even, x_odd, tab, c_low, c_high):
        e = dot(x_even, tab[0])
        o = dot(x_odd, tab[1])
        low, high = e + o, e - o
        prod = jnp.concatenate([c_low * low * low, c_high * high * high], 0).astype(BF16)
        n = low.shape[0]
        back_e = dot_nt(prod, tab[0])
        back_o = dot_nt(prod, tab[1])
        return back_e[:n] + back_e[n:], back_o[:n] - back_o[n:]

    x_even = jnp.concatenate([natural[:96, :NC], natural[96:, :NC]], 1)
    x_odd = jnp.concatenate([natural[:96, NC:], natural[96:, NC:]], 1)
    fe, fo = grid(
        x_even, x_odd, tf,
        jnp.concatenate([coefx[:, pl.ds(0, HALF)]] * 3, 0), jnp.concatenate([coefx[:, pl.ds(HALF, HALF)]] * 3, 0),
    )
    row = lax.broadcasted_iota(jnp.int32, (96, 1), 0)
    wt = jnp.where(row < 32, weights[0], jnp.where(row < 64, weights[1], weights[2]))
    wt = jnp.where(lax.rem(row, 8) < 6, wt, 0.0)
    be = (fe * wt).astype(BF16)
    bo = (fo * wt).astype(BF16)
    y = [jnp.concatenate([be[:, c * NC : c * NC + NC], bo[:, c * NC : c * NC + NC]], 1) for c in range(2)]
    slot = dot(jnp.concatenate(y, 0), onehot[...])
    for j in range(3):
        pieces = []
        for i in range(2):
            for lev in range(NT):
                for c in range(2):
                    r = c * 96 + j * 32 + lev * 8
                    pieces.append(slot[r : r + 8, i * NC : i * NC + NC])
        back = jnp.concatenate(pieces, 0).T
        for p in range(2):
            stage[:, pl.ds(j * 16 + p * 8, 8), :] = back[p * 128 : p * 128 + 128].reshape(ND, 8, 128)
        o = dot(permt[...], back[256:].astype(BF16))
        s3b[:, pl.ds(j * 16, 16), :] = o.astype(BF16).reshape(NZ, 16, 128)
    s3a[...] = stage[...].astype(BF16)
    e3ad = lambda k: d_copy(k, s3a, r3a, 2)
    e3bz = lambda k: z_copy(k, s3b, r3b, 2)
    start(ND, e3ad)
    start(NZ, e3bz)
    r3a[d] = s3a[d]
    r3b[z] = s3b[z]

    row = lax.broadcasted_iota(jnp.int32, (32, 1), 0)
    wt_c = jnp.where(row < 8, weights[0], jnp.where(row < 16, weights[1], weights[2]))

    def coarse_grid(x):
        g = dot(x, tslot[...])
        prod = (jnp.concatenate([ccoef[...]] * 4, 0) * g * g).astype(BF16)
        return dot_nt(prod, tslot[...]) * wt_c

    xold[pl.ds(24, 8), :] = jnp.zeros((8, 2 * NC), F32)
    oldback[...] = coarse_grid(xold[...].astype(BF16))

    arrive(ND, e3ad)
    stage[...] = r3a[...].astype(F32)
    e3az = [lambda k, p=p: z_copy(k, s4a.at[p], r4a.at[p], 3 + p * 4) for p in range(2)]
    for p in range(2):
        for j in range(3):
            x = stage[:, pl.ds(j * 16 + p * 8, 8), :].reshape(128, 128).astype(BF16)
            s4a[p, :, pl.ds(j * 16, 16), :] = dot(permt[...], x).astype(BF16).reshape(NZ, 16, 128)
        start(NZ, e3az[p])
        r4a[p, z] = s4a[p, z]
    arrive(NZ, e3bz)
    for j in range(3):
        o = dot(perm[...], r3b[:, pl.ds(j * 16, 16), :].reshape(128, 128))
        stageb[:, pl.ds(j * 8, 8), :] = o.reshape(ND, 8, 128)
    s4b[...] = stageb[...].astype(BF16)
    e3bd = lambda k: d_copy(k, s4b, r4b, 3)
    start(ND, e3bd)
    r4b[d] = s4b[d]

    wto[...] = dot(dot(to_rows[...], mto[...], HIGHEST), to_cols[...], HIGHEST) * to_mask[...]
    mixed = dot(dot(mix_rows[...], mfrom[...], HIGHEST), mix_cols[...], HIGHEST) * mix_mask[...]
    wmix[pl.ds(0, 16), :] = mixed[:16, :16]
    wplace[...] = mixed[16:]
    mixed = dot(dot(mix_rows[pl.ds(0, 16), :], mto[...], HIGHEST), mix_cols[...], HIGHEST) * mix_mask[pl.ds(0, 16), :]
    wmix[pl.ds(16, 16), :] = mixed[:, :16]
    keeps = [m0s[p, pl.ds(6, 1), pl.ds(0, NC)] for p in range(3)]
    for p in range(3):
        x = gat[p, :, :, pl.ds(0, NC)].reshape(64, NC).astype(F32)
        states[p] = dot(wto[pl.ds(0, 48), :], x, HIGHEST) * keeps[p]

    def forward(p, x):
        o = dot_nt(x.T, leg[p])
        k0 = jnp.concatenate([m0s[p]] * 4, 0)
        k1 = jnp.concatenate([m1s[p]] * 4, 0)
        part = o[:64] * k0 + o[64:] * k1
        parts[p] = part
        mixed = dot(wto[pl.ds(48, 32), :], part[:, :NC] * keeps[p], HIGHEST).astype(BF16)
        vmid[t, p] = mixed[:16]
        vend[t, p] = mixed[16:]

    arrive(ND, e3bd)
    stageb[...] = r4b[...].astype(F32)
    pieces = []
    for j in range(3):
        x = stageb[:, pl.ds(j * 8, 8), :].reshape(128, 128).astype(BF16)
        pieces.append(dot(permt[...], x).astype(BF16).reshape(NZ, 16, 128))
    forward(2, jnp.concatenate(pieces, 1).reshape(NC, 128))
    for p in range(2):
        arrive(NZ, e3az[p])
        forward(p, r4a[p].reshape(NC, 128))
    e4 = lambda k: gather_copy(k, vmid, 1)
    start(NT, e4)
    for p in range(3):
        s5[:, p] = parts[p].astype(BF16).reshape(NT, 16, ROWS)

    mode = lax.rem(lax.broadcasted_iota(jnp.int32, (16, NC), 0), 8)
    rate = jnp.zeros((16, NC), F32)
    for q in range(8):
        rate = jnp.where(mode == q, rates_s[q], rate)
    col = lax.broadcasted_iota(jnp.int32, (16, NC), 1)
    known = []
    for p in range(3):
        degree = (col + folds[p]).astype(F32)
        stiff = rate * (degree * (degree + 1.0) / (NC * (NC + 1.0)))
        old = [states[p, pl.ds(b * 16, 16), :] for b in range(3)]
        int_mid = stiff * (QUAD[0][0] * old[0] + QUAD[0][1] * old[1] + QUAD[0][2] * old[2])
        int_end = stiff * (QUAD[1][0] * old[0] + QUAD[1][1] * old[1] + QUAD[1][2] * old[2])
        inv = 1.0 / (1.0 + 0.5 * stiff)
        known.append((inv, old[0] + 0.5 * stiff * old[1] - int_mid, 0.5 * stiff * old[2] - int_end, old[1], old[2]))
    arrive(NT, e4)
    mids = []
    for p in range(3):
        tend = (vmid[0, p].astype(F32) + vmid[1, p].astype(F32)) + (vmid[2, p].astype(F32) + vmid[3, p].astype(F32))
        mids.append((known[p][1] + tend) * known[p][0])
    levels = dot(wmix[pl.ds(0, 16), :], jnp.concatenate(mids, 1), HIGHEST)
    fourier = []
    for p in range(3):
        x = (levels[:, p * NC : p * NC + NC] * keeps[p]).astype(BF16)
        fourier.append(dot(x, leg[p, pl.ds(0, NC), :]))
    rest = jnp.zeros((80, NC), F32)
    f = jnp.concatenate(fourier + [rest], 0).T.reshape(NZ, 48, 128)
    s6[:, pl.ds(0, 16), :] = (f[:, :16] + pltpu.roll(f[:, 16:32], 64, 2)).astype(BF16)
    s6[:, pl.ds(16, 16), :] = f[:, 32:].astype(BF16)
    e5a = lambda k: z_copy(k, s6, r6, 4)
    start(NZ, e5a)
    r6[z] = s6[z]
    e4e = lambda k: gather_copy(k, vend, 4)
    start(NT, e4e)
    e4t = lambda k: scatter_copy(k, s5, r5, 2)
    start(NT, e4t)
    r5[t] = s5[t]
    place = wplace[...]
    lift[0] = dot(place, jnp.concatenate([mids[p] - known[p][3] for p in range(3)], 0), HIGHEST).reshape(NT, 16, NC)
    arrive(NZ, e5a)
    for h in range(2):
        o = dot(perm[...], r6[:, pl.ds(h * 16, 16), :].reshape(128, 128))
        cstage[:, pl.ds(h * 8, 8), :] = o.reshape(ND, 8, 128)
    s7[...] = cstage[...].astype(BF16)
    e5b = lambda k: d_copy(k, s7, r7, 4)
    start(ND, e5b)
    r7[d] = s7[d]
    arrive(NT, e4e)
    ends = []
    for p in range(3):
        inv, known_mid, known_end, old_1, old_2 = known[p]
        tend = (vend[0, p].astype(F32) + vend[1, p].astype(F32)) + (vend[2, p].astype(F32) + vend[3, p].astype(F32))
        ends.append((mids[p] + known_end + tend) * inv - old_2)
    lift[1] = dot(place, jnp.concatenate(ends, 0), HIGHEST).reshape(NT, 16, NC)
    arrive(ND, e5b)

    cstage[...] = r7[...].astype(F32)
    turned = [cstage[:, pl.ds(h * 8, 8), :].reshape(128, 128).T for h in range(2)]
    at_j = ((0, 0), (0, 64), (1, 0))
    rows = []
    for h, first_row in at_j:
        at = [first_row + p * 16 + c * 8 for c in range(2) for p in range(3)]
        rows.append(jnp.concatenate([turned[h][r : r + 8] for r in at], 1))
    rows.append(jnp.zeros((8, 2 * NC), F32))
    fresh = coarse_grid(jnp.concatenate(rows, 0).astype(BF16))
    slot = (fresh - oldback[...]).astype(BF16).astype(F32)
    by_j = []
    for j in range(3):
        by_j.append([slot[j * 8 : j * 8 + 8, c * NC + p * 128 : c * NC + p * 128 + 128] for p in range(3) for c in range(2)])
    gap = [jnp.zeros((16, 128), F32)]
    for h, group in enumerate((by_j[0] + gap + by_j[1] + gap, by_j[2] + gap * 5)):
        cstage[:, pl.ds(h * 8, 8), :] = jnp.concatenate(group, 0).T.reshape(ND, 8, 128)
    s8[...] = cstage[...].astype(BF16)
    e6a = lambda k: d_copy(k, s8, r8, 5)
    start(ND, e6a)
    r8[d] = s8[d]
    for a in range(2):
        for b in range(2):
            for p in range(3):
                corr[a, b, p] = fs[a, b + 1, p]
    mid_own = lift[0, t]
    for p in range(3):
        for a in range(2):
            r = p * 4 + a * 2
            corr[a, 0, p, :, pl.ds(0, NC)] = fs[a, 1, p, :, pl.ds(0, NC)] + mid_own[r : r + 2]
    for make in (*e1, e4, e4e, e4t):
        sent(NT, make)
    for make in (*e2az, e2bz, e3bz, *e3az, e5a):
        sent(NZ, make)
    for make in (e2bd, e2ad, e3ad, e3bd, e5b):
        sent(ND, make)
    arrive(NT, e4t)
    for p in range(3):
        total = (r5[0, p].astype(F32) + r5[1, p].astype(F32)) + (r5[2, p].astype(F32) + r5[3, p].astype(F32))
        for c in range(2):
            for a in range(2):
                for b in range(3):
                    r = c * 8 + b * 2 + a
                    tend_out[a, b, p, pl.ds(c, 1), :] = total[r : r + 1]
    arrive(ND, e6a)
    cstage[...] = r8[...].astype(F32)
    for h in range(2):
        x = cstage[:, pl.ds(h * 8, 8), :].reshape(128, 128).astype(BF16)
        s9[:, pl.ds(h * 16, 16), :] = dot(permt[...], x).astype(BF16).reshape(NZ, 16, 128)
    e6b = lambda k: z_copy(k, s9, r9, 5)
    start(NZ, e6b)
    r9[z] = s9[z]
    sent(ND, e6a)
    arrive(NZ, e6b)
    x = r9[...].astype(F32)
    back = jnp.concatenate([x[:, :16], pltpu.roll(x[:, :16], 64, 2), x[:, 16:]], 1).reshape(NC, 128).T
    partial = []
    for p in range(3):
        partial.append(dot_nt(back[p * 16 : p * 16 + 16].astype(BF16), leg[p, pl.ds(0, NC), :]) * keeps[p])
    diff = dot(wmix[pl.ds(16, 16), :], jnp.concatenate(partial, 1), HIGHEST)
    scaled = [diff[:, p * NC : p * NC + NC] * (0.5 * known[p][0]) for p in range(3)]
    total = dot(place, jnp.concatenate(scaled, 0), HIGHEST)
    s10[...] = total.astype(BF16).reshape(NT, 16, NC)
    e7 = lambda k: scatter_copy(k, s10, r10, 3)
    start(NT, e7)
    r10[t] = s10[t]
    arrive(NT, e7)
    end_own = lift[1, t] + ((r10[0].astype(F32) + r10[1].astype(F32)) + (r10[2].astype(F32) + r10[3].astype(F32)))
    for p in range(3):
        for a in range(2):
            r = p * 4 + a * 2
            corr[a, 1, p, :, pl.ds(0, NC)] = fs[a, 2, p, :, pl.ds(0, NC)] + end_own[r : r + 2]
    sent(NT, e7)
    sent(NZ, e6b)


def per_device(fine_state, fold_pairs, legendre, gauss_weights, grid_coef, modes_from, modes_to, mode_rates):
    fine_table, coarse_table = tables()
    sels = selectors()
    fs = jnp.transpose(fine_state, (0, 1, 3, 2, 4))
    leg = jnp.transpose(legendre, (0, 2, 1))
    vm = pl.BlockSpec(memory_space=pltpu.VMEM)
    hbm = pl.BlockSpec(memory_space=pltpu.HBM)
    v, sm = pltpu.VMEM, pltpu.SMEM
    dma = pltpu.SemaphoreType.DMA
    scratch = [
        v((2, 3, 3, 2, ROWS), F32), sm((NC,), jnp.int32), v((NC,), jnp.int32), sm((NC,), F32), sm((LEV,), F32),
        v((LEV, NLON), F32), v((8, 8), F32), v((8, 8), F32), v((80, 8), F32), v((80, 64), F32), v((8, 64), F32),
        v((80, 8), F32), v((80, 48), F32), v((8, 48), F32),
        v((3, ROWS, NC), BF16), v((2, 768, HALF), BF16), v((2, NC, CLON), BF16),
        v((3, 16, ROWS), F32), v((3, NT, 16, ROWS), BF16), v((3, 16, ROWS), F32), v((3, 16, ROWS), F32),
        v((768, 768), BF16), v((NC, NC), BF16), v((768, CLON), BF16), v((128, 128), BF16), v((128, 128), BF16),
        v((32, NLON), F32), v((LEV, CLON), F32), v((80, 64), F32), v((32, 16), F32), v((64, 48), F32),
        v((3, 48, NC), F32), v((3, 64, ROWS), F32), v((32, 768), F32), v((2, NT, 16, NC), F32), v((32, 768), F32),
        v((ND, 48, 128), F32), v((ND, 32, 128), F32), v((ND, 16, 128), F32),
    ]
    z_two, z_one = v((2, NZ, 48, 128), BF16), v((NZ, 48, 128), BF16)
    d_two, d_one = v((ND, 48, 128), BF16), v((ND, 32, 128), BF16)
    scratch += [z_two, z_two, d_two, d_two, d_one, d_one, z_one, z_one]
    scratch += [d_two, d_two, z_two, z_two, z_one, z_one, d_one, d_one]
    scratch += [v((NT, 3, 16, NC), BF16), v((NT, 3, 16, NC), BF16), v((NT, 3, 16, ROWS), BF16), v((NT, 3, 16, ROWS), BF16)]
    z_coarse, d_coarse, lev_coarse = v((NZ, 32, 128), BF16), v((ND, 16, 128), BF16), v((NT, 16, NC), BF16)
    scratch += [z_coarse] * 2 + [d_coarse] * 4 + [z_coarse] * 2 + [lev_coarse] * 2
    scratch += [
        dma((17,)), dma((8, NZ)), dma((8, NZ)), dma((6, ND)), dma((6, ND)), dma((8, NT)), dma((8, NT)),
    ]
    operands = [
        fs, leg, fold_pairs, gauss_weights, mode_rates, grid_coef, modes_to, modes_from,
        jnp.asarray(fine_table), jnp.asarray(coarse_table), *[jnp.asarray(s) for s in sels],
    ]
    corr, tend = pl.pallas_call(
        kernel,
        out_shape=(
            jax.ShapeDtypeStruct((2, 2, 3, 2, ROWS), F32),
            jax.ShapeDtypeStruct((2, 3, 3, 2, ROWS), F32),
        ),
        in_specs=[hbm] * 16,
        out_specs=(vm, vm),
        scratch_shapes=scratch,
        compiler_params=pltpu.CompilerParams(
            collective_id=0, has_side_effects=True, vmem_limit_bytes=48 * 1024 * 1024
        ),
        name="sweep",
    )(*[pltpu.with_memory_space_constraint(x, pltpu.HBM) for x in operands])
    return (jnp.transpose(corr, (0, 1, 3, 2, 4)), jnp.transpose(tend, (0, 1, 3, 2, 4)))


def solution(mesh):
    placed = (
        P("lev", None, None, "wave", None),
        P(),
        P("wave", "lev", None),
        P("lev"),
        P(),
        P(),
        P(),
        P(),
    )
    return jax.shard_map(
        per_device,
        mesh=mesh,
        in_specs=placed,
        out_specs=(P("lev", None, None, "wave", None), P("lev", None, None, "wave", None)),
        check_vma=False,
    )
```

```python
import functools
import math

import jax
import jax.numpy as jnp
import ml_dtypes
import numpy as np
from jax import lax
from jax.experimental import pallas as pl
from jax.experimental.pallas import tpu as pltpu
from jax.sharding import PartitionSpec as P

F32 = jnp.float32
BF16 = jnp.bfloat16
HIGHEST = lax.Precision.HIGHEST
MESH = pl.DeviceIdType.MESH

NLON, LEV, WAVES, ROWS, NC = 2560, 8, 768, 769, 384
HALF, CLON = NLON // 2, NLON // 2
NZ, ND, NT = 8, 16, 4
FACTOR = 2.0 * WAVES / NLON
QUAD = ((5.0 / 24.0, 1.0 / 3.0, -1.0 / 24.0), (-1.0 / 24.0, 1.0 / 3.0, 5.0 / 24.0))


def table(waves, points, amplitude, count):
    turns = np.outer(waves, np.arange(count)) % points
    angles = turns * (2.0 * math.pi / points)
    return np.concatenate([np.cos(angles), -np.sin(angles)], 0).reshape(2, len(waves), count) * amplitude


def tables():
    t = np.arange(192)
    fine = []
    for parity in (0, 1):
        low = 2 * t + parity
        high = (WAVES - 2 - 2 * t) + parity
        fine.append(table(np.concatenate([low, high]), NLON, WAVES**-0.5, HALF).reshape(768, HALF))
    coarse = table(np.arange(NC), NLON // 2, NC**-0.5, NLON // 2)
    as_bf16 = lambda values: values.astype(np.float32).astype(ml_dtypes.bfloat16)
    return as_bf16(np.stack(fine)), as_bf16(coarse)


def selectors():
    to_rows = np.zeros((80, 8), np.float32)
    to_mask = np.zeros((80, 64), np.float32)
    to_cols = np.zeros((8, 64), np.float32)
    for lev in range(4):
        for c in range(2):
            for rho in range(8):
                col = lev * 16 + c * 8 + rho
                to_cols[lev * 2 + rho % 2, col] = 1
                node = rho // 2
                for q in range(8):
                    if node < 3:
                        to_mask[node * 16 + c * 8 + q, col] = 1
                        to_mask[48 + c * 8 + q, col] = QUAD[0][node]
                        to_mask[64 + c * 8 + q, col] = QUAD[1][node]
    for row in range(80):
        to_rows[row, row % 8] = 1
    mix_cols = np.zeros((8, 48), np.float32)
    mix_rows = np.zeros((80, 8), np.float32)
    mix_mask = np.zeros((80, 48), np.float32)
    for c in range(2):
        for q in range(8):
            for p in range(3):
                mix_cols[q, p * 16 + c * 8 + q] = 1
            for a in range(8):
                mix_rows[c * 8 + a, a] = 1
                mix_mask[c * 8 + a, c * 8 + q] = 1
                for p in range(3):
                    row = 16 + (a // 2) * 16 + p * 4 + (a % 2) * 2 + c
                    mix_rows[row, a] = 1
                    mix_mask[row, p * 16 + c * 8 + q] = 1
    return to_rows, to_mask, to_cols, mix_rows, mix_mask, mix_cols


def dot(a, b, precision=None):
    return lax.dot_general(a, b, (((1,), (0,)), ((), ())), precision=precision, preferred_element_type=F32)


def dot_nt(a, b):
    return lax.dot_general(a, b, (((1,), (1,)), ((), ())), preferred_element_type=F32)


def kernel(
    fs_hbm, leg_hbm, fold_hbm, gauss_hbm, rates_hbm, coef_hbm, mto_hbm, mfrom_hbm, tf_hbm, tc_hbm,
    to_rows_hbm, to_mask_hbm, to_cols_hbm, mix_rows_hbm, mix_mask_hbm, mix_cols_hbm,
    corr, tend_out,
    fs, fold_s, fold_v, gauss_s, rates_s, coef, mto, mfrom,
    to_rows, to_mask, to_cols, mix_rows, mix_mask, mix_cols,
    leg, tf, tc, xf, gat, m0s, m1s, onehot, ordered, tslot, perm, permt, coefx, ccoef, wto, wmix, wplace, states, parts, oldback, lift, xold,
    stage, stageb, cstage,
    s1a, r1a, s2a, r2a, s1b, r1b, s2b, r2b, s3a, r3a, s4a, r4a, s3b, r3b, s4b, r4b,
    vmid, vend, s5, r5, s6, r6, s7, r7, s8, r8, s9, r9, s10, r10,
    load_sem, z_send, z_recv, d_send, d_recv, lev_send, lev_recv,
):
    w = lax.axis_index("wave")
    t = lax.axis_index("lev")
    z, d = w // ND, w % ND

    pairs = (
        (leg_hbm, leg), (tf_hbm, tf), (tc_hbm, tc), (fs_hbm, fs), (fold_hbm, fold_s), (fold_hbm, fold_v),
        (gauss_hbm, gauss_s), (rates_hbm, rates_s), (coef_hbm, coef), (mto_hbm, mto), (mfrom_hbm, mfrom),
        (to_rows_hbm, to_rows), (to_mask_hbm, to_mask), (to_cols_hbm, to_cols), (mix_rows_hbm, mix_rows),
        (mix_mask_hbm, mix_mask), (mix_cols_hbm, mix_cols),
    )
    loads = [pltpu.make_async_copy(src, dst, load_sem.at[n]) for n, (src, dst) in enumerate(pairs)]
    loads[3].start()

    barrier = pltpu.get_barrier_semaphore()

    def lev_dev(k):
        return {"lev": lax.rem(t + k, NT)}

    def z_dev(k):
        return {"wave": lax.rem(z + k, NZ) * ND + d}

    def d_dev(k):
        return {"wave": z * ND + lax.rem(d + k, ND)}

    groups = ((NT, lev_dev), (NZ, z_dev), (ND, d_dev))
    for count, dev in groups:
        @pl.loop(1, count)
        def _(k):
            pl.semaphore_signal(barrier, inc=1, device_id=dev(k), device_id_type=MESH)

    for n in (0, 4, 5) + tuple(range(6, 17)) + (1, 2):
        loads[n].start()

    def lev_copy(k, src, dst, row):
        return pltpu.make_async_remote_copy(
            src_ref=src, dst_ref=dst, send_sem=lev_send.at[row, k], recv_sem=lev_recv.at[row, k],
            device_id=lev_dev(k), device_id_type=MESH)

    def z_copy(k, src, dst, row):
        return pltpu.make_async_remote_copy(
            src_ref=src.at[lax.rem(z + k, NZ)], dst_ref=dst.at[z], send_sem=z_send.at[row, k],
            recv_sem=z_recv.at[row, k], device_id=z_dev(k), device_id_type=MESH)

    def d_copy(k, src, dst, row):
        return pltpu.make_async_remote_copy(
            src_ref=src.at[lax.rem(d + k, ND)], dst_ref=dst.at[d], send_sem=d_send.at[row, k],
            recv_sem=d_recv.at[row, k], device_id=d_dev(k), device_id_type=MESH)

    def gather_copy(k, buf, row):
        return lev_copy(k, buf.at[t], buf.at[t], row)

    def scatter_copy(k, src, dst, row):
        return lev_copy(k, src.at[lax.rem(t + k, NT)], dst.at[t], row)

    def start(count, make):
        @pl.loop(1, count)
        def _(k):
            make(k).start()

    def arrive(count, make):
        @pl.loop(1, count)
        def _(k):
            make(k).wait_recv()

    def sent(count, make):
        @pl.loop(1, count)
        def _(k):
            make(k).wait_send()

    loads[3].wait()
    for p in range(3):
        for c in range(2):
            for a in range(2):
                for b in range(3):
                    xf[p, pl.ds(c * 8 + b * 2 + a, 1), :] = fs[a, b, p, pl.ds(c, 1), :]
                xf[p, pl.ds(c * 8 + 6 + a, 1), :] = fs[a, 1, p, pl.ds(c, 1), :]
    for p in range(3):
        gat[p, t] = xf[p].astype(BF16)
    pl.semaphore_wait(barrier, (NT - 1) + (NZ - 1) + (ND - 1))
    e1 = [lambda k, p=p: gather_copy(k, gat.at[p], 5 + p) for p in range(3)]
    for p in (2, 0, 1):
        start(NT, e1[p])

    for n in range(4, 17):
        loads[n].wait()
    folds = [fold_s[w * 3 + p] for p in range(3)]
    rho = lax.rem(lax.broadcasted_iota(jnp.int32, (16, ROWS), 0), 8)
    row_r = lax.broadcasted_iota(jnp.int32, (16, ROWS), 1)
    for p in range(3):
        first = jnp.where(row_r < WAVES - folds[p], 1.0, 0.0)
        keep = jnp.where(row_r < NC - folds[p], 1.0, 0.0)
        m0s[p] = jnp.where(rho < 6, first, keep)
        m1s[p] = jnp.where(rho < 6, 1.0 - first, 0.0)
    pr = lax.broadcasted_iota(jnp.int32, (128, 128), 0)
    pc = lax.broadcasted_iota(jnp.int32, (128, 128), 1)
    perm[...] = jnp.where(pc == lax.rem(pr, NZ) * ND + pr // NZ, 1.0, 0.0).astype(BF16)
    permt[...] = jnp.where(pr == lax.rem(pc, NZ) * ND + pc // NZ, 1.0, 0.0).astype(BF16)
    stageb[:, pl.ds(24, 8), :] = jnp.zeros((ND, 8, 128), F32)
    loads[0].wait()

    def inverse(p):
        arrive(NT, e1[p])
        x = gat[p].reshape(64, ROWS)
        k0 = jnp.concatenate([m0s[p].astype(BF16)] * 4, 0)
        k1 = jnp.concatenate([m1s[p].astype(BF16)] * 4, 0)
        low = pl.ds(0, ROWS - 1)
        both = jnp.concatenate([(x * k0)[:, : ROWS - 1], (x * k1)[:, : ROWS - 1]], 0)
        f = dot(both, leg[p, low, :])
        last = (x * k1)[:, ROWS - 1 :].astype(F32) * leg[p, pl.ds(ROWS - 1, 1), :].astype(F32)
        f = jnp.concatenate([f[:64], f[64:] + last], 0)
        return f.astype(BF16).T.reshape(NZ, 48, 128)

    f = inverse(2)
    for j in range(3):
        o = dot(perm[...], f[:, j * 16 : j * 16 + 16].reshape(128, 128))
        stageb[:, pl.ds(j * 8, 8), :] = o.reshape(ND, 8, 128)
    s1b[...] = stageb[...].astype(BF16)
    e2bd = lambda k: d_copy(k, s1b, r1b, 0)
    start(ND, e2bd)
    r1b[d] = s1b[d]
    e2az = [lambda k, p=p: z_copy(k, s1a.at[p], r1a.at[p], p * 6) for p in range(2)]
    for p in range(2):
        s1a[p] = inverse(p)
        start(NZ, e2az[p])
        r1a[p, z] = s1a[p, z]

    sr = lax.broadcasted_iota(jnp.int32, (NC, NC), 0)
    sc = lax.broadcasted_iota(jnp.int32, (NC, NC), 1)
    slot_of = (lax.rem(sc, NZ) * ND + lax.rem(sc, 128) // NZ) * 3 + sc // 128
    to_order = jnp.where(sr == slot_of, 1.0, 0.0)
    fold = dot(jnp.broadcast_to(fold_v[...].reshape(1, NC).astype(F32), (8, NC)), to_order, HIGHEST)[:1]
    fold = (fold + 0.5).astype(jnp.int32)
    half_fold, odd = fold // 2, lax.rem(fold, 2)
    rows_n = lax.broadcasted_iota(jnp.int32, (2 * NC, NC), 0)
    onehot[:, pl.ds(0, NC)] = jnp.where(rows_n == half_fold + NC * odd, 1.0, 0.0).astype(BF16)
    onehot[:, pl.ds(NC, NC)] = jnp.where(rows_n == 192 + half_fold + NC * (1 - odd), 1.0, 0.0).astype(BF16)
    ordered[...] = jnp.where(sr == fold, 1.0, 0.0).T.astype(BF16)

    for p in range(2):
        arrive(NZ, e2az[p])
        for j in range(3):
            o = dot(perm[...], r1a[p, :, pl.ds(j * 16, 16), :].reshape(128, 128))
            stage[:, pl.ds(j * 16 + p * 8, 8), :] = o.reshape(ND, 8, 128)
    s2a[...] = stage[...].astype(BF16)
    e2ad = lambda k: d_copy(k, s2a, r2a, 1)
    start(ND, e2ad)
    r2a[d] = s2a[d]
    arrive(ND, e2bd)
    stageb[...] = r1b[...].astype(F32)
    for j in range(3):
        x = stageb[:, pl.ds(j * 8, 8), :].reshape(128, 128).astype(BF16)
        s2b[:, pl.ds(j * 16, 16), :] = dot(permt[...], x).astype(BF16).reshape(NZ, 16, 128)
    e2bz = lambda k: z_copy(k, s2b, r2b, 1)
    start(NZ, e2bz)
    r2b[z] = s2b[z]

    for lev in range(NT):
        for n in range(4):
            coefx[pl.ds(lev * 8 + n * 2, 2), :] = coef[pl.ds(lev * 2, 2), :]
    sel_r = lax.broadcasted_iota(jnp.int32, (256, 128), 0)
    sel_c = lax.broadcasted_iota(jnp.int32, (256, 128), 1)
    even = jnp.where(sel_r == 2 * sel_c, 1.0, 0.0)
    chunks = jnp.concatenate([coef[:, pl.ds(n * 256, 256)] for n in range(10)], 0)
    picked = dot(chunks, even, HIGHEST)
    ccoef[...] = jnp.concatenate([picked[n * 8 : n * 8 + 8] for n in range(10)], 1)
    weights = [gauss_s[z * 48 + j * 16 + d] * FACTOR for j in range(3)]
    loads[1].wait()
    loads[2].wait()
    arrive(NZ, e2bz)
    arrive(ND, e2ad)

    stage[...] = r2a[...].astype(F32)
    turned = []
    for j in range(3):
        by_p = [stage[:, pl.ds(j * 16 + p * 8, 8), :].reshape(128, 128) for p in range(2)]
        by_p.append(dot(perm[...], r2b[:, pl.ds(j * 16, 16), :].reshape(128, 128)))
        turned.append(jnp.concatenate(by_p, 0).T)
    rows = []
    for c in range(2):
        for j in range(3):
            members = []
            for i in range(2):
                at = [i * 64 + lev * 16 + c * 8 for lev in range(NT)]
                members.append(jnp.concatenate([turned[j][r : r + 8] for r in at], 0))
            rows.append(jnp.concatenate(members, 1))
            for lev in range(NT):
                r = lev * 16 + c * 8 + 6
                xold[pl.ds(j * 8 + lev * 2, 2), pl.ds(c * NC, NC)] = turned[j][r : r + 2]
    natural = dot_nt(jnp.concatenate(rows, 0).astype(BF16), onehot[...]).astype(BF16)

    def grid(x_even, x_odd, tab, c_low, c_high):
        e = dot(x_even, tab[0])
        o = dot(x_odd, tab[1])
        low, high = e + o, e - o
        prod = jnp.concatenate([c_low * low * low, c_high * high * high], 0).astype(BF16)
        n = low.shape[0]
        back_e = dot_nt(prod, tab[0])
        back_o = dot_nt(prod, tab[1])
        return back_e[:n] + back_e[n:], back_o[:n] - back_o[n:]

    x_even = jnp.concatenate([natural[:96, :NC], natural[96:, :NC]], 1)
    x_odd = jnp.concatenate([natural[:96, NC:], natural[96:, NC:]], 1)
    fe, fo = grid(
        x_even, x_odd, tf,
        jnp.concatenate([coefx[:, pl.ds(0, HALF)]] * 3, 0), jnp.concatenate([coefx[:, pl.ds(HALF, HALF)]] * 3, 0),
    )
    row = lax.broadcasted_iota(jnp.int32, (96, 1), 0)
    wt = jnp.where(row < 32, weights[0], jnp.where(row < 64, weights[1], weights[2]))
    wt = jnp.where(lax.rem(row, 8) < 6, wt, 0.0)
    be = (fe * wt).astype(BF16)
    bo = (fo * wt).astype(BF16)
    y = [jnp.concatenate([be[:, c * NC : c * NC + NC], bo[:, c * NC : c * NC + NC]], 1) for c in range(2)]
    slot = dot(jnp.concatenate(y, 0), onehot[...])
    for j in range(3):
        pieces = []
        for i in range(2):
            for lev in range(NT):
                for c in range(2):
                    r = c * 96 + j * 32 + lev * 8
                    pieces.append(slot[r : r + 8, i * NC : i * NC + NC])
        back = jnp.concatenate(pieces, 0).T
        for p in range(2):
            stage[:, pl.ds(j * 16 + p * 8, 8), :] = back[p * 128 : p * 128 + 128].reshape(ND, 8, 128)
        o = dot(permt[...], back[256:].astype(BF16))
        s3b[:, pl.ds(j * 16, 16), :] = o.astype(BF16).reshape(NZ, 16, 128)
    s3a[...] = stage[...].astype(BF16)
    e3ad = lambda k: d_copy(k, s3a, r3a, 2)
    e3bz = lambda k: z_copy(k, s3b, r3b, 2)
    start(ND, e3ad)
    start(NZ, e3bz)
    r3a[d] = s3a[d]
    r3b[z] = s3b[z]

    row = lax.broadcasted_iota(jnp.int32, (32, 1), 0)
    wt_c = jnp.where(row < 8, weights[0], jnp.where(row < 16, weights[1], weights[2]))

    def coarse_grid(x):
        g = dot(x, tslot[...])
        prod = (jnp.concatenate([ccoef[...]] * 4, 0) * g * g).astype(BF16)
        return dot_nt(prod, tslot[...]) * wt_c

    for c in range(2):
        tslot[pl.ds(c * NC, NC), :] = dot(ordered[...], tc[c]).astype(BF16)
    xold[pl.ds(24, 8), :] = jnp.zeros((8, 2 * NC), F32)
    oldback[...] = coarse_grid(xold[...].astype(BF16))

    arrive(ND, e3ad)
    stage[...] = r3a[...].astype(F32)
    e3az = [lambda k, p=p: z_copy(k, s4a.at[p], r4a.at[p], 3 + p * 4) for p in range(2)]
    for p in range(2):
        for j in range(3):
            x = stage[:, pl.ds(j * 16 + p * 8, 8), :].reshape(128, 128).astype(BF16)
            s4a[p, :, pl.ds(j * 16, 16), :] = dot(permt[...], x).astype(BF16).reshape(NZ, 16, 128)
        start(NZ, e3az[p])
        r4a[p, z] = s4a[p, z]
    arrive(NZ, e3bz)
    for j in range(3):
        o = dot(perm[...], r3b[:, pl.ds(j * 16, 16), :].reshape(128, 128))
        stageb[:, pl.ds(j * 8, 8), :] = o.reshape(ND, 8, 128)
    s4b[...] = stageb[...].astype(BF16)
    e3bd = lambda k: d_copy(k, s4b, r4b, 3)
    start(ND, e3bd)
    r4b[d] = s4b[d]

    wto[...] = dot(dot(to_rows[...], mto[...], HIGHEST), to_cols[...], HIGHEST) * to_mask[...]
    mixed = dot(dot(mix_rows[...], mfrom[...], HIGHEST), mix_cols[...], HIGHEST) * mix_mask[...]
    wmix[pl.ds(0, 16), :] = mixed[:16, :16]
    wplace[...] = mixed[16:]
    mixed = dot(dot(mix_rows[pl.ds(0, 16), :], mto[...], HIGHEST), mix_cols[...], HIGHEST) * mix_mask[pl.ds(0, 16), :]
    wmix[pl.ds(16, 16), :] = mixed[:, :16]
    keeps = [m0s[p, pl.ds(6, 1), pl.ds(0, NC)] for p in range(3)]
    for p in range(3):
        x = gat[p, :, :, pl.ds(0, NC)].reshape(64, NC).astype(F32)
        states[p] = dot(wto[pl.ds(0, 48), :], x, HIGHEST) * keeps[p]

    e4 = [lambda k, p=p: gather_copy(k, vmid.at[p], 8 + p) for p in range(3)]

    def forward(p, x):
        o = dot_nt(x.T, leg[p])
        k0 = jnp.concatenate([m0s[p]] * 4, 0)
        k1 = jnp.concatenate([m1s[p]] * 4, 0)
        part = o[:64] * k0 + o[64:] * k1
        parts[p] = part
        mixed = dot(wto[pl.ds(48, 32), :], part[:, :NC] * keeps[p], HIGHEST).astype(BF16)
        vmid[p, t] = mixed[:16]
        vend[t, p] = mixed[16:]
        start(NT, e4[p])

    arrive(ND, e3bd)
    stageb[...] = r4b[...].astype(F32)
    pieces = []
    for j in range(3):
        x = stageb[:, pl.ds(j * 8, 8), :].reshape(128, 128).astype(BF16)
        pieces.append(dot(permt[...], x).astype(BF16).reshape(NZ, 16, 128))
    forward(2, jnp.concatenate(pieces, 1).reshape(NC, 128))
    for p in range(2):
        arrive(NZ, e3az[p])
        forward(p, r4a[p].reshape(NC, 128))
    for p in range(3):
        s5[:, p] = parts[p].astype(BF16).reshape(NT, 16, ROWS)

    mode = lax.rem(lax.broadcasted_iota(jnp.int32, (16, NC), 0), 8)
    rate = jnp.zeros((16, NC), F32)
    for q in range(8):
        rate = jnp.where(mode == q, rates_s[q], rate)
    col = lax.broadcasted_iota(jnp.int32, (16, NC), 1)
    known = []
    for p in range(3):
        degree = (col + folds[p]).astype(F32)
        stiff = rate * (degree * (degree + 1.0) / (NC * (NC + 1.0)))
        old = [states[p, pl.ds(b * 16, 16), :] for b in range(3)]
        int_mid = stiff * (QUAD[0][0] * old[0] + QUAD[0][1] * old[1] + QUAD[0][2] * old[2])
        int_end = stiff * (QUAD[1][0] * old[0] + QUAD[1][1] * old[1] + QUAD[1][2] * old[2])
        inv = 1.0 / (1.0 + 0.5 * stiff)
        known.append((inv, old[0] + 0.5 * stiff * old[1] - int_mid, 0.5 * stiff * old[2] - int_end, old[1], old[2]))
    for p in range(3):
        arrive(NT, e4[p])
    mids = []
    for p in range(3):
        tend = (vmid[p, 0].astype(F32) + vmid[p, 1].astype(F32)) + (vmid[p, 2].astype(F32) + vmid[p, 3].astype(F32))
        mids.append((known[p][1] + tend) * known[p][0])
    levels = dot(wmix[pl.ds(0, 16), :], jnp.concatenate(mids, 1), HIGHEST)
    fourier = []
    for p in range(3):
        x = (levels[:, p * NC : p * NC + NC] * keeps[p]).astype(BF16)
        fourier.append(dot(x, leg[p, pl.ds(0, NC), :]))
    rest = jnp.zeros((80, NC), F32)
    f = jnp.concatenate(fourier + [rest], 0).T.reshape(NZ, 48, 128)
    s6[:, pl.ds(0, 16), :] = (f[:, :16] + pltpu.roll(f[:, 16:32], 64, 2)).astype(BF16)
    s6[:, pl.ds(16, 16), :] = f[:, 32:].astype(BF16)
    e5a = lambda k: z_copy(k, s6, r6, 4)
    start(NZ, e5a)
    r6[z] = s6[z]
    e4e = lambda k: gather_copy(k, vend, 4)
    start(NT, e4e)
    e4t = lambda k: scatter_copy(k, s5, r5, 2)
    start(NT, e4t)
    r5[t] = s5[t]
    place = wplace[...]
    lift[0] = dot(place, jnp.concatenate([mids[p] - known[p][3] for p in range(3)], 0), HIGHEST).reshape(NT, 16, NC)
    arrive(NZ, e5a)
    for h in range(2):
        o = dot(perm[...], r6[:, pl.ds(h * 16, 16), :].reshape(128, 128))
        cstage[:, pl.ds(h * 8, 8), :] = o.reshape(ND, 8, 128)
    s7[...] = cstage[...].astype(BF16)
    e5b = lambda k: d_copy(k, s7, r7, 4)
    start(ND, e5b)
    r7[d] = s7[d]
    arrive(NT, e4e)
    ends = []
    for p in range(3):
        inv, known_mid, known_end, old_1, old_2 = known[p]
        tend = (vend[0, p].astype(F32) + vend[1, p].astype(F32)) + (vend[2, p].astype(F32) + vend[3, p].astype(F32))
        ends.append((mids[p] + known_end + tend) * inv - old_2)
    lift[1] = dot(place, jnp.concatenate(ends, 0), HIGHEST).reshape(NT, 16, NC)
    arrive(ND, e5b)

    cstage[...] = r7[...].astype(F32)
    turned = [cstage[:, pl.ds(h * 8, 8), :].reshape(128, 128).T for h in range(2)]
    at_j = ((0, 0), (0, 64), (1, 0))
    rows = []
    for h, first_row in at_j:
        at = [first_row + p * 16 + c * 8 for c in range(2) for p in range(3)]
        rows.append(jnp.concatenate([turned[h][r : r + 8] for r in at], 1))
    rows.append(jnp.zeros((8, 2 * NC), F32))
    fresh = coarse_grid(jnp.concatenate(rows, 0).astype(BF16))
    slot = (fresh - oldback[...]).astype(BF16).astype(F32)
    by_j = []
    for j in range(3):
        by_j.append([slot[j * 8 : j * 8 + 8, c * NC + p * 128 : c * NC + p * 128 + 128] for p in range(3) for c in range(2)])
    gap = [jnp.zeros((16, 128), F32)]
    for h, group in enumerate((by_j[0] + gap + by_j[1] + gap, by_j[2] + gap * 5)):
        cstage[:, pl.ds(h * 8, 8), :] = jnp.concatenate(group, 0).T.reshape(ND, 8, 128)
    s8[...] = cstage[...].astype(BF16)
    e6a = lambda k: d_copy(k, s8, r8, 5)
    start(ND, e6a)
    r8[d] = s8[d]
    for a in range(2):
        for b in range(2):
            for p in range(3):
                corr[a, b, p] = fs[a, b + 1, p]
    mid_own = lift[0, t]
    for p in range(3):
        for a in range(2):
            r = p * 4 + a * 2
            corr[a, 0, p, :, pl.ds(0, NC)] = fs[a, 1, p, :, pl.ds(0, NC)] + mid_own[r : r + 2]
    for make in (*e1, *e4, e4e, e4t):
        sent(NT, make)
    for make in (*e2az, e2bz, e3bz, *e3az, e5a):
        sent(NZ, make)
    for make in (e2bd, e2ad, e3ad, e3bd, e5b):
        sent(ND, make)
    arrive(NT, e4t)
    for p in range(3):
        total = (r5[0, p].astype(F32) + r5[1, p].astype(F32)) + (r5[2, p].astype(F32) + r5[3, p].astype(F32))
        for c in range(2):
            for a in range(2):
                for b in range(3):
                    r = c * 8 + b * 2 + a
                    tend_out[a, b, p, pl.ds(c, 1), :] = total[r : r + 1]
    arrive(ND, e6a)
    cstage[...] = r8[...].astype(F32)
    for h in range(2):
        x = cstage[:, pl.ds(h * 8, 8), :].reshape(128, 128).astype(BF16)
        s9[:, pl.ds(h * 16, 16), :] = dot(permt[...], x).astype(BF16).reshape(NZ, 16, 128)
    e6b = lambda k: z_copy(k, s9, r9, 5)
    start(NZ, e6b)
    r9[z] = s9[z]
    sent(ND, e6a)
    arrive(NZ, e6b)
    x = r9[...].astype(F32)
    back = jnp.concatenate([x[:, :16], pltpu.roll(x[:, :16], 64, 2), x[:, 16:]], 1).reshape(NC, 128).T
    partial = []
    for p in range(3):
        partial.append(dot_nt(back[p * 16 : p * 16 + 16].astype(BF16), leg[p, pl.ds(0, NC), :]) * keeps[p])
    diff = dot(wmix[pl.ds(16, 16), :], jnp.concatenate(partial, 1), HIGHEST)
    scaled = [diff[:, p * NC : p * NC + NC] * (0.5 * known[p][0]) for p in range(3)]
    total = dot(place, jnp.concatenate(scaled, 0), HIGHEST)
    s10[...] = total.astype(BF16).reshape(NT, 16, NC)
    e7 = lambda k: scatter_copy(k, s10, r10, 3)
    start(NT, e7)
    r10[t] = s10[t]
    arrive(NT, e7)
    end_own = lift[1, t] + ((r10[0].astype(F32) + r10[1].astype(F32)) + (r10[2].astype(F32) + r10[3].astype(F32)))
    for p in range(3):
        for a in range(2):
            r = p * 4 + a * 2
            corr[a, 1, p, :, pl.ds(0, NC)] = fs[a, 2, p, :, pl.ds(0, NC)] + end_own[r : r + 2]
    sent(NT, e7)
    sent(NZ, e6b)


def per_device(fine_state, fold_pairs, legendre, gauss_weights, grid_coef, modes_from, modes_to, mode_rates):
    fine_table, coarse_table = tables()
    sels = selectors()
    fs = jnp.transpose(fine_state, (0, 1, 3, 2, 4))
    leg = jnp.transpose(legendre, (0, 2, 1))
    vm = pl.BlockSpec(memory_space=pltpu.VMEM)
    hbm = pl.BlockSpec(memory_space=pltpu.HBM)
    v, sm = pltpu.VMEM, pltpu.SMEM
    dma = pltpu.SemaphoreType.DMA
    scratch = [
        v((2, 3, 3, 2, ROWS), F32), sm((NC,), jnp.int32), v((NC,), jnp.int32), sm((NC,), F32), sm((LEV,), F32),
        v((LEV, NLON), F32), v((8, 8), F32), v((8, 8), F32), v((80, 8), F32), v((80, 64), F32), v((8, 64), F32),
        v((80, 8), F32), v((80, 48), F32), v((8, 48), F32),
        v((3, ROWS, NC), BF16), v((2, 768, HALF), BF16), v((2, NC, CLON), BF16),
        v((3, 16, ROWS), F32), v((3, NT, 16, ROWS), BF16), v((3, 16, ROWS), F32), v((3, 16, ROWS), F32),
        v((768, 768), BF16), v((NC, NC), BF16), v((768, CLON), BF16), v((128, 128), BF16), v((128, 128), BF16),
        v((32, NLON), F32), v((LEV, CLON), F32), v((80, 64), F32), v((32, 16), F32), v((64, 48), F32),
        v((3, 48, NC), F32), v((3, 64, ROWS), F32), v((32, 768), F32), v((2, NT, 16, NC), F32), v((32, 768), F32),
        v((ND, 48, 128), F32), v((ND, 32, 128), F32), v((ND, 16, 128), F32),
    ]
    z_two, z_one = v((2, NZ, 48, 128), BF16), v((NZ, 48, 128), BF16)
    d_two, d_one = v((ND, 48, 128), BF16), v((ND, 32, 128), BF16)
    scratch += [z_two, z_two, d_two, d_two, d_one, d_one, z_one, z_one]
    scratch += [d_two, d_two, z_two, z_two, z_one, z_one, d_one, d_one]
    scratch += [v((3, NT, 16, NC), BF16), v((NT, 3, 16, NC), BF16), v((NT, 3, 16, ROWS), BF16), v((NT, 3, 16, ROWS), BF16)]
    z_coarse, d_coarse, lev_coarse = v((NZ, 32, 128), BF16), v((ND, 16, 128), BF16), v((NT, 16, NC), BF16)
    scratch += [z_coarse] * 2 + [d_coarse] * 4 + [z_coarse] * 2 + [lev_coarse] * 2
    scratch += [
        dma((17,)), dma((8, NZ)), dma((8, NZ)), dma((6, ND)), dma((6, ND)), dma((11, NT)), dma((11, NT)),
    ]
    operands = [
        fs, leg, fold_pairs, gauss_weights, mode_rates, grid_coef, modes_to, modes_from,
        jnp.asarray(fine_table), jnp.asarray(coarse_table), *[jnp.asarray(s) for s in sels],
    ]
    corr, tend = pl.pallas_call(
        kernel,
        out_shape=(
            jax.ShapeDtypeStruct((2, 2, 3, 2, ROWS), F32),
            jax.ShapeDtypeStruct((2, 3, 3, 2, ROWS), F32),
        ),
        in_specs=[hbm] * 16,
        out_specs=(vm, vm),
        scratch_shapes=scratch,
        compiler_params=pltpu.CompilerParams(
            collective_id=0, has_side_effects=True, vmem_limit_bytes=48 * 1024 * 1024
        ),
        name="sweep",
    )(*[pltpu.with_memory_space_constraint(x, pltpu.HBM) for x in operands])
    return (jnp.transpose(corr, (0, 1, 3, 2, 4)), jnp.transpose(tend, (0, 1, 3, 2, 4)))


def solution(mesh):
    placed = (
        P("lev", None, None, "wave", None),
        P(),
        P("wave", "lev", None),
        P("lev"),
        P(),
        P(),
        P(),
        P(),
    )
    return jax.shard_map(
        per_device,
        mesh=mesh,
        in_specs=placed,
        out_specs=(P("lev", None, None, "wave", None), P("lev", None, None, "wave", None)),
        check_vma=False,
    )
```
